128 devices in a mesh: cp: 16 (over y_hi, x, core), hd: 8 (over z, y_lo).
Axes of the slice: x: 4, y: 4 (y_hi: 2, y_lo: 2; y = y_hi * 2 + y_lo), z: 4, core: 2. Of those that a mesh axis runs over, the one named last changes fastest.
Arguments:
- hidden_in: bfloat16 [2, 8192, 1024], P(None, ('cp', 'hd')), may hold values from -6 to 6
- doc_ids: int32 [2, 8192], replicated, may hold values from 0 to 2, as said below
- w_query: bfloat16 [1024, 1024], P('cp'), may hold values from -0.1875 to 0.1875
- w_key: bfloat16 [1024, 1024], P('cp'), may hold values from -0.1875 to 0.1875
- w_value: bfloat16 [1024, 2048], P('cp'), may hold values from -0.1875 to 0.1875
- w_decay: bfloat16 [1024, 8], P('cp'), may hold values from -0.1875 to 0.1875
- w_beta: bfloat16 [1024, 8], P('cp'), may hold values from -0.1875 to 0.1875
- w_gate_out: bfloat16 [1024, 2048], P('cp'), may hold values from -0.1875 to 0.1875
- w_output: bfloat16 [2048, 1024], P('cp'), may hold values from -0.25 to 0.25
- w_ffn_gate: bfloat16 [1024, 2816], P('cp'), may hold values from -0.1875 to 0.1875
- w_ffn_up: bfloat16 [1024, 2816], P('cp'), may hold values from -0.1875 to 0.1875
- w_ffn_down: bfloat16 [2816, 1024], P('cp'), may hold values from -0.21875 to 0.21875
- conv_query: bfloat16 [4, 1024], P(None, 'hd'), may hold values from -3 to 3
- conv_key: bfloat16 [4, 1024], P(None, 'hd'), may hold values from -3 to 3
- conv_value: bfloat16 [4, 2048], P(None, 'hd'), may hold values from -3 to 3
- decay_log: bfloat16 [8], P('hd'), may hold values from -9 to -3
- decay_bias: bfloat16 [8], P('hd'), may hold values from -1 to 1
- gain_attn: bfloat16 [1024], P('cp'), may hold values from 0.5 to 1.5
- gain_ffn: bfloat16 [1024], P('cp'), may hold values from 0.5 to 1.5
- gain_head: bfloat16 [256], P('cp'), may hold values from 0.5 to 1.5
- cotangent: bfloat16 [2, 8192, 1024], P(None, ('cp', 'hd')), may hold values from -6 to 6
Outputs:
- block_out: bfloat16 [2, 8192, 1024], P(None, ('cp', 'hd'))
- grad_in: bfloat16 [2, 8192, 1024], P(None, ('cp', 'hd'))
- grad_w_query: float32 [1024, 1024], P('cp')
- grad_w_key: float32 [1024, 1024], P('cp')
- grad_w_value: float32 [1024, 2048], P('cp')
- grad_w_decay: float32 [1024, 8], P('cp')
- grad_w_beta: float32 [1024, 8], P('cp')
- grad_w_gate_out: float32 [1024, 2048], P('cp')
- grad_w_output: float32 [2048, 1024], P('cp')
- grad_w_ffn_gate: float32 [1024, 2816], P('cp')
- grad_w_ffn_up: float32 [1024, 2816], P('cp')
- grad_w_ffn_down: float32 [2816, 1024], P('cp')
- grad_conv_query: float32 [4, 1024], P(None, 'hd')
- grad_conv_key: float32 [4, 1024], P(None, 'hd')
- grad_conv_value: float32 [4, 2048], P(None, 'hd')
- grad_decay_log: float32 [8], P('hd')
- grad_decay_bias: float32 [8], P('hd')
- grad_gain_attn: float32 [1024], P('cp')
- grad_gain_ffn: float32 [1024], P('cp')
- grad_gain_head: float32 [256], P('cp')
The draws below stay inside these ranges and needn't reach their ends.
Inputs may be any that keep to these rules, and one draw needn't show every extreme that they name: `doc_ids`: each row never falls; document 0 ends within the first 64 tokens of a sequence and document 2 starts within its last 63 tokens.
All inputs are finite; a program needn't handle non-finite values.
Results may differ from the reference program's by a relative error of at most 0.025.
Values may be sent and summed in bfloat16 or wider, within the bound.
A program may use at most 256 MiB of HBM per device.

```python
import jax
import jax.numpy as jnp
from jax import lax

D = 1024
H = 8
DK = 128
DV = 256
FF = 2816
CONV = 4
STRETCH = 64
TD = 64
SEQS = 2
LEN = 8192


def draw_doc_ids(key, part):
    first_key, second_key = jax.random.split(jax.random.fold_in(key, 7))
    first_end = jax.random.randint(first_key, (SEQS, 1), 1, TD)
    second_start = jax.random.randint(second_key, (SEQS, 1), LEN - TD + 1, LEN)
    places = jnp.arange(LEN)[None, :]
    return (places >= first_end).astype(jnp.int32) + (places >= second_start).astype(jnp.int32)


def block_scale(key, dims, cuts, least, top_value):
    def one(axis_at, shards_of):
        heights = jax.random.uniform(jax.random.fold_in(jax.random.fold_in(key, 6), axis_at), (shards_of,), jnp.float32, least / len(cuts), top_value / len(cuts))
        return jnp.repeat(jnp.exp(heights), dims[axis_at] // shards_of).reshape((-1,) + (1,) * (len(dims) - axis_at - 1))

    level = one(*cuts[0])
    for cut in cuts[1:]:
        level = level * one(*cut)
    return level


def noise(own_key, extent, width, reach, cuts=(), kind=jnp.bfloat16):
    values = jax.random.normal(own_key, extent, jnp.float32) * width
    if len(cuts) > 0:
        values = block_scale(own_key, extent, cuts, -0.22, 0.18) * values
    return jnp.clip(values, min=-reach, max=reach).astype(kind)


def setup_inputs(seed: int = 0) -> dict:
    seeds = jax.random.split(jax.random.key(seed), 22)
    hidden_in = noise(seeds[0], (SEQS, LEN, D), 1.0, 6.0, ((1, 128),))
    doc_ids = draw_doc_ids(jax.random.fold_in(seeds[21], 71), 0)
    w_query = noise(seeds[2], (D, H * DK), D ** -0.5, 0.1875, ((0, 16),))
    w_key = noise(seeds[3], (D, H * DK), D ** -0.5, 0.1875, ((0, 16),))
    w_value = noise(seeds[4], (D, H * DV), D ** -0.5, 0.1875, ((0, 16),))
    w_decay = noise(seeds[5], (D, H), D ** -0.5, 0.1875, ((0, 16),))
    w_beta = noise(seeds[6], (D, H), D ** -0.5, 0.1875, ((0, 16),))
    w_gate_out = noise(seeds[7], (D, H * DV), D ** -0.5, 0.1875, ((0, 16),))
    w_output = noise(seeds[8], (H * DV, D), (H * DV // 4) ** -0.5, 0.25, ((0, 16),))
    w_ffn_gate = noise(seeds[9], (D, FF), D ** -0.5, 0.1875, ((0, 16),))
    w_ffn_up = noise(seeds[10], (D, FF), D ** -0.5, 0.1875, ((0, 16),))
    w_ffn_down = noise(seeds[11], (FF, D), (FF // 4) ** -0.5, 0.21875, ((0, 16),))
    conv_query = noise(seeds[12], (CONV, H * DK), CONV ** -0.5, 3.0, ((1, 8),))
    conv_key = noise(seeds[13], (CONV, H * DK), CONV ** -0.5, 3.0, ((1, 8),))
    conv_value = noise(seeds[14], (CONV, H * DV), CONV ** -0.5, 3.0, ((1, 8),))
    decay_log = jnp.clip(-9.0 + 6.0 * jax.random.uniform(seeds[15], (H,), jnp.float32) ** block_scale(seeds[15], (H,), ((0, 8),), -0.2, 0.2), -9.0, -3.0).astype(jnp.bfloat16)
    decay_bias = jnp.clip(jax.random.uniform(seeds[16], (H,), jnp.float32, -1.0, 1.0) * block_scale(seeds[16], (H,), ((0, 8),), -0.4, 0.0), -1.0, 1.0).astype(jnp.bfloat16)
    gain_attn = jnp.clip(1.0 + 0.1 * jax.random.normal(seeds[17], (D,), jnp.float32), 0.5, 1.5).astype(jnp.bfloat16)
    gain_ffn = jnp.clip(1.0 + 0.1 * jax.random.normal(seeds[18], (D,), jnp.float32), 0.5, 1.5).astype(jnp.bfloat16)
    gain_head = jnp.clip(1.0 + 0.1 * jax.random.normal(seeds[19], (DV,), jnp.float32), 0.5, 1.5).astype(jnp.bfloat16)
    cotangent = noise(seeds[20], (SEQS, LEN, D), 1.0, 6.0, ((1, 128),))
    return {"hidden_in": hidden_in, "doc_ids": doc_ids, "w_query": w_query, "w_key": w_key, "w_value": w_value, "w_decay": w_decay, "w_beta": w_beta, "w_gate_out": w_gate_out, "w_output": w_output, "w_ffn_gate": w_ffn_gate, "w_ffn_up": w_ffn_up, "w_ffn_down": w_ffn_down, "conv_query": conv_query, "conv_key": conv_key, "conv_value": conv_value, "decay_log": decay_log, "decay_bias": decay_bias, "gain_attn": gain_attn, "gain_ffn": gain_ffn, "gain_head": gain_head, "cotangent": cotangent}


HIGHEST = lax.Precision.HIGHEST
EPSILON = 1e-06

@jax.custom_vjp
def low(v):
    return lax.optimization_barrier(v.astype(jnp.bfloat16)).astype(jnp.float32)

@jax.custom_vjp
def low_back(v):
    return v

def low_keep(v):
    return (low(v), None)

def low_pass(kept, grad):
    return (grad,)

def back_keep(v):
    return (v, None)

def back_low(kept, grad):
    return (low(grad),)
low.defvjp(low_keep, low_pass)
low_back.defvjp(back_keep, back_low)

def norm_gain(source, gain_vec):
    return source * lax.rsqrt(lax.optimization_barrier(jnp.mean(source * source, -1, keepdims=True)) + EPSILON) * gain_vec

def unit_rows(source):
    return source * lax.rsqrt(lax.optimization_barrier(jnp.sum(source * source, -1, keepdims=True)) + EPSILON)

def gated_norm(mixed_head, gate_pre, gain_vec):
    scale = lax.rsqrt(lax.optimization_barrier(jnp.mean(mixed_head * mixed_head, -1, keepdims=True)) + EPSILON)
    return mixed_head * scale * gain_vec * jax.nn.silu(gate_pre.reshape(mixed_head.shape))

def block_terms(key_rows, beta_rows, decays, doc_rows, doc_before):
    length = key_rows.shape[0]
    cumulative = jnp.cumsum(decays)
    survive = jnp.exp(cumulative) * (doc_rows == doc_before).astype(jnp.float32)
    places = jnp.arange(length)
    linked = (places[:, None] >= places[None, :]) & (doc_rows[:, None] == doc_rows[None, :])
    between = jnp.where(linked, jnp.exp(jnp.where(linked, cumulative[:, None] - cumulative[None, :], 0.0)), 0.0)
    strict = (places[:, None] > places[None, :]).astype(jnp.float32)
    system = jnp.eye(length, dtype=jnp.float32) + beta_rows[:, None] * between * strict * jnp.dot(key_rows, key_rows.T, precision=HIGHEST)
    return (survive, between, system)

def block_step(state_now, pieces):
    queries, key_rows, values, beta_rows, decays, doc_rows, doc_before = pieces
    survive, between, system = block_terms(key_rows, beta_rows, decays, doc_rows, doc_before)
    target = beta_rows[:, None] * (values - survive[:, None] * jnp.dot(key_rows, state_now, precision=HIGHEST))
    update = jax.scipy.linalg.solve_triangular(system, target, lower=True, unit_diagonal=True)
    scores = jnp.dot(queries, key_rows.T, precision=HIGHEST) * between
    output = survive[:, None] * jnp.dot(queries, state_now, precision=HIGHEST) + jnp.dot(scores, update, precision=HIGHEST)
    state_next = survive[-1] * state_now + jnp.dot(key_rows.T, between[-1][:, None] * update, precision=HIGHEST)
    return (state_next, output)

def delta_rule(queries, key_rows, values, beta_rows, decays, doc_rows):
    blocks = queries.shape[0] // STRETCH
    starts = jnp.concatenate([jnp.full((1,), -1, jnp.int32), doc_rows[:-1]]).reshape(blocks, STRETCH)[:, 0]
    pieces = (queries.reshape(blocks, STRETCH, -1), key_rows.reshape(blocks, STRETCH, -1), values.reshape(blocks, STRETCH, -1), beta_rows.reshape(blocks, STRETCH), decays.reshape(blocks, STRETCH), doc_rows.reshape(blocks, STRETCH), starts)
    start_state = jnp.zeros((queries.shape[1], values.shape[1]), jnp.float32)
    _, outputs = lax.scan(jax.checkpoint(block_step), start_state, pieces)
    return outputs.reshape(queries.shape[0], -1)

def conv_core(padded, weight, doc_pad):
    tap_count = weight.shape[0]
    length = padded.shape[1] - (tap_count - 1)
    current = doc_pad[:, tap_count - 1:]
    summed = jnp.zeros((padded.shape[0], length, padded.shape[2]), jnp.float32)
    for offset in range(tap_count):
        first_row = tap_count - 1 - offset
        window = padded[:, first_row:first_row + length]
        same_doc = (doc_pad[:, first_row:first_row + length] == current).astype(jnp.float32)
        summed = summed + weight[offset] * window * same_doc[:, :, None]
    return jax.nn.silu(summed)

def short_conv(before, weight, doc_ids):
    tap_count = weight.shape[0]
    padded = jnp.concatenate([jnp.zeros((before.shape[0], tap_count - 1, before.shape[2]), jnp.float32), before], 1)
    doc_pad = jnp.concatenate([jnp.full((doc_ids.shape[0], tap_count - 1), -1, jnp.int32), doc_ids], 1)
    return conv_core(padded, weight, doc_pad)

def forward(floats, doc_ids):
    hidden_in, w_query, w_key, w_value, w_decay, w_beta, w_gate_out, w_output, w_ffn_gate, w_ffn_up, w_ffn_down, conv_query, conv_key, conv_value, decay_log, decay_bias, gain_attn, gain_ffn, gain_head = floats
    sequences, length = (hidden_in.shape[0], hidden_in.shape[1])
    head_count = decay_log.shape[0]
    normed = low(norm_gain(hidden_in, gain_attn))

    def project(matrix):
        return jnp.einsum('std,de->ste', normed, matrix, precision=HIGHEST)
    query_pre = low_back(low(project(w_query)))
    key_pre = low_back(low(project(w_key)))
    value_pre = low_back(low(project(w_value)))
    decay_pre = low_back(low(project(w_decay)))
    beta_pre = low_back(low(project(w_beta)))
    gate_pre = low_back(project(w_gate_out))
    queries = short_conv(query_pre, conv_query, doc_ids).reshape(sequences, length, head_count, -1)
    key_rows = short_conv(key_pre, conv_key, doc_ids).reshape(sequences, length, head_count, -1)
    values = short_conv(value_pre, conv_value, doc_ids).reshape(sequences, length, head_count, -1)
    queries = unit_rows(queries) * queries.shape[-1] ** (-0.5)
    key_rows = unit_rows(key_rows)
    beta_rows = jax.nn.sigmoid(beta_pre)
    decays = -jnp.exp(decay_log) * jax.nn.softplus(decay_pre + decay_bias)
    per_head = jax.vmap(jax.vmap(delta_rule, (1, 1, 1, 1, 1, None), 1), (0, 0, 0, 0, 0, 0), 0)
    mixed_head = low_back(low(per_head(queries, key_rows, values, beta_rows, decays, doc_ids)))
    normed_head = low(gated_norm(mixed_head, gate_pre, gain_head).reshape(sequences, length, -1))
    attention = low_back(jnp.einsum('ste,ed->std', normed_head, w_output, precision=HIGHEST))
    middle = hidden_in + attention
    ffn_in = low(norm_gain(middle, gain_ffn))
    gate_val = low_back(jnp.einsum('std,df->stf', ffn_in, w_ffn_gate, precision=HIGHEST))
    up_val = low_back(jnp.einsum('std,df->stf', ffn_in, w_ffn_up, precision=HIGHEST))
    inner_act = low(jax.nn.silu(gate_val) * up_val)
    return middle + jnp.einsum('stf,fd->std', inner_act, w_ffn_down, precision=HIGHEST)

def reference(hidden_in, doc_ids, w_query, w_key, w_value, w_decay, w_beta, w_gate_out, w_output, w_ffn_gate, w_ffn_up, w_ffn_down, conv_query, conv_key, conv_value, decay_log, decay_bias, gain_attn, gain_ffn, gain_head, cotangent):
    floats = tuple((entry.astype(jnp.float32) for entry in (hidden_in, w_query, w_key, w_value, w_decay, w_beta, w_gate_out, w_output, w_ffn_gate, w_ffn_up, w_ffn_down, conv_query, conv_key, conv_value, decay_log, decay_bias, gain_attn, gain_ffn, gain_head)))
    result, pullback = jax.vjp(lambda *entries: forward(entries, doc_ids), *floats)
    gradients = pullback(cotangent.astype(jnp.float32))
    return (result.astype(jnp.bfloat16), gradients[0].astype(jnp.bfloat16), gradients[1], gradients[2], gradients[3], gradients[4], gradients[5], gradients[6], gradients[7], gradients[8], gradients[9], gradients[10], gradients[11], gradients[12], gradients[13], gradients[14], gradients[15], gradients[16], gradients[17], gradients[18])
```

```python
import jax
import jax.numpy as jnp
from jax import lax
from jax.experimental import pallas as pl
from jax.experimental.pallas import tpu as pltpu
from jax.sharding import PartitionSpec as P

STRETCH = 64
LANES = 128
HIGHEST = lax.Precision.HIGHEST
EPSILON = 1e-06
bf16, f32 = jnp.bfloat16, jnp.float32
VMEM_LIMIT = 48 * 1024 * 1024


def mm(a, b, ca=1, cb=0):
    return lax.dot_general(
        a, b, (((ca,), (cb,)), ((), ())), precision=HIGHEST, preferred_element_type=f32
    )


def lower_strict():
    rows = lax.broadcasted_iota(jnp.int32, (STRETCH, STRETCH), 0)
    cols = lax.broadcasted_iota(jnp.int32, (STRETCH, STRETCH), 1)
    return (rows > cols).astype(f32), (rows == cols).astype(f32)


def block_rows(n):
    return pl.ds(pl.multiple_of(n * STRETCH, STRETCH), STRETCH)


def maps_kernel(k_ref, v_ref, aux_ref, between_ref, x_ref, end_ref, w_ref, u_ref, inv_ref):
    sequences, length, dk = k_ref.shape
    dv = v_ref.shape[2]
    blocks = length // STRETCH
    strict, unit = lower_strict()

    def prepare_block(n, carry):
        rows = block_rows(n)
        for s in range(sequences):
            k = k_ref[s, rows]
            beta = aux_ref[s, rows, 0:1]
            gamma = aux_ref[s, rows, 1:2]
            power = -beta * (between_ref[s, n] * strict) * mm(k, k, 1, 1)
            inverse = unit + power
            for level in range(STRETCH.bit_length() - 2):
                power = mm(power, power)
                inverse = inverse + mm(inverse, power)
            inv_ref[s, n] = inverse
            w_ref[s, rows] = mm(inverse, beta * gamma * k)
            u_ref[s, rows] = mm(inverse, beta * v_ref[s, rows])
        return carry

    lax.fori_loop(0, blocks, prepare_block, 0)

    wide = (dk, dk + dv)
    start = (
        lax.broadcasted_iota(jnp.int32, wide, 0) == lax.broadcasted_iota(jnp.int32, wide, 1)
    ).astype(f32)

    def chain_block(n, states):
        rows = block_rows(n)
        after = []
        for s in range(sequences):
            x = states[s]
            x_ref[s, n] = x
            gone = mm(w_ref[s, rows], x)
            update = jnp.concatenate([-gone[:, :dk], u_ref[s, rows] - gone[:, dk:]], 1)
            rho = aux_ref[s, rows, 2:3]
            last = aux_ref[s, rows, 1:2][STRETCH - 1 :]
            after.append(last * x + mm(k_ref[s, rows], rho * update, 0, 0))
        return tuple(after)

    ends = lax.fori_loop(0, blocks, chain_block, (start,) * sequences)
    for s in range(sequences):
        end_ref[s] = ends[s].astype(end_ref.dtype)


def run_kernel(
    place_ref, maps_ref, x_ref, q_ref, k_ref, aux_ref, between_ref, w_ref, u_ref,
    out_ref, state_ref, update_ref,
):
    sequences, length, dk = k_ref.shape
    dv = u_ref.shape[2]
    blocks = length // STRETCH

    def enter(hop, states):
        return tuple(
            mm(maps_ref[hop, s, :, :dk].astype(f32), states[s])
            + maps_ref[hop, s, :, dk:].astype(f32)
            for s in range(sequences)
        )

    entry = lax.fori_loop(
        0, place_ref[0], enter, (jnp.zeros((dk, dv), f32),) * sequences
    )

    def run_block(n, carry):
        rows = block_rows(n)
        for s in range(sequences):
            q, k = q_ref[s, rows], k_ref[s, rows]
            state = mm(x_ref[s, n, :, :dk], entry[s]) + x_ref[s, n, :, dk:]
            update = u_ref[s, rows] - mm(w_ref[s, rows], state)
            scores = mm(q, k, 1, 1) * between_ref[s, n]
            out = aux_ref[s, rows, 1:2] * mm(q, state) + mm(scores, update)
            state_ref[s, n] = state
            update_ref[s, rows] = update
            out_ref[s, rows] = out.astype(out_ref.dtype)
        return carry

    lax.fori_loop(0, blocks, run_block, 0)


def back_local_kernel(
    q_ref, k_ref, aux_ref, between_ref, w_ref, grad_ref, through_ref, inflow_ref, local_ref
):
    sequences, length, dk = k_ref.shape
    dv = grad_ref.shape[2]
    blocks = length // STRETCH

    def prepare_block(n, carry):
        rows = block_rows(n)
        for s in range(sequences):
            q, k = q_ref[s, rows], k_ref[s, rows]
            grad = grad_ref[s, rows].astype(f32)
            scores = mm(q, k, 1, 1) * between_ref[s, n]
            through_ref[s, rows] = mm(scores, grad, 0, 0)
            inflow_ref[s, n] = mm(q, aux_ref[s, rows, 1:2] * grad, 0, 0)
        return carry

    lax.fori_loop(0, blocks, prepare_block, 0)

    def chain_block(back, states):
        n = blocks - 1 - back
        rows = block_rows(n)
        after = []
        for s in range(sequences):
            rho = aux_ref[s, rows, 2:3]
            last = aux_ref[s, rows, 1:2][STRETCH - 1 :]
            grad_update = through_ref[s, rows] + rho * mm(k_ref[s, rows], states[s])
            after.append(
                last * states[s] + inflow_ref[s, n] - mm(w_ref[s, rows], grad_update, 0, 0)
            )
        return tuple(after)

    ends = lax.fori_loop(0, blocks, chain_block, (jnp.zeros((dk, dv), f32),) * sequences)
    for s in range(sequences):
        local_ref[s] = ends[s].astype(local_ref.dtype)


def back_kernel(
    place_ref, maps_ref, locals_ref, q_ref, k_ref, v_ref, aux_ref, between_ref, w_ref, inv_ref,
    state_ref, update_ref, grad_ref, through_ref, inflow_ref,
    grad_q_ref, grad_k_ref, grad_v_ref, grad_aux_ref, grad_row_ref,
):
    sequences, length, dk = k_ref.shape
    dv = v_ref.shape[2]
    blocks = length // STRETCH
    segments = maps_ref.shape[0]
    strict, _ = lower_strict()
    at_last = lax.broadcasted_iota(jnp.int32, (STRETCH, 1), 0) == STRETCH - 1
    lane = lax.broadcasted_iota(jnp.int32, (STRETCH, grad_aux_ref.shape[2]), 1)

    def leave(hop, states):
        source = segments - 1 - hop
        return tuple(
            mm(maps_ref[source, s, :, :dk].astype(f32), states[s], 0, 0)
            + locals_ref[source, s].astype(f32)
            for s in range(sequences)
        )

    exits = lax.fori_loop(
        0, segments - 1 - place_ref[0], leave, (jnp.zeros((dk, dv), f32),) * sequences
    )

    def row_sum(a):
        return jnp.sum(a, axis=1, keepdims=True)

    def chain_block(back, states):
        n = blocks - 1 - back
        rows = block_rows(n)
        after = []
        for s in range(sequences):
            grad_next = states[s]
            q, k, v = q_ref[s, rows], k_ref[s, rows], v_ref[s, rows]
            beta, gamma, rho = (aux_ref[s, rows, c : c + 1] for c in range(3))
            last = gamma[STRETCH - 1 :]
            between = between_ref[s, n]
            state, update = state_ref[s, n], update_ref[s, rows]
            grad = grad_ref[s, rows].astype(f32)
            key_next = mm(k, grad_next)
            grad_update = through_ref[s, rows] + rho * key_next
            after.append(last * grad_next + inflow_ref[s, n] - mm(w_ref[s, rows], grad_update, 0, 0))
            grad_target = mm(inv_ref[s, n], grad_update, 0, 0)
            key_state, query_state = mm(k, state), mm(q, state)
            key_key, query_key = mm(k, k, 1, 1), mm(q, k, 1, 1)
            grad_query_key = mm(grad, update, 1, 1) * between
            grad_system = -mm(grad_target, update, 1, 1) * strict * between
            grad_key_key = beta * grad_system
            grad_key_state = -(beta * gamma) * grad_target
            grad_q_ref[s, rows] = gamma * mm(grad, state, 1, 1) + mm(grad_query_key, k)
            grad_k_ref[s, rows] = (
                mm(grad_query_key, q, 0, 0)
                + mm(rho * update, grad_next, 1, 1)
                + mm(grad_key_key, k)
                + mm(grad_key_key, k, 0, 0)
                + mm(grad_key_state, state, 1, 1)
            )
            grad_v_ref[s, rows] = beta * grad_target
            grad_beta = row_sum(grad_system * key_key) + row_sum(
                grad_target * (v - gamma * key_state)
            )
            grad_gamma = row_sum(grad * query_state) - beta * row_sum(grad_target * key_state)
            spread = grad_query_key * query_key + grad_key_key * key_key
            grad_rho = row_sum(key_next * update) * rho
            at_end = jnp.sum(grad_rho) + jnp.sum(row_sum(state * grad_next) * last)
            grad_cumulative = (
                row_sum(spread) + grad_gamma * gamma - grad_rho + jnp.where(at_last, at_end, 0.0)
            )
            grad_row_ref[s, pl.ds(n, 1)] = jnp.sum(spread, axis=0, keepdims=True)
            grad_aux_ref[s, rows] = jnp.where(lane == 0, grad_beta, grad_cumulative)
        return tuple(after)

    lax.fori_loop(0, blocks, chain_block, exits)


def kernel_call(body, out_shape, *operands, scalars=0):
    whole = pl.BlockSpec(memory_space=pltpu.VMEM)
    return pl.pallas_call(
        body,
        out_shape=out_shape,
        in_specs=[pl.BlockSpec(memory_space=pltpu.SMEM)] * scalars
        + [whole] * (len(operands) - scalars),
        out_specs=jax.tree.map(lambda _: whole, out_shape),
        compiler_params=pltpu.CompilerParams(vmem_limit_bytes=VMEM_LIMIT),
    )(*operands)


def shaped(shape, kind=f32):
    return jax.ShapeDtypeStruct(shape, kind)


def norm_gain(source, gain_vec):
    return source * lax.rsqrt(jnp.mean(source * source, -1, keepdims=True) + EPSILON) * gain_vec


def unit_rows(source):
    return source * lax.rsqrt(jnp.sum(source * source, -1, keepdims=True) + EPSILON)


def gated_norm(mixed_head, gate_pre, gain_vec):
    scale = lax.rsqrt(jnp.mean(mixed_head * mixed_head, -1, keepdims=True) + EPSILON)
    return mixed_head * scale * gain_vec * jax.nn.silu(gate_pre)


def conv_core(padded, weight, doc_pad):
    tap_count = weight.shape[0]
    length = padded.shape[1] - (tap_count - 1)
    current = doc_pad[:, tap_count - 1 :]
    summed = jnp.zeros((padded.shape[0], length, padded.shape[2]), f32)
    for offset in range(tap_count):
        first_row = tap_count - 1 - offset
        window = padded[:, first_row : first_row + length]
        same_doc = (doc_pad[:, first_row : first_row + length] == current).astype(f32)
        summed = summed + weight[offset] * window * same_doc[:, :, None]
    return jax.nn.silu(summed)


def prepare(packed_ext, decay_head, beta_head, taps, decay_log, decay_bias, doc_ext, dk):
    mixed = conv_core(packed_ext, taps, doc_ext)
    queries = unit_rows(mixed[:, :, :dk]) * dk ** (-0.5)
    key_rows = unit_rows(mixed[:, :, dk : 2 * dk])
    values = mixed[:, :, 2 * dk :]
    beta_rows = jax.nn.sigmoid(beta_head)
    decays = -jnp.exp(decay_log) * jax.nn.softplus(decay_head + decay_bias)
    sequences, length = decays.shape
    cumulative = jnp.cumsum(decays.reshape(sequences, length // STRETCH, STRETCH), -1)
    return queries, key_rows, values, beta_rows, cumulative


def block_gates(cumulative, doc_blocks, doc_starts):
    places = jnp.arange(STRETCH)
    linked = (places[:, None] >= places[None, :]) & (
        doc_blocks[..., :, None] == doc_blocks[..., None, :]
    )
    apart = cumulative[..., :, None] - cumulative[..., None, :]
    between = jnp.where(linked, jnp.exp(jnp.where(linked, apart, 0.0)), 0.0)
    survive = jnp.exp(cumulative) * (doc_blocks == doc_starts[..., None]).astype(f32)
    return survive, between, between[..., -1, :]


def each_peer(axis, action):
    count, me = lax.axis_size(axis), lax.axis_index(axis)

    def step(distance, carry):
        action(distance, lax.rem(me + distance, count), lax.rem(me + count - distance, count))
        return carry

    lax.fori_loop(1, count, step, 0)


def owner_targets(action):
    hd, me, head = lax.axis_size("hd"), lax.axis_index("cp"), lax.axis_index("hd")
    cp = lax.axis_size("cp")
    share = cp // hd

    def step(turn, carry):
        piece = lax.rem(turn + me, cp)
        to = (share * head + piece // hd, lax.rem(piece, hd))
        action(piece, to, (to[0] == me) & (to[1] == head))
        return carry

    lax.fori_loop(0, cp, step, 0)


def owner_sources(action):
    hd, me, head = lax.axis_size("hd"), lax.axis_index("cp"), lax.axis_index("hd")
    cp = lax.axis_size("cp")
    column = me // (cp // hd)

    def step(source, carry):
        action(source, (source, column), (source == me) & (column == head))
        return carry

    lax.fori_loop(0, cp, step, 0)


def meet(axes, owners=False):
    barrier = pltpu.get_barrier_semaphore()
    total = 0
    for axis in axes:
        each_peer(
            axis,
            lambda _, to, source, axis=axis: pl.semaphore_signal(
                barrier, inc=1, device_id={axis: to}, device_id_type=pl.DeviceIdType.MESH
            ),
        )
        total += lax.axis_size(axis) - 1
    if owners:
        cp, hd = lax.axis_size("cp"), lax.axis_size("hd")

        def greet(source, at, own):
            @pl.when(jnp.logical_not(own))
            def _():
                pl.semaphore_signal(
                    barrier, inc=1, device_id=at, device_id_type=pl.DeviceIdType.MESH
                )

        owner_sources(greet)
        alone = lax.axis_index("cp") // (cp // hd) == lax.axis_index("hd")
        total = total + cp - alone.astype(jnp.int32)
    pl.semaphore_wait(barrier, total)


def remote(src, dst, send, recv, target):
    return pltpu.make_async_remote_copy(
        src_ref=src,
        dst_ref=dst,
        send_sem=send,
        recv_sem=recv,
        device_id=target,
        device_id_type=pl.DeviceIdType.MESH,
    )


class Exchange:
    def __init__(self, axis, source, landing, send, recv, local):
        self.axis, self.source, self.landing = axis, source, landing
        self.send, self.recv = send, recv
        me = lax.axis_index(axis)
        self.own = pltpu.make_async_copy(source(me), landing(me), local)

    def copy(self, distance, block, place, to):
        return remote(
            block, place, self.send.at[distance], self.recv.at[distance], {self.axis: to}
        )

    def start(self):
        me = lax.axis_index(self.axis)
        each_peer(
            self.axis,
            lambda distance, to, source: self.copy(
                distance, self.source(to), self.landing(me), to
            ).start(),
        )
        self.own.start()

    def arrive(self):
        each_peer(
            self.axis,
            lambda distance, to, source: self.copy(
                distance, self.source(to), self.landing(source), to
            ).wait_recv(),
        )
        self.own.wait()

    def leave(self):
        each_peer(
            self.axis,
            lambda distance, to, source: self.copy(
                distance, self.source(to), self.landing(source), to
            ).wait_send(),
        )


class OwnerExchange:
    def __init__(self, source, landing, send, recv, local):
        self.source, self.landing = source, landing
        self.send, self.recv, self.local = send, recv, local

    def start(self):
        me = lax.axis_index("cp")

        def go(piece, to, own):
            @pl.when(own)
            def _():
                pltpu.make_async_copy(self.source(piece), self.landing(me), self.local).start()

            @pl.when(jnp.logical_not(own))
            def _():
                remote(
                    self.source(piece), self.landing(me), self.send.at[piece], self.recv.at[me], to
                ).start()

        owner_targets(go)

    def arrive(self):
        def get(source, at, own):
            @pl.when(own)
            def _():
                pltpu.make_async_copy(
                    self.source(source), self.landing(source), self.local
                ).wait()

            @pl.when(jnp.logical_not(own))
            def _():
                remote(
                    self.source(source),
                    self.landing(source),
                    self.send.at[source],
                    self.recv.at[source],
                    at,
                ).wait_recv()

        owner_sources(get)

    def leave(self):
        def done(piece, to, own):
            @pl.when(jnp.logical_not(own))
            def _():
                remote(
                    self.source(piece), self.landing(piece), self.send.at[piece],
                    self.recv.at[piece], to,
                ).wait_send()

        owner_targets(done)


def sems(*counts):
    found = []
    for count in counts:
        found += [pltpu.SemaphoreType.DMA((count,))] * 2 + [pltpu.SemaphoreType.DMA]
    return found


def token_rows(ref, index, tokens):
    return ref.at[:, pl.ds(pl.multiple_of(index * tokens, tokens), tokens)]


def lead_rows(ref, index, rows):
    return ref.at[pl.ds(pl.multiple_of(index * rows, rows), rows)]


def comm_call(body, out_shape, places, operands, spots, scratch, number):
    kinds = {"any": pl.ANY, "vmem": pltpu.VMEM}
    return pl.pallas_call(
        body,
        out_shape=out_shape,
        in_specs=[pl.BlockSpec(memory_space=kinds[k]) for k in places],
        out_specs=tuple(pl.BlockSpec(memory_space=kinds[k]) for k in spots),
        scratch_shapes=scratch,
        compiler_params=pltpu.CompilerParams(
            collective_id=number, has_side_effects=True, vmem_limit_bytes=VMEM_LIMIT
        ),
    )(*operands)


def open_kernel(hidden_ref, front_ref, hidden_all_ref, front_all_ref, *flags):
    tokens, shard = hidden_ref.shape[1], front_ref.shape[0]
    meet(("hd", "cp"))
    moves = (
        Exchange(
            "hd", lambda to: hidden_ref, lambda at: token_rows(hidden_all_ref, at, tokens), *flags[:3]
        ),
        Exchange(
            "cp", lambda to: front_ref, lambda at: lead_rows(front_all_ref, at, shard), *flags[3:6]
        ),
    )
    for move in moves:
        move.start()
    for move in moves:
        move.arrive()
        move.leave()


def stack_kernel(part_ref, all_ref, *flags):
    meet(("cp",))
    move = Exchange("cp", lambda to: part_ref, lambda at: all_ref.at[at], *flags)
    move.start()
    move.arrive()
    move.leave()


def gather_stack(part, number):
    cp = lax.axis_size("cp")
    return comm_call(
        stack_kernel, (shaped((cp, *part.shape), part.dtype),), ("any",), (part,), ("any",),
        sems(cp), number,
    )[0]


def added(landed_ref):
    total = landed_ref[0].astype(f32)
    for index in range(1, landed_ref.shape[0]):
        total += landed_ref[index].astype(f32)
    return total


def spread_own(own_ref, all_ref, tokens, flags):
    move = Exchange("hd", lambda to: own_ref, lambda at: token_rows(all_ref, at, tokens), *flags)
    move.start()
    return move


def middle_kernel(
    partial_ref, hidden_ref, gain_ref, middle_ref, ffn_all_ref, landed_ref, own_ref, *flags
):
    tokens = hidden_ref.shape[1]
    meet(("hd",))
    move = Exchange(
        "hd", lambda to: token_rows(partial_ref, to, tokens), lambda at: landed_ref.at[at], *flags[:3]
    )
    move.start()
    move.arrive()
    middle = hidden_ref[...].astype(f32) + added(landed_ref)
    middle_ref[...] = middle
    own_ref[...] = norm_gain(middle, gain_ref[...]).astype(bf16)
    after = spread_own(own_ref, ffn_all_ref, tokens, flags[3:6])
    move.leave()
    after.arrive()
    after.leave()


def norm_back(source, gain_vec, grad):
    scale = lax.rsqrt(jnp.mean(source * source, -1, keepdims=True) + EPSILON)
    lifted = grad * gain_vec
    mixed = jnp.mean(source * lifted, -1, keepdims=True)
    return scale * lifted - source * (scale * scale * scale) * mixed, source * scale * grad


def ffn_back_kernel(
    out_part_ref, grad_part_ref, middle_ref, cot_ref, gain_ref,
    block_ref, grad_middle_ref, grad_gain_ref, grad_all_ref,
    out_landed_ref, grad_landed_ref, own_ref, *flags
):
    tokens = middle_ref.shape[1]
    meet(("hd",))
    moves = [
        Exchange(
            "hd",
            lambda to, ref=ref: token_rows(ref, to, tokens),
            lambda at, landed=landed: landed.at[at],
            *flags[3 * n : 3 * n + 3],
        )
        for n, (ref, landed) in enumerate(
            ((grad_part_ref, grad_landed_ref), (out_part_ref, out_landed_ref))
        )
    ]
    for move in moves:
        move.start()
    moves[0].arrive()
    middle = middle_ref[...]
    back, gain_terms = norm_back(middle, gain_ref[...], added(grad_landed_ref))
    grad_middle = cot_ref[...].astype(f32) + back
    grad_middle_ref[...] = grad_middle
    own_ref[...] = grad_middle.astype(bf16)
    after = spread_own(own_ref, grad_all_ref, tokens, flags[6:9])
    grad_gain_ref[...] = jnp.sum(jnp.sum(gain_terms, axis=0), axis=0, keepdims=True)
    moves[1].arrive()
    block_ref[...] = (middle + added(out_landed_ref)).astype(bf16)
    for move in moves:
        move.leave()
    after.arrive()
    after.leave()


def close_kernel(
    normed_part_ref, front_ref, ffn_ref, output_ref, down_ref, small_ref,
    hidden_ref, grad_middle_ref, gain_ref,
    grad_in_ref, front_all_ref, ffn_all_ref, output_all_ref, down_all_ref, small_sum_ref,
    normed_landed, front_landed, ffn_landed, output_landed, down_landed, small_landed,
    front_own, ffn_own, output_own, down_own, *flags
):
    tokens = hidden_ref.shape[1]
    shard = front_own.shape[0]
    meet(("hd", "cp"), owners=True)

    def over_cp(ref, landed, flags):
        return Exchange("cp", lambda to: lead_rows(ref, to, shard), lambda at: landed.at[at], *flags)

    def to_owner(ref, landed, flags):
        return OwnerExchange(lambda piece: ref.at[piece], lambda at: landed.at[at], *flags)

    groups = [flags[3 * n : 3 * n + 3] for n in range(10)]
    normed_move = Exchange(
        "hd",
        lambda to: token_rows(normed_part_ref, to, tokens),
        lambda at: normed_landed.at[at],
        *groups[0],
    )
    weights = [
        (to_owner(down_ref, down_landed, groups[1]), down_landed, down_own, down_all_ref),
        (over_cp(ffn_ref, ffn_landed, groups[2]), ffn_landed, ffn_own, ffn_all_ref),
        (to_owner(output_ref, output_landed, groups[3]), output_landed, output_own, output_all_ref),
        (over_cp(front_ref, front_landed, groups[4]), front_landed, front_own, front_all_ref),
    ]
    small_move = Exchange(
        "cp", lambda to: small_ref, lambda at: small_landed.at[at], *groups[5]
    )
    normed_move.start()
    for move, _, _, _ in weights:
        move.start()
    small_move.start()
    spreads = []
    for n, (move, landed, own, everywhere) in enumerate(weights):
        move.arrive()
        own[...] = added(landed).astype(bf16)
        spread = Exchange(
            "hd",
            lambda to, own=own: own,
            lambda at, everywhere=everywhere: everywhere.at[at],
            *groups[6 + n],
        )
        spread.start()
        spreads.append(spread)
    normed_move.arrive()
    back, _ = norm_back(hidden_ref[...].astype(f32), gain_ref[...], added(normed_landed))
    grad_in_ref[...] = (grad_middle_ref[...] + back).astype(bf16)
    small_move.arrive()
    small_sum_ref[...] = added(small_landed)
    for move in (normed_move, small_move, *(entry[0] for entry in weights)):
        move.leave()
    for spread in spreads:
        spread.arrive()
        spread.leave()


def passed_along(block, axis, distance):
    devices = range(lax.axis_size(axis))
    route = [(i - distance, i) for i in devices if i - distance in devices]
    return lax.ppermute(block, axis, route)


def head_rows(shard, place):
    cp, hd = lax.axis_size("cp"), lax.axis_size("hd")
    share = cp // hd
    got = []
    for turn in range(share):
        route = [
            (i * hd + j, (share * j + (turn + i) % share) * hd + i // share)
            for i in range(cp)
            for j in range(hd)
        ]
        got.append(lax.ppermute(shard, ("cp", "hd"), route))
    stack = jnp.stack(got)
    order = (place - jnp.arange(share)) % share
    return jnp.take(stack, order, axis=0).reshape(share * shard.shape[0], shard.shape[1])


def on_device(
    hidden_in, doc_ids, w_query, w_key, w_value, w_decay, w_beta, w_gate_out, w_output,
    w_ffn_gate, w_ffn_up, w_ffn_down, conv_query, conv_key, conv_value, decay_log, decay_bias,
    gain_attn, gain_ffn, gain_head, cotangent,
):
    place, head = lax.axis_index("cp"), lax.axis_index("hd")
    cp, hd = lax.axis_size("cp"), lax.axis_size("hd")
    sequences, tokens, width = hidden_in.shape
    shard = w_query.shape[0]
    dk, dv = w_query.shape[1] // hd, w_value.shape[1] // hd
    ff = w_ffn_gate.shape[1] // hd
    ffp = -(-ff // LANES) * LANES
    qkv = 2 * dk + dv
    side = qkv + dv
    span = tokens * hd
    blocks = span // STRETCH

    def part(weight):
        cols = weight.shape[1] // hd
        return lax.dynamic_slice_in_dim(weight, head * cols, cols, 1)

    def ff_pad(weight):
        return jnp.pad(part(weight), ((0, 0), (0, ffp - ff)))

    head_share = gain_head.shape[0]
    side_cols = jnp.stack(
        [
            part(w_decay)[:, 0],
            part(w_beta)[:, 0],
            gain_attn,
            gain_ffn,
            jnp.pad(gain_head, (0, shard - head_share)),
        ],
        1,
    )
    front = jnp.concatenate(
        [
            part(w_query),
            part(w_key),
            part(w_value),
            part(w_gate_out),
            jnp.pad(side_cols, ((0, 0), (0, LANES - side_cols.shape[1]))),
        ],
        1,
    )
    hidden_all, front_full = comm_call(
        open_kernel,
        (shaped((sequences, span, width), bf16), shaped((width, front.shape[1]), bf16)),
        ("any", "any"),
        (hidden_in, front),
        ("any", "any"),
        sems(hd, cp),
        1,
    )
    output_part = head_rows(w_output, place)
    ffn_full = lax.all_gather(
        jnp.concatenate([ff_pad(w_ffn_gate), ff_pad(w_ffn_up)], 1), "cp", axis=0, tiled=True
    )
    down_part = jnp.pad(head_rows(w_ffn_down, place), ((0, ffp - ff), (0, 0)))
    cot_all = lax.all_gather(cotangent, "hd", axis=1, tiled=True)

    attn_gain = front_full[:, side + 2].astype(f32)
    ffn_gain = front_full[:, side + 3].astype(f32)
    head_gain = front_full[:, side + 4].reshape(cp, shard)[:, :head_share].reshape(-1).astype(f32)

    def dot(a, b, spec):
        return jnp.einsum(spec, a, b, preferred_element_type=f32)

    inputs_all = hidden_all.astype(f32)
    scale_all = lax.rsqrt(jnp.mean(inputs_all * inputs_all, -1, keepdims=True) + EPSILON)
    normed = (inputs_all * scale_all * attn_gain).astype(bf16)
    projected = dot(normed, front_full, "std,de->ste")
    packed = projected[:, :, :qkv].astype(bf16)
    gate_pre = projected[:, :, qkv:side]
    decay_head = projected[:, :, side].astype(bf16).astype(f32)
    beta_head = projected[:, :, side + 1].astype(bf16).astype(f32)

    margin = conv_query.shape[0] - 1
    rim = passed_along(packed[:, -margin:], "cp", 1)
    doc_pad = jnp.concatenate([jnp.full((sequences, margin), -1, jnp.int32), doc_ids], 1)
    doc_ext = lax.dynamic_slice_in_dim(doc_pad, place * span, span + margin, 1)
    doc_blocks = doc_ext[:, margin:].reshape(sequences, blocks, STRETCH)
    doc_starts = doc_ext[:, margin - 1 : -1].reshape(sequences, blocks, STRETCH)[:, :, 0]
    taps = jnp.concatenate([conv_query, conv_key, conv_value], 1).astype(f32)
    prepared, prepare_pull = jax.vjp(
        lambda *entries: prepare(*entries, doc_ext, dk),
        jnp.concatenate([rim, packed], 1).astype(f32),
        decay_head,
        beta_head,
        taps,
        decay_log.astype(f32),
        decay_bias.astype(f32),
    )
    queries, key_rows, values, beta_rows, cumulative = prepared
    survive, between, rho = block_gates(cumulative, doc_blocks, doc_starts)
    flat = (sequences, span)
    aux = jnp.stack([beta_rows, survive.reshape(flat), rho.reshape(flat)], -1)
    aux = jnp.pad(aux, ((0, 0), (0, 0), (0, 5)))
    prefix, segment, weighted, written, inverse = kernel_call(
        maps_kernel,
        (
            shaped((sequences, blocks, dk, dk + dv)),
            shaped((sequences, dk, dk + dv), bf16),
            shaped((sequences, span, dk)),
            shaped((sequences, span, dv)),
            shaped((sequences, blocks, STRETCH, STRETCH)),
        ),
        key_rows, values, aux, between,
    )
    segments = gather_stack(segment, 2)
    place_vec = place.reshape(1).astype(jnp.int32)
    mixed, states, updates = kernel_call(
        run_kernel,
        (
            shaped((sequences, span, dv), bf16),
            shaped((sequences, blocks, dk, dv)),
            shaped((sequences, span, dv)),
        ),
        place_vec, segments, prefix, queries, key_rows, aux, between, weighted, written,
        scalars=1,
    )
    mixed_float = mixed.astype(f32)
    normed_head, gated_pull = jax.vjp(gated_norm, mixed_float, gate_pre, head_gain)
    normed_head = normed_head.astype(bf16)
    landing = pltpu.VMEM((hd, sequences, tokens, width), bf16)
    own_tokens = pltpu.VMEM((sequences, tokens, width), bf16)
    ffn_gain = ffn_gain[None]
    middle, ffn_all = comm_call(
        middle_kernel,
        (shaped(hidden_in.shape), shaped((sequences, span, width), bf16)),
        ("any", "vmem", "vmem"),
        (dot(normed_head, output_part, "ste,ed->std").astype(bf16), hidden_in, ffn_gain),
        ("vmem", "any"),
        [landing, own_tokens, *sems(hd, hd)],
        4,
    )
    gate_up = dot(ffn_all, ffn_full, "std,df->stf")
    inner, swiglu_pull = jax.vjp(
        lambda both: jax.nn.silu(both[..., :ffp]) * both[..., ffp:], gate_up
    )
    inner = inner.astype(bf16)
    grad_inner = dot(cot_all, down_part, "std,fd->stf")
    grad_gate_up = swiglu_pull(grad_inner)[0].astype(bf16)
    block_out, grad_middle, grad_ffn_gain, grad_attention = comm_call(
        ffn_back_kernel,
        (
            shaped(hidden_in.shape, bf16),
            shaped(hidden_in.shape),
            shaped((1, width)),
            shaped((sequences, span, width), bf16),
        ),
        ("any", "any", "vmem", "vmem", "vmem"),
        (
            dot(inner, down_part, "stf,fd->std").astype(bf16),
            dot(grad_gate_up, ffn_full, "stf,df->std").astype(bf16),
            middle, cotangent, ffn_gain,
        ),
        ("vmem", "vmem", "vmem", "any"),
        [landing, landing, own_tokens, *sems(hd, hd, hd)],
        5,
    )

    def weight_grad(left_side, right_side):
        return dot(left_side, right_side, "std,ste->de")

    def pieces(grad):
        rows = grad.shape[0] // cp
        split = grad.reshape(cp, rows, width)
        return jnp.pad(split, ((0, 0), (0, -rows % 16), (0, 0))).astype(bf16)

    grad_ffn = weight_grad(ffn_all, grad_gate_up).astype(bf16)
    grad_down = pieces(weight_grad(inner, cot_all)[:ff])

    grad_normed_head = dot(grad_attention, output_part, "std,ed->ste")
    grad_output = pieces(weight_grad(normed_head, grad_attention))
    grad_mixed, grad_gate_pre, grad_head_gain = gated_pull(grad_normed_head)
    grad_mixed = grad_mixed.astype(bf16)
    through, inflow, local = kernel_call(
        back_local_kernel,
        (
            shaped((sequences, span, dv)),
            shaped((sequences, blocks, dk, dv)),
            shaped((sequences, dk, dv), bf16),
        ),
        queries, key_rows, aux, between, weighted, grad_mixed,
    )
    locals_all = gather_stack(local, 3)
    grad_q, grad_k, grad_v, grad_aux, grad_row = kernel_call(
        back_kernel,
        (
            shaped((sequences, span, dk)),
            shaped((sequences, span, dk)),
            shaped((sequences, span, dv)),
            shaped((sequences, span, 8)),
            shaped((sequences, blocks, STRETCH)),
        ),
        place_vec, segments, locals_all, queries, key_rows, values, aux, between, weighted,
        inverse, states, updates, grad_mixed, through, inflow,
        scalars=1,
    )
    grad_cumulative = grad_aux[:, :, 1].reshape(sequences, blocks, STRETCH) - grad_row
    grad_ext, grad_decay, grad_beta, grad_taps, grad_log, grad_bias = prepare_pull(
        (grad_q, grad_k, grad_v, grad_aux[:, :, 0], grad_cumulative)
    )
    back = passed_along(grad_ext[:, :margin], "cp", -1)
    grad_packed = grad_ext[:, margin:].at[:, -margin:].add(back).astype(bf16)
    grad_projected = jnp.concatenate(
        [
            grad_packed,
            grad_gate_pre.astype(bf16),
            jnp.pad(
                jnp.stack([grad_decay, grad_beta], -1).astype(bf16),
                ((0, 0), (0, 0), (0, LANES - 2)),
            ),
        ],
        -1,
    )
    partial_normed = dot(grad_projected, front_full, "ste,de->std")
    grad_attn_gain = jnp.sum(inputs_all * scale_all * partial_normed, (0, 1))
    grad_front = weight_grad(normed, grad_projected)
    spread_gain = jnp.pad(
        grad_head_gain.reshape(cp, head_share), ((0, 0), (0, shard - head_share))
    ).reshape(-1)
    gains = jnp.stack([grad_attn_gain, grad_ffn_gain[0], spread_gain], 1)
    grad_front = jnp.concatenate(
        [grad_front[:, : side + 2], gains, grad_front[:, side + 5 :]], 1
    )
    small = jnp.concatenate(
        [
            grad_taps,
            jnp.pad(jnp.stack([grad_log, grad_bias], 1), ((0, 0), (0, qkv - 2))),
        ],
        0,
    )
    small = jnp.pad(small, ((0, -small.shape[0] % 8), (0, 0)))
    weight_parts = (grad_front.astype(bf16), grad_ffn, grad_output, grad_down)
    shares = ((shard, grad_front.shape[1]), (shard, 2 * ffp), grad_output.shape[1:], grad_down.shape[1:])
    grad_in, grad_front, grad_ffn, grad_output, grad_down, small = comm_call(
        close_kernel,
        (shaped(hidden_in.shape, bf16), *(shaped((hd, *share), bf16) for share in shares), shaped(small.shape)),
        ("any",) * 6 + ("vmem",) * 3,
        (partial_normed.astype(bf16), *weight_parts, small, hidden_in, grad_middle, attn_gain[None]),
        ("vmem",) + ("any",) * 4 + ("vmem",),
        [
            landing,
            *(pltpu.VMEM((cp, *share), bf16) for share in shares),
            pltpu.VMEM((cp, *small.shape), f32),
            *(pltpu.VMEM(share, bf16) for share in shares),
            *sems(hd, cp, cp, cp, cp, cp, hd, hd, hd, hd),
        ],
        6,
    )

    def owned(grad, rows):
        return grad[:, : rows // hd].reshape(rows, width).astype(f32)

    taps_rows = margin + 1

    def columns(grad):
        return jnp.swapaxes(grad, 0, 1).reshape(grad.shape[1], -1).astype(f32)

    gain_sums = jnp.sum(grad_front[:, :, side + 2 : side + 5].astype(f32), 0)
    return (
        block_out,
        grad_in,
        columns(grad_front[:, :, :dk]),
        columns(grad_front[:, :, dk : 2 * dk]),
        columns(grad_front[:, :, 2 * dk : qkv]),
        columns(grad_front[:, :, side : side + 1]),
        columns(grad_front[:, :, side + 1 : side + 2]),
        columns(grad_front[:, :, qkv:side]),
        owned(grad_output, w_output.shape[0]),
        columns(grad_ffn[:, :, :ff]),
        columns(grad_ffn[:, :, ffp : ffp + ff]),
        owned(grad_down, w_ffn_down.shape[0]),
        small[:taps_rows, :dk],
        small[:taps_rows, dk : 2 * dk],
        small[:taps_rows, 2 * dk :],
        small[taps_rows, :1],
        small[taps_rows, 1:2],
        gain_sums[:, 0],
        gain_sums[:, 1],
        gain_sums[:head_share, 2],
    )


def solution(mesh):
    tokens, rows, cols = P(None, ("cp", "hd"), None), P("cp", None), P(None, "hd")
    weights = (rows,) * 10
    return jax.shard_map(
        on_device,
        mesh=mesh,
        in_specs=(tokens, P(), *weights, cols, cols, cols, P("hd"), P("hd"))
        + (P("cp"),) * 3
        + (tokens,),
        out_specs=(tokens, tokens, *weights, cols, cols, cols, P("hd"), P("hd"))
        + (P("cp"),) * 3,
        check_vma=False,
    )
```

```python
import jax
import jax.numpy as jnp
from jax import lax
from jax.experimental import pallas as pl
from jax.experimental.pallas import tpu as pltpu
from jax.sharding import PartitionSpec as P

STRETCH = 64
LANES = 128
CORES = 2
HIGHEST = lax.Precision.HIGHEST
EPSILON = 1e-06
bf16, f32 = jnp.bfloat16, jnp.float32
VMEM_LIMIT = 48 * 1024 * 1024


def mm(a, b, ca=1, cb=0):
    return lax.dot_general(
        a, b, (((ca,), (cb,)), ((), ())), precision=HIGHEST, preferred_element_type=f32
    )


def lower_strict():
    rows = lax.broadcasted_iota(jnp.int32, (STRETCH, STRETCH), 0)
    cols = lax.broadcasted_iota(jnp.int32, (STRETCH, STRETCH), 1)
    return (rows > cols).astype(f32), (rows == cols).astype(f32)


def block_rows(n):
    return pl.ds(pl.multiple_of(n * STRETCH, STRETCH), STRETCH)


def segment_maps(k_ref, v_ref, aux_ref, between_ref, x_ref, end_ref, w_ref, u_ref, inv_ref):
    sequences, length, dk = k_ref.shape
    dv = v_ref.shape[2]
    blocks = length // STRETCH
    strict, unit = lower_strict()

    def prepare_block(pair, carry):
        streams = [(s, 2 * pair + half) for s in range(sequences) for half in range(2)]
        powers, inverses = [], []
        for s, n in streams:
            k = k_ref[s, block_rows(n)]
            beta = aux_ref[s, block_rows(n), 0:1]
            powers.append(-beta * (between_ref[s, n] * strict) * mm(k, k, 1, 1))
            inverses.append(unit + powers[-1])
        for level in range(STRETCH.bit_length() - 2):
            powers = [mm(power, power) for power in powers]
            inverses = [
                inverse + mm(inverse, power) for inverse, power in zip(inverses, powers)
            ]
        for (s, n), inverse in zip(streams, inverses):
            rows = block_rows(n)
            beta = aux_ref[s, rows, 0:1]
            gamma = aux_ref[s, rows, 1:2]
            inv_ref[s, n] = inverse
            w_ref[s, rows] = mm(inverse, beta * gamma * k_ref[s, rows])
            u_ref[s, rows] = mm(inverse, beta * v_ref[s, rows])
        return carry

    lax.fori_loop(0, blocks // 2, prepare_block, 0)

    wide = (dk, dk + dv)
    start = (
        lax.broadcasted_iota(jnp.int32, wide, 0) == lax.broadcasted_iota(jnp.int32, wide, 1)
    ).astype(f32)

    def chain_block(n, states):
        rows = block_rows(n)
        after = []
        for s in range(sequences):
            x = states[s]
            x_ref[s, n] = x
            gone = mm(w_ref[s, rows], x)
            update = jnp.concatenate([-gone[:, :dk], u_ref[s, rows] - gone[:, dk:]], 1)
            rho = aux_ref[s, rows, 2:3]
            last = aux_ref[s, rows, 1:2][STRETCH - 1 :]
            after.append(last * x + mm(k_ref[s, rows], rho * update, 0, 0))
        return tuple(after)

    ends = lax.fori_loop(0, blocks, chain_block, (start,) * sequences)
    for s in range(sequences):
        end_ref[s] = ends[s].astype(end_ref.dtype)


def run_segment(
    entry_ref, x_ref, q_ref, k_ref, aux_ref, between_ref, w_ref, u_ref,
    out_ref, state_ref, update_ref,
):
    sequences, length, dk = k_ref.shape
    blocks = length // STRETCH

    def run_block(n, carry):
        rows = block_rows(n)
        for s in range(sequences):
            q, k = q_ref[s, rows], k_ref[s, rows]
            state = mm(x_ref[s, n, :, :dk], entry_ref[s]) + x_ref[s, n, :, dk:]
            update = u_ref[s, rows] - mm(w_ref[s, rows], state)
            scores = mm(q, k, 1, 1) * between_ref[s, n]
            out = aux_ref[s, rows, 1:2] * mm(q, state) + mm(scores, update)
            state_ref[s, n] = state
            update_ref[s, rows] = update
            out_ref[s, rows] = out.astype(out_ref.dtype)
        return carry

    lax.fori_loop(0, blocks, run_block, 0)


def segment_local(
    q_ref, k_ref, aux_ref, between_ref, w_ref, grad_ref, through_ref, inflow_ref, local_ref
):
    sequences, length, dk = k_ref.shape
    dv = grad_ref.shape[2]
    blocks = length // STRETCH

    def prepare_block(n, carry):
        rows = block_rows(n)
        for s in range(sequences):
            q, k = q_ref[s, rows], k_ref[s, rows]
            grad = grad_ref[s, rows].astype(f32)
            scores = mm(q, k, 1, 1) * between_ref[s, n]
            through_ref[s, rows] = mm(scores, grad, 0, 0)
            inflow_ref[s, n] = mm(q, aux_ref[s, rows, 1:2] * grad, 0, 0)
        return carry

    lax.fori_loop(0, blocks, prepare_block, 0)

    def chain_block(back, states):
        n = blocks - 1 - back
        rows = block_rows(n)
        after = []
        for s in range(sequences):
            rho = aux_ref[s, rows, 2:3]
            last = aux_ref[s, rows, 1:2][STRETCH - 1 :]
            grad_update = through_ref[s, rows] + rho * mm(k_ref[s, rows], states[s])
            after.append(
                last * states[s] + inflow_ref[s, n] - mm(w_ref[s, rows], grad_update, 0, 0)
            )
        return tuple(after)

    ends = lax.fori_loop(0, blocks, chain_block, (jnp.zeros((dk, dv), f32),) * sequences)
    for s in range(sequences):
        local_ref[s] = ends[s].astype(local_ref.dtype)


def back_blocks(
    first, count, exits,
    q_ref, k_ref, v_ref, aux_ref, between_ref, w_ref, inv_ref,
    state_ref, update_ref, grad_ref, through_ref, inflow_ref,
    grad_q_ref, grad_k_ref, grad_v_ref, grad_aux_ref, grad_row_ref,
):
    sequences, length, dk = k_ref.shape
    blocks = length // STRETCH
    strict, _ = lower_strict()
    at_last = lax.broadcasted_iota(jnp.int32, (STRETCH, 1), 0) == STRETCH - 1
    lane = lax.broadcasted_iota(jnp.int32, (STRETCH, grad_aux_ref.shape[2]), 1)

    def row_sum(a):
        return jnp.sum(a, axis=1, keepdims=True)

    def chain_block(back, states):
        n = blocks - 1 - back
        rows = block_rows(n)
        after = []
        for s in range(sequences):
            grad_next = states[s]
            q, k, v = q_ref[s, rows], k_ref[s, rows], v_ref[s, rows]
            beta, gamma, rho = (aux_ref[s, rows, c : c + 1] for c in range(3))
            last = gamma[STRETCH - 1 :]
            between = between_ref[s, n]
            state, update = state_ref[s, n], update_ref[s, rows]
            grad = grad_ref[s, rows].astype(f32)
            key_next = mm(k, grad_next)
            grad_update = through_ref[s, rows] + rho * key_next
            after.append(last * grad_next + inflow_ref[s, n] - mm(w_ref[s, rows], grad_update, 0, 0))
            grad_target = mm(inv_ref[s, n], grad_update, 0, 0)
            key_state, query_state = mm(k, state), mm(q, state)
            key_key, query_key = mm(k, k, 1, 1), mm(q, k, 1, 1)
            grad_query_key = mm(grad, update, 1, 1) * between
            grad_system = -mm(grad_target, update, 1, 1) * strict * between
            grad_key_key = beta * grad_system
            grad_key_state = -(beta * gamma) * grad_target
            grad_q_ref[s, rows] = gamma * mm(grad, state, 1, 1) + mm(grad_query_key, k)
            grad_k_ref[s, rows] = (
                mm(grad_query_key, q, 0, 0)
                + mm(rho * update, grad_next, 1, 1)
                + mm(grad_key_key, k)
                + mm(grad_key_key, k, 0, 0)
                + mm(grad_key_state, state, 1, 1)
            )
            grad_v_ref[s, rows] = beta * grad_target
            grad_beta = row_sum(grad_system * key_key) + row_sum(
                grad_target * (v - gamma * key_state)
            )
            grad_gamma = row_sum(grad * query_state) - beta * row_sum(grad_target * key_state)
            spread = grad_query_key * query_key + grad_key_key * key_key
            grad_rho = row_sum(key_next * update) * rho
            at_end = jnp.sum(grad_rho) + jnp.sum(row_sum(state * grad_next) * last)
            grad_cumulative = (
                row_sum(spread) + grad_gamma * gamma - grad_rho + jnp.where(at_last, at_end, 0.0)
            )
            grad_row_ref[s, pl.ds(n, 1)] = jnp.sum(spread, axis=0, keepdims=True)
            grad_aux_ref[s, rows] = jnp.where(lane == 0, grad_beta, grad_cumulative)
        return tuple(after)

    return lax.fori_loop(first, first + count, chain_block, exits)


def shaped(shape, kind=f32):
    return jax.ShapeDtypeStruct(shape, kind)


def norm_gain(source, gain_vec):
    return source * lax.rsqrt(jnp.mean(source * source, -1, keepdims=True) + EPSILON) * gain_vec


def unit_rows(source):
    return source * lax.rsqrt(jnp.sum(source * source, -1, keepdims=True) + EPSILON)


def gated_norm(mixed_head, gate_pre, gain_vec):
    scale = lax.rsqrt(jnp.mean(mixed_head * mixed_head, -1, keepdims=True) + EPSILON)
    return mixed_head * scale * gain_vec * jax.nn.silu(gate_pre)


def conv_core(padded, weight, doc_pad):
    tap_count = weight.shape[0]
    length = padded.shape[1] - (tap_count - 1)
    current = doc_pad[:, tap_count - 1 :]
    summed = jnp.zeros((padded.shape[0], length, padded.shape[2]), f32)
    for offset in range(tap_count):
        first_row = tap_count - 1 - offset
        window = padded[:, first_row : first_row + length]
        same_doc = (doc_pad[:, first_row : first_row + length] == current).astype(f32)
        summed = summed + weight[offset] * window * same_doc[:, :, None]
    return jax.nn.silu(summed)


def prepare(packed_ext, decay_head, beta_head, taps, decay_log, decay_bias, doc_ext, dk):
    mixed = conv_core(packed_ext, taps, doc_ext)
    queries = unit_rows(mixed[:, :, :dk]) * dk ** (-0.5)
    key_rows = unit_rows(mixed[:, :, dk : 2 * dk])
    values = mixed[:, :, 2 * dk :]
    beta_rows = jax.nn.sigmoid(beta_head)
    decays = -jnp.exp(decay_log) * jax.nn.softplus(decay_head + decay_bias)
    sequences, length = decays.shape
    cumulative = jnp.cumsum(decays.reshape(sequences, length // STRETCH, STRETCH), -1)
    return queries, key_rows, values, beta_rows, cumulative


def block_gates(cumulative, doc_blocks, doc_starts):
    places = jnp.arange(STRETCH)
    linked = (places[:, None] >= places[None, :]) & (
        doc_blocks[..., :, None] == doc_blocks[..., None, :]
    )
    apart = cumulative[..., :, None] - cumulative[..., None, :]
    between = jnp.where(linked, jnp.exp(jnp.where(linked, apart, 0.0)), 0.0)
    survive = jnp.exp(cumulative) * (doc_blocks == doc_starts[..., None]).astype(f32)
    return survive, between, between[..., -1, :]


def each_peer(axis, action):
    count, me = lax.axis_size(axis), lax.axis_index(axis)

    def step(distance, carry):
        action(distance, lax.rem(me + distance, count), lax.rem(me + count - distance, count))
        return carry

    lax.fori_loop(1, count, step, 0)


def chip_devices(action):
    count, me = lax.axis_size("cp") // CORES, lax.axis_index("cp")
    chip, core = me // CORES, lax.rem(me, CORES)

    def step(distance, carry):
        ahead, behind = lax.rem(chip + distance, count), lax.rem(chip + count - distance, count)
        action(distance, ahead * CORES + core, behind * CORES + core)
        return carry

    lax.fori_loop(1, count, step, 0)


def sibling():
    me = lax.axis_index("cp")
    return me + 1 - 2 * lax.rem(me, CORES)


def owner_target(turn):
    hd = lax.axis_size("hd")
    share = lax.axis_size("cp") // hd
    piece = CORES * turn + lax.rem(lax.axis_index("cp"), CORES)
    return share * lax.axis_index("hd") + piece // hd, lax.rem(piece, hd)


def owner_source(chip):
    share = lax.axis_size("cp") // lax.axis_size("hd")
    core = lax.rem(lax.axis_index("hd"), CORES)
    return CORES * chip + core, lax.axis_index("cp") // share


def column_target(turn):
    return CORES * turn + lax.rem(lax.axis_index("cp"), CORES), lax.axis_index("hd")


def row_target(turn):
    share = lax.axis_size("cp") // lax.axis_size("hd")
    return share * lax.axis_index("hd") + turn, lax.axis_index("cp") // share


def is_me(at):
    return (at[0] == lax.axis_index("cp")) & (at[1] == lax.axis_index("hd"))


def each(count, action):
    def step(turn, carry):
        action(turn)
        return carry

    lax.fori_loop(0, count, step, 0)


def signal(target):
    pl.semaphore_signal(
        pltpu.get_barrier_semaphore(), inc=1, device_id=target,
        device_id_type=pl.DeviceIdType.MESH,
    )


def meet(heads=False, chips=False, owners=False, rows=False):
    cp, hd = lax.axis_size("cp"), lax.axis_size("hd")
    total = jnp.int32(0)
    if heads:
        each_peer("hd", lambda _, to, source: signal({"hd": to}))
        total += hd - 1
    if chips:
        chip_devices(lambda _, to, source: signal({"cp": to}))
        signal({"cp": sibling()})
        total += cp // CORES
    for wanted, count, source_of, target_of in (
        (owners, cp // CORES, owner_source, owner_target),
        (rows, cp // hd, row_target, row_target),
    ):
        if wanted:

            def greet(turn, source_of=source_of):
                at = source_of(turn)

                @pl.when(jnp.logical_not(is_me(at)))
                def _():
                    signal(at)

            each(count, greet)
            total += count
            for turn in range(count):
                total -= is_me(target_of(turn)).astype(jnp.int32)
    pl.semaphore_wait(pltpu.get_barrier_semaphore(), total)


def remote(src, dst, send, recv, target):
    return pltpu.make_async_remote_copy(
        src_ref=src,
        dst_ref=dst,
        send_sem=send,
        recv_sem=recv,
        device_id=target,
        device_id_type=pl.DeviceIdType.MESH,
    )


class Exchange:
    def __init__(self, axis, source, landing, send, recv, local):
        self.axis, self.source, self.landing = axis, source, landing
        self.send, self.recv = send, recv
        me = lax.axis_index(axis)
        self.own = pltpu.make_async_copy(source(me), landing(me), local)

    def copy(self, distance, block, place, to):
        return remote(
            block, place, self.send.at[distance], self.recv.at[distance], {self.axis: to}
        )

    def start(self):
        me = lax.axis_index(self.axis)
        each_peer(
            self.axis,
            lambda distance, to, source: self.copy(
                distance, self.source(to), self.landing(me), to
            ).start(),
        )
        self.own.start()

    def arrive(self):
        each_peer(
            self.axis,
            lambda distance, to, source: self.copy(
                distance, self.source(to), self.landing(source), to
            ).wait_recv(),
        )
        self.own.wait()

    def leave(self):
        each_peer(
            self.axis,
            lambda distance, to, source: self.copy(
                distance, self.source(to), self.landing(source), to
            ).wait_send(),
        )


class PairGather:
    def __init__(self, source, landing, send, recv, local):
        self.source, self.landing, self.send, self.recv = source, landing, send, recv
        self.me = lax.axis_index("cp")
        self.count = lax.axis_size("cp") // CORES
        self.own = pltpu.make_async_copy(source, landing(self.me), local)

    def copy(self, block, index, slot, to):
        return remote(
            block, self.landing(index), self.send.at[slot], self.recv.at[index], {"cp": to}
        )

    def start(self):
        chip_devices(lambda d, to, source: self.copy(self.source, self.me, d, to).start())
        self.copy(self.source, self.me, 0, sibling()).start()
        self.own.start()

    def arrive(self):
        def hand_on(d, to, source):
            self.copy(self.source, source, d, to).wait_recv()
            self.copy(self.landing(source), source, self.count + d, sibling()).start()

        chip_devices(hand_on)
        other = sibling()
        self.copy(self.source, other, 0, other).wait_recv()
        shift = other - self.me
        chip_devices(
            lambda d, to, source: self.copy(self.source, source + shift, d, other).wait_recv()
        )
        self.own.wait()

    def leave(self):
        chip_devices(lambda d, to, source: self.copy(self.source, self.me, d, to).wait_send())
        self.copy(self.source, self.me, 0, sibling()).wait_send()
        chip_devices(
            lambda d, to, source: self.copy(
                self.source, source, self.count + d, sibling()
            ).wait_send()
        )


class PairReduce:
    def __init__(self, parts, inbox, sums, landed, swap, send, recv, local, target, source):
        self.parts, self.inbox, self.sums, self.landed = parts, inbox, sums, landed
        self.send, self.recv, self.local = send, recv, local
        self.target, self.source = target, source
        me = lax.axis_index("cp")
        self.chip, self.core = me // CORES, lax.rem(me, CORES)
        self.swap = remote(
            parts.at[:, 1 - self.core], inbox, swap.at[0], swap.at[1], {"cp": sibling()}
        )

    def start(self):
        self.swap.start()

    def move(self, turn, slot, to):
        return remote(
            self.sums.at[turn], self.landed.at[slot], self.send.at[turn], self.recv.at[slot], to
        )

    def add_pairs(self):
        self.swap.wait()

        def go(turn):
            total = self.parts[turn, self.core].astype(f32) + self.inbox[turn].astype(f32)
            self.sums[turn] = total.astype(bf16)
            to = self.target(turn)
            own = is_me(to)

            @pl.when(own)
            def _():
                pltpu.make_async_copy(
                    self.sums.at[turn], self.landed.at[self.chip], self.local
                ).start()

            @pl.when(jnp.logical_not(own))
            def _():
                self.move(turn, self.chip, to).start()

        each(self.sums.shape[0], go)

    def total(self):
        def get(chip):
            at = self.source(chip)
            own = is_me(at)

            @pl.when(own)
            def _():
                pltpu.make_async_copy(
                    self.sums.at[chip], self.landed.at[chip], self.local
                ).wait()

            @pl.when(jnp.logical_not(own))
            def _():
                self.move(chip, chip, at).wait_recv()

        each(self.landed.shape[0], get)
        return added(self.landed).astype(bf16)

    def leave(self):
        def done(turn):
            to = self.target(turn)

            @pl.when(jnp.logical_not(is_me(to)))
            def _():
                self.move(turn, turn, to).wait_send()

        each(self.sums.shape[0], done)


class RowMove:
    def __init__(self, rows, landing, send, recv, local):
        self.rows, self.send, self.recv, self.local = rows, send, recv, local
        self.count = lax.axis_size("cp") // lax.axis_size("hd")
        self.slot = lax.rem(lax.axis_index("cp"), self.count)
        self.landing = lambda slot: lead_rows(landing, slot, rows.shape[0])

    def copy(self, turn, slot, to):
        return remote(self.rows, self.landing(slot), self.send.at[turn], self.recv.at[slot], to)

    def kept(self):
        return pltpu.make_async_copy(self.rows, self.landing(self.slot), self.local)

    def start(self):
        def go(turn):
            to = row_target(turn)

            @pl.when(is_me(to))
            def _():
                self.kept().start()

            @pl.when(jnp.logical_not(is_me(to)))
            def _():
                self.copy(turn, self.slot, to).start()

        each(self.count, go)

    def arrive(self):
        def get(turn):
            at = row_target(turn)

            @pl.when(is_me(at))
            def _():
                self.kept().wait()

            @pl.when(jnp.logical_not(is_me(at)))
            def _():
                self.copy(turn, turn, at).wait_recv()
                self.copy(turn, turn, at).wait_send()

        each(self.count, get)

    def leave(self):
        pass


def sems(*counts):
    found = []
    for count in counts:
        found += [pltpu.SemaphoreType.DMA((count,))] * 2 + [pltpu.SemaphoreType.DMA]
    return found


def reduce_scratch(parts):
    half = (parts.shape[0], *parts.shape[2:])
    return [pltpu.VMEM(half, bf16)] * 3 + [
        pltpu.SemaphoreType.DMA((2,)), *sems(parts.shape[0])
    ]


def token_rows(ref, index, tokens):
    return ref.at[:, pl.ds(pl.multiple_of(index * tokens, tokens), tokens)]


def lead_rows(ref, index, rows):
    return ref.at[pl.ds(pl.multiple_of(index * rows, rows), rows)]


def comm_call(body, out_shape, places, operands, spots, scratch, number):
    kinds = {"any": pl.ANY, "vmem": pltpu.VMEM}
    return pl.pallas_call(
        body,
        out_shape=out_shape,
        in_specs=[pl.BlockSpec(memory_space=kinds[k]) for k in places],
        out_specs=tuple(pl.BlockSpec(memory_space=kinds[k]) for k in spots),
        scratch_shapes=scratch,
        compiler_params=pltpu.CompilerParams(
            collective_id=number, has_side_effects=True, vmem_limit_bytes=VMEM_LIMIT
        ),
    )(*operands)


def open_kernel(hidden_ref, front_ref, hidden_all_ref, front_all_ref, *flags):
    tokens, shard = hidden_ref.shape[1], front_ref.shape[0]
    meet(heads=True, chips=True)
    moves = (
        Exchange(
            "hd", lambda to: hidden_ref, lambda at: token_rows(hidden_all_ref, at, tokens), *flags[:3]
        ),
        PairGather(front_ref, lambda at: lead_rows(front_all_ref, at, shard), *flags[3:6]),
    )
    for move in moves:
        move.start()
    for move in reversed(moves):
        move.arrive()
        move.leave()


def place_of():
    me = lax.axis_index("cp")
    return me // CORES, lax.rem(me, CORES)


def forward_kernel(
    q_ref, k_ref, v_ref, aux_ref, between_ref, cot_ref, ffn_ref, output_ref, down_ref,
    mixed_ref, state_ref, update_ref, w_ref, inv_ref, maps_ref, both_ref,
    cot_all_ref, ffn_all_ref, output_part_ref, down_part_ref,
    x_ref, u_ref, own_ref, other_ref, entry_ref, give_ref, pair_sems, *flags
):
    sequences, _, dk = k_ref.shape
    dv = v_ref.shape[2]
    tokens, shard = cot_ref.shape[1], ffn_ref.shape[0]
    chip, core = place_of()
    early = core == 0
    meet(heads=True, chips=True, rows=True)
    carried = (
        PairGather(ffn_ref, lambda at: lead_rows(ffn_all_ref, at, shard), *flags[:3]),
        RowMove(output_ref, output_part_ref, *flags[3:6]),
        RowMove(down_ref, down_part_ref, *flags[6:9]),
        Exchange(
            "hd", lambda to: cot_ref, lambda at: token_rows(cot_all_ref, at, tokens), *flags[9:12]
        ),
    )
    for move in carried:
        move.start()
    segment_maps(k_ref, v_ref, aux_ref, between_ref, x_ref, own_ref, w_ref, u_ref, inv_ref)
    swap = remote(
        own_ref.at[1 - core], other_ref, pair_sems.at[0], pair_sems.at[1], {"cp": sibling()}
    )
    swap.start()
    swap.wait()
    mine, theirs = own_ref[core], other_ref[...]
    both_ref[0] = jnp.where(early, mine, theirs)
    both_ref[1] = jnp.where(early, theirs, mine)
    first, second = both_ref[0].astype(f32), both_ref[1].astype(f32)
    pair = mm(second[:, :dk], first)
    pair = jnp.concatenate([pair[:, :dk], pair[:, dk:] + second[:, dk:]], 1)
    maps_ref[chip] = pair.astype(bf16)
    spread_chips(maps_ref, flags[12], flags[13])

    def enter(hop, state):
        return mm(maps_ref[hop, :, :dk].astype(f32), state) + maps_ref[hop, :, dk:].astype(f32)

    entered = lax.fori_loop(0, chip, enter, jnp.zeros((dk, dv), f32))
    halfway = mm(first[:, :dk], entered) + first[:, dk:]
    entry_ref[core] = jnp.where(early, entered, halfway)
    give_ref[...] = jnp.where(early, halfway, entered)
    give = remote(
        give_ref, entry_ref.at[core], pair_sems.at[2], pair_sems.at[3], {"cp": sibling()}
    )
    give.start()
    remote(
        give_ref, entry_ref.at[1 - core], pair_sems.at[2], pair_sems.at[3], {"cp": sibling()}
    ).wait()
    run_segment(
        entry_ref, x_ref, q_ref, k_ref, aux_ref, between_ref, w_ref, u_ref,
        mixed_ref, state_ref, update_ref,
    )
    for move in carried:
        move.arrive()
    for move in carried:
        move.leave()


def spread_chips(ref, send, recv):
    chip, _ = place_of()

    def copy(distance, index, to):
        return remote(ref.at[index], ref.at[index], send.at[distance], recv.at[distance], {"cp": to})

    chip_devices(lambda d, to, source: copy(d, chip, to).start())
    chip_devices(lambda d, to, source: copy(d, source // CORES, to).wait_recv())
    chip_devices(lambda d, to, source: copy(d, chip, to).wait_send())


def backward_kernel(
    q_ref, k_ref, v_ref, aux_ref, between_ref, w_ref, inv_ref, state_ref, update_ref, grad_ref,
    maps_ref, both_ref, ffn_ref, down_ref,
    grad_q_ref, grad_k_ref, grad_v_ref, grad_aux_ref, grad_row_ref, ffn_all_ref, down_all_ref,
    through_ref, inflow_ref, own_ref, other_ref, locals_ref, exit_ref, give_ref,
    ffn_own_ref, down_own_ref, pair_sems, chip_send, chip_recv, *flags
):
    sequences, length, dk = k_ref.shape
    dv = v_ref.shape[2]
    blocks = length // STRETCH
    chip, core = place_of()
    chips = locals_ref.shape[0]
    late = core == CORES - 1
    meet(heads=True, chips=True, owners=True)
    reduces = (
        PairReduce(ffn_ref, *flags[:7], column_target, column_source),
        PairReduce(down_ref, *flags[7:14], owner_target, owner_source),
    )
    for move in reduces:
        move.start()
    segment_local(
        q_ref, k_ref, aux_ref, between_ref, w_ref, grad_ref, through_ref, inflow_ref, own_ref
    )
    swap = remote(
        own_ref.at[1 - core], other_ref, pair_sems.at[0], pair_sems.at[1], {"cp": sibling()}
    )
    swap.start()
    swap.wait()
    mine, theirs = own_ref[core].astype(f32), other_ref[...].astype(f32)
    first, second = jnp.where(late, theirs, mine), jnp.where(late, mine, theirs)
    locals_ref[chip] = (mm(both_ref[0, :, :dk].astype(f32), second, 0, 0) + first).astype(bf16)
    spread_chips(locals_ref, chip_send, chip_recv)
    for move in reduces:
        move.add_pairs()

    def leave(hop, state):
        source = chips - 1 - hop
        return mm(maps_ref[source, :, :dk].astype(f32), state, 0, 0) + locals_ref[
            source
        ].astype(f32)

    left = lax.fori_loop(0, chips - 1 - chip, leave, jnp.zeros((dk, dv), f32))
    halfway = mm(both_ref[1, :, :dk].astype(f32), left, 0, 0) + second
    exit_ref[core] = jnp.where(late, left, halfway)
    give_ref[...] = jnp.where(late, halfway, left)
    remote(
        give_ref, exit_ref.at[core], pair_sems.at[2], pair_sems.at[3], {"cp": sibling()}
    ).start()
    remote(
        give_ref, exit_ref.at[1 - core], pair_sems.at[2], pair_sems.at[3], {"cp": sibling()}
    ).wait()
    refs = (
        q_ref, k_ref, v_ref, aux_ref, between_ref, w_ref, inv_ref, state_ref, update_ref,
        grad_ref, through_ref, inflow_ref,
        grad_q_ref, grad_k_ref, grad_v_ref, grad_aux_ref, grad_row_ref,
    )
    exits = tuple(exit_ref[s] for s in range(sequences))
    exits = back_blocks(0, blocks // 2, exits, *refs)
    spreads = []
    for n, (move, own, everywhere) in enumerate(
        zip(reduces, (ffn_own_ref, down_own_ref), (ffn_all_ref, down_all_ref))
    ):
        own[...] = move.total()
        spreads.append(spread_piece(own, everywhere, flags[14 + 3 * n : 17 + 3 * n]))
    back_blocks(blocks // 2, blocks - blocks // 2, exits, *refs)
    for move in reduces:
        move.leave()
    for spread in spreads:
        spread.arrive()
        spread.leave()


def column_source(chip):
    return column_target(chip)


def spread_piece(own, everywhere, flags):
    spread = Exchange("hd", lambda to: own, lambda at: everywhere.at[at], *flags)
    spread.start()
    return spread


def added(landed_ref):
    total = landed_ref[0].astype(f32)
    for index in range(1, landed_ref.shape[0]):
        total += landed_ref[index].astype(f32)
    return total


def spread_own(own_ref, all_ref, tokens, flags):
    move = Exchange("hd", lambda to: own_ref, lambda at: token_rows(all_ref, at, tokens), *flags)
    move.start()
    return move


def middle_kernel(
    partial_ref, hidden_ref, gain_ref, middle_ref, ffn_all_ref, landed_ref, own_ref, *flags
):
    tokens = hidden_ref.shape[1]
    meet(heads=True)
    move = Exchange(
        "hd", lambda to: token_rows(partial_ref, to, tokens), lambda at: landed_ref.at[at], *flags[:3]
    )
    move.start()
    move.arrive()
    middle = hidden_ref[...].astype(f32) + added(landed_ref)
    middle_ref[...] = middle
    own_ref[...] = norm_gain(middle, gain_ref[...]).astype(bf16)
    after = spread_own(own_ref, ffn_all_ref, tokens, flags[3:6])
    move.leave()
    after.arrive()
    after.leave()


def norm_back(source, gain_vec, grad):
    scale = lax.rsqrt(jnp.mean(source * source, -1, keepdims=True) + EPSILON)
    lifted = grad * gain_vec
    mixed = jnp.mean(source * lifted, -1, keepdims=True)
    return scale * lifted - source * (scale * scale * scale) * mixed, source * scale * grad


def ffn_back_kernel(
    out_part_ref, grad_part_ref, middle_ref, cot_ref, gain_ref,
    block_ref, grad_middle_ref, grad_gain_ref, grad_all_ref,
    out_landed_ref, grad_landed_ref, own_ref, *flags
):
    tokens = middle_ref.shape[1]
    meet(heads=True)
    moves = [
        Exchange(
            "hd",
            lambda to, ref=ref: token_rows(ref, to, tokens),
            lambda at, landed=landed: landed.at[at],
            *flags[3 * n : 3 * n + 3],
        )
        for n, (ref, landed) in enumerate(
            ((grad_part_ref, grad_landed_ref), (out_part_ref, out_landed_ref))
        )
    ]
    for move in moves:
        move.start()
    moves[0].arrive()
    middle = middle_ref[...]
    back, gain_terms = norm_back(middle, gain_ref[...], added(grad_landed_ref))
    grad_middle = cot_ref[...].astype(f32) + back
    grad_middle_ref[...] = grad_middle
    own_ref[...] = grad_middle.astype(bf16)
    after = spread_own(own_ref, grad_all_ref, tokens, flags[6:9])
    grad_gain_ref[...] = jnp.sum(jnp.sum(gain_terms, axis=0), axis=0, keepdims=True)
    moves[1].arrive()
    block_ref[...] = (middle + added(out_landed_ref)).astype(bf16)
    for move in moves:
        move.leave()
    after.arrive()
    after.leave()


def close_kernel(
    normed_part_ref, front_ref, output_ref, small_ref, hidden_ref, grad_middle_ref, gain_ref,
    grad_in_ref, front_all_ref, output_all_ref, small_sum_ref,
    normed_landed, small_landed, front_own, output_own, *flags
):
    tokens = hidden_ref.shape[1]
    meet(heads=True, chips=True, owners=True)
    reduces = (
        PairReduce(front_ref, *flags[:7], column_target, column_source),
        PairReduce(output_ref, *flags[7:14], owner_target, owner_source),
    )
    normed_move = Exchange(
        "hd",
        lambda to: token_rows(normed_part_ref, to, tokens),
        lambda at: normed_landed.at[at],
        *flags[14:17],
    )
    small_move = PairGather(small_ref, lambda at: small_landed.at[at], *flags[17:20])
    for move in reduces:
        move.start()
    normed_move.start()
    for move in reduces:
        move.add_pairs()
    small_move.start()
    spreads = []
    for n, (move, own, everywhere) in enumerate(
        zip(reduces, (front_own, output_own), (front_all_ref, output_all_ref))
    ):
        own[...] = move.total()
        spreads.append(spread_piece(own, everywhere, flags[20 + 3 * n : 23 + 3 * n]))
    normed_move.arrive()
    back, _ = norm_back(hidden_ref[...].astype(f32), gain_ref[...], added(normed_landed))
    grad_in_ref[...] = (grad_middle_ref[...] + back).astype(bf16)
    small_move.arrive()
    small_sum_ref[...] = added(small_landed)
    for move in (normed_move, small_move, *reduces):
        move.leave()
    for spread in spreads:
        spread.arrive()
        spread.leave()


def passed_along(block, axis, distance):
    devices = range(lax.axis_size(axis))
    route = [(i - distance, i) for i in devices if i - distance in devices]
    return lax.ppermute(block, axis, route)


def on_device(
    hidden_in, doc_ids, w_query, w_key, w_value, w_decay, w_beta, w_gate_out, w_output,
    w_ffn_gate, w_ffn_up, w_ffn_down, conv_query, conv_key, conv_value, decay_log, decay_bias,
    gain_attn, gain_ffn, gain_head, cotangent,
):
    place, head = lax.axis_index("cp"), lax.axis_index("hd")
    cp, hd = lax.axis_size("cp"), lax.axis_size("hd")
    sequences, tokens, width = hidden_in.shape
    shard = w_query.shape[0]
    dk, dv = w_query.shape[1] // hd, w_value.shape[1] // hd
    ff = w_ffn_gate.shape[1] // hd
    ffp = -(-ff // LANES) * LANES
    qkv = 2 * dk + dv
    side = qkv + dv
    span = tokens * hd
    blocks = span // STRETCH

    def part(weight):
        cols = weight.shape[1] // hd
        return lax.dynamic_slice_in_dim(weight, head * cols, cols, 1)

    def ff_pad(weight):
        return jnp.pad(part(weight), ((0, 0), (0, ffp - ff)))

    head_share = gain_head.shape[0]
    side_cols = jnp.stack(
        [
            part(w_decay)[:, 0],
            part(w_beta)[:, 0],
            gain_attn,
            gain_ffn,
            jnp.pad(gain_head, (0, shard - head_share)),
        ],
        1,
    )
    front = jnp.concatenate(
        [
            part(w_query),
            part(w_key),
            part(w_value),
            part(w_gate_out),
            jnp.pad(side_cols, ((0, 0), (0, LANES - side_cols.shape[1]))),
        ],
        1,
    )
    hidden_all, front_full = comm_call(
        open_kernel,
        (shaped((sequences, span, width), bf16), shaped((width, front.shape[1]), bf16)),
        ("any", "any"),
        (hidden_in, front),
        ("any", "any"),
        sems(hd, cp),
        1,
    )
    ffn_front = jnp.concatenate([ff_pad(w_ffn_gate), ff_pad(w_ffn_up)], 1)

    attn_gain = front_full[:, side + 2].astype(f32)
    ffn_gain = front_full[:, side + 3].astype(f32)
    head_gain = front_full[:, side + 4].reshape(cp, shard)[:, :head_share].reshape(-1).astype(f32)

    def dot(a, b, spec):
        return jnp.einsum(spec, a, b, preferred_element_type=f32)

    inputs_all = hidden_all.astype(f32)
    scale_all = lax.rsqrt(jnp.mean(inputs_all * inputs_all, -1, keepdims=True) + EPSILON)
    normed = (inputs_all * scale_all * attn_gain).astype(bf16)
    projected = dot(normed, front_full, "std,de->ste")
    packed = projected[:, :, :qkv].astype(bf16)
    gate_pre = projected[:, :, qkv:side]
    decay_head = projected[:, :, side].astype(bf16).astype(f32)
    beta_head = projected[:, :, side + 1].astype(bf16).astype(f32)

    margin = conv_query.shape[0] - 1
    rim = passed_along(packed[:, -margin:], "cp", 1)
    doc_pad = jnp.concatenate([jnp.full((sequences, margin), -1, jnp.int32), doc_ids], 1)
    doc_ext = lax.dynamic_slice_in_dim(doc_pad, place * span, span + margin, 1)
    doc_blocks = doc_ext[:, margin:].reshape(sequences, blocks, STRETCH)
    doc_starts = doc_ext[:, margin - 1 : -1].reshape(sequences, blocks, STRETCH)[:, :, 0]
    taps = jnp.concatenate([conv_query, conv_key, conv_value], 1).astype(f32)
    prepared, prepare_pull = jax.vjp(
        lambda *entries: prepare(*entries, doc_ext, dk),
        jnp.concatenate([rim, packed], 1).astype(f32),
        decay_head,
        beta_head,
        taps,
        decay_log.astype(f32),
        decay_bias.astype(f32),
    )
    queries, key_rows, values, beta_rows, cumulative = prepared
    survive, between, rho = block_gates(cumulative, doc_blocks, doc_starts)
    flat = (sequences, span)
    aux = jnp.stack([beta_rows, survive.reshape(flat), rho.reshape(flat)], -1)
    aux = jnp.pad(aux, ((0, 0), (0, 0), (0, 5)))
    chips = cp // CORES
    share = cp // hd
    (
        mixed, states, updates, weighted, inverse, maps, both,
        cot_all, ffn_full, output_part, down_part,
    ) = comm_call(
        forward_kernel,
        (
            shaped((sequences, span, dv), bf16),
            shaped((sequences, blocks, dk, dv)),
            shaped((sequences, span, dv)),
            shaped((sequences, span, dk)),
            shaped((sequences, blocks, STRETCH, STRETCH)),
            shaped((chips, dk, dk + dv), bf16),
            shaped((CORES, dk, dk + dv), bf16),
            shaped((sequences, span, width), bf16),
            shaped((width, 2 * ffp), bf16),
            shaped((share * w_output.shape[0], width), bf16),
            shaped((share * w_ffn_down.shape[0], width), bf16),
        ),
        ("vmem",) * 5 + ("any",) * 4,
        (
            queries, key_rows, values, aux, between, cotangent, ffn_front, w_output, w_ffn_down,
        ),
        ("vmem",) * 7 + ("any",) * 4,
        [
            pltpu.VMEM((sequences, blocks, dk, dk + dv), f32),
            pltpu.VMEM((sequences, span, dv), f32),
            pltpu.VMEM((sequences, dk, dk + dv), bf16),
            pltpu.VMEM((dk, dk + dv), bf16),
            pltpu.VMEM((sequences, dk, dv), f32),
            pltpu.VMEM((dk, dv), f32),
            pltpu.SemaphoreType.DMA((4,)),
            *sems(cp, share, share, hd),
            pltpu.SemaphoreType.DMA((chips,)),
            pltpu.SemaphoreType.DMA((chips,)),
        ],
        2,
    )
    down_part = jnp.pad(down_part, ((0, ffp - ff), (0, 0)))
    mixed_float = mixed.astype(f32)
    normed_head, gated_pull = jax.vjp(gated_norm, mixed_float, gate_pre, head_gain)
    normed_head = normed_head.astype(bf16)
    landing = pltpu.VMEM((hd, sequences, tokens, width), bf16)
    own_tokens = pltpu.VMEM((sequences, tokens, width), bf16)
    ffn_gain = ffn_gain[None]
    middle, ffn_all = comm_call(
        middle_kernel,
        (shaped(hidden_in.shape), shaped((sequences, span, width), bf16)),
        ("any", "vmem", "vmem"),
        (dot(normed_head, output_part, "ste,ed->std").astype(bf16), hidden_in, ffn_gain),
        ("vmem", "any"),
        [landing, own_tokens, *sems(hd, hd)],
        4,
    )
    gate_up = dot(ffn_all, ffn_full, "std,df->stf")
    inner, swiglu_pull = jax.vjp(
        lambda both: jax.nn.silu(both[..., :ffp]) * both[..., ffp:], gate_up
    )
    inner = inner.astype(bf16)
    grad_inner = dot(cot_all, down_part, "std,fd->stf")
    grad_gate_up = swiglu_pull(grad_inner)[0].astype(bf16)
    block_out, grad_middle, grad_ffn_gain, grad_attention = comm_call(
        ffn_back_kernel,
        (
            shaped(hidden_in.shape, bf16),
            shaped(hidden_in.shape),
            shaped((1, width)),
            shaped((sequences, span, width), bf16),
        ),
        ("any", "any", "vmem", "vmem", "vmem"),
        (
            dot(inner, down_part, "stf,fd->std").astype(bf16),
            dot(grad_gate_up, ffn_full, "stf,df->std").astype(bf16),
            middle, cotangent, ffn_gain,
        ),
        ("vmem", "vmem", "vmem", "any"),
        [landing, landing, own_tokens, *sems(hd, hd, hd)],
        5,
    )

    def weight_grad(left_side, right_side):
        return dot(left_side, right_side, "std,ste->de")

    def pieces(grad):
        rows = grad.shape[0] // cp
        split = grad.reshape(chips, CORES, rows, width)
        return jnp.pad(split, ((0, 0), (0, 0), (0, -rows % 16), (0, 0))).astype(bf16)

    def by_owner(grad):
        return grad.reshape(chips, CORES, shard, grad.shape[1]).astype(bf16)

    grad_ffn = by_owner(weight_grad(ffn_all, grad_gate_up))
    grad_down = pieces(weight_grad(inner, cot_all)[:ff])

    grad_normed_head = dot(grad_attention, output_part, "std,ed->ste")
    grad_output = pieces(weight_grad(normed_head, grad_attention))
    grad_mixed, grad_gate_pre, grad_head_gain = gated_pull(grad_normed_head)
    grad_mixed = grad_mixed.astype(bf16)
    ffn_share, down_share = (entry.shape[2:] for entry in (grad_ffn, grad_down))
    grad_q, grad_k, grad_v, grad_aux, grad_row, grad_ffn, grad_down = comm_call(
        backward_kernel,
        (
            shaped((sequences, span, dk)),
            shaped((sequences, span, dk)),
            shaped((sequences, span, dv)),
            shaped((sequences, span, 8)),
            shaped((sequences, blocks, STRETCH)),
            shaped((hd, *ffn_share), bf16),
            shaped((hd, *down_share), bf16),
        ),
        ("vmem",) * 14,
        (
            queries, key_rows, values, aux, between, weighted, inverse, states, updates,
            grad_mixed, maps, both, grad_ffn, grad_down,
        ),
        ("vmem",) * 5 + ("any",) * 2,
        [
            pltpu.VMEM((sequences, span, dv), f32),
            pltpu.VMEM((sequences, blocks, dk, dv), f32),
            pltpu.VMEM((sequences, dk, dv), bf16),
            pltpu.VMEM((dk, dv), bf16),
            pltpu.VMEM((chips, dk, dv), bf16),
            pltpu.VMEM((sequences, dk, dv), f32),
            pltpu.VMEM((dk, dv), f32),
            pltpu.VMEM(ffn_share, bf16),
            pltpu.VMEM(down_share, bf16),
            pltpu.SemaphoreType.DMA((4,)),
            pltpu.SemaphoreType.DMA((chips,)),
            pltpu.SemaphoreType.DMA((chips,)),
            *reduce_scratch(grad_ffn),
            *reduce_scratch(grad_down),
            *sems(hd, hd),
        ],
        3,
    )
    grad_cumulative = grad_aux[:, :, 1].reshape(sequences, blocks, STRETCH) - grad_row
    grad_ext, grad_decay, grad_beta, grad_taps, grad_log, grad_bias = prepare_pull(
        (grad_q, grad_k, grad_v, grad_aux[:, :, 0], grad_cumulative)
    )
    back = passed_along(grad_ext[:, :margin], "cp", -1)
    grad_packed = grad_ext[:, margin:].at[:, -margin:].add(back).astype(bf16)
    grad_projected = jnp.concatenate(
        [
            grad_packed,
            grad_gate_pre.astype(bf16),
            jnp.pad(
                jnp.stack([grad_decay, grad_beta], -1).astype(bf16),
                ((0, 0), (0, 0), (0, LANES - 2)),
            ),
        ],
        -1,
    )
    partial_normed = dot(grad_projected, front_full, "ste,de->std")
    grad_attn_gain = jnp.sum(inputs_all * scale_all * partial_normed, (0, 1))
    grad_front = weight_grad(normed, grad_projected)
    spread_gain = jnp.pad(
        grad_head_gain.reshape(cp, head_share), ((0, 0), (0, shard - head_share))
    ).reshape(-1)
    gains = jnp.stack([grad_attn_gain, grad_ffn_gain[0], spread_gain], 1)
    grad_front = jnp.concatenate(
        [grad_front[:, : side + 2], gains, grad_front[:, side + 5 :]], 1
    )
    small = jnp.concatenate(
        [
            grad_taps,
            jnp.pad(jnp.stack([grad_log, grad_bias], 1), ((0, 0), (0, qkv - 2))),
        ],
        0,
    )
    small = jnp.pad(small, ((0, -small.shape[0] % 8), (0, 0)))
    grad_front = by_owner(grad_front)
    front_share, output_share = (entry.shape[2:] for entry in (grad_front, grad_output))
    grad_in, grad_front, grad_output, small = comm_call(
        close_kernel,
        (
            shaped(hidden_in.shape, bf16),
            shaped((hd, *front_share), bf16),
            shaped((hd, *output_share), bf16),
            shaped(small.shape),
        ),
        ("any", "vmem", "vmem", "any") + ("vmem",) * 3,
        (
            partial_normed.astype(bf16), grad_front, grad_output, small, hidden_in, grad_middle,
            attn_gain[None],
        ),
        ("vmem", "any", "any", "vmem"),
        [
            landing,
            pltpu.VMEM((cp, *small.shape), f32),
            pltpu.VMEM(front_share, bf16),
            pltpu.VMEM(output_share, bf16),
            *reduce_scratch(grad_front),
            *reduce_scratch(grad_output),
            *sems(hd, cp, hd, hd),
        ],
        6,
    )

    def owned(grad, rows):
        return grad[:, : rows // hd].reshape(rows, width).astype(f32)

    taps_rows = margin + 1

    def columns(grad):
        return jnp.swapaxes(grad, 0, 1).reshape(grad.shape[1], -1).astype(f32)

    gain_sums = jnp.sum(grad_front[:, :, side + 2 : side + 5].astype(f32), 0)
    return (
        block_out,
        grad_in,
        columns(grad_front[:, :, :dk]),
        columns(grad_front[:, :, dk : 2 * dk]),
        columns(grad_front[:, :, 2 * dk : qkv]),
        columns(grad_front[:, :, side : side + 1]),
        columns(grad_front[:, :, side + 1 : side + 2]),
        columns(grad_front[:, :, qkv:side]),
        owned(grad_output, w_output.shape[0]),
        columns(grad_ffn[:, :, :ff]),
        columns(grad_ffn[:, :, ffp : ffp + ff]),
        owned(grad_down, w_ffn_down.shape[0]),
        small[:taps_rows, :dk],
        small[:taps_rows, dk : 2 * dk],
        small[:taps_rows, 2 * dk :],
        small[taps_rows, :1],
        small[taps_rows, 1:2],
        gain_sums[:, 0],
        gain_sums[:, 1],
        gain_sums[:head_share, 2],
    )


def solution(mesh):
    tokens, rows, cols = P(None, ("cp", "hd"), None), P("cp", None), P(None, "hd")
    weights = (rows,) * 10
    return jax.shard_map(
        on_device,
        mesh=mesh,
        in_specs=(tokens, P(), *weights, cols, cols, cols, P("hd"), P("hd"))
        + (P("cp"),) * 3
        + (tokens,),
        out_specs=(tokens, tokens, *weights, cols, cols, cols, P("hd"), P("hd"))
        + (P("cp"),) * 3,
        check_vma=False,
    )
```

```python
import jax
import jax.numpy as jnp
from jax import lax
from jax.experimental import pallas as pl
from jax.experimental.pallas import tpu as pltpu
from jax.sharding import PartitionSpec as P

STRETCH = 64
LANES = 128
CORES = 2
HIGHEST = lax.Precision.HIGHEST
EPSILON = 1e-06
bf16, f32 = jnp.bfloat16, jnp.float32
VMEM_LIMIT = 48 * 1024 * 1024


def mm(a, b, ca=1, cb=0):
    return lax.dot_general(
        a, b, (((ca,), (cb,)), ((), ())), precision=HIGHEST, preferred_element_type=f32
    )


def lower_strict():
    rows = lax.broadcasted_iota(jnp.int32, (STRETCH, STRETCH), 0)
    cols = lax.broadcasted_iota(jnp.int32, (STRETCH, STRETCH), 1)
    return (rows > cols).astype(f32), (rows == cols).astype(f32)


def block_rows(n):
    return pl.ds(pl.multiple_of(n * STRETCH, STRETCH), STRETCH)


def segment_maps(
    k_ref, v_ref, aux_ref, between_ref, x_ref, end_ref, w_ref, u_ref, inv_ref, halfway
):
    sequences, length, dk = k_ref.shape
    dv = v_ref.shape[2]
    blocks = length // STRETCH
    strict, unit = lower_strict()

    def prepare_block(pair, carry):
        streams = [(s, 2 * pair + half) for s in range(sequences) for half in range(2)]
        powers, inverses = [], []
        for s, n in streams:
            k = k_ref[s, block_rows(n)]
            beta = aux_ref[s, block_rows(n), 0:1]
            powers.append(-beta * (between_ref[s, n] * strict) * mm(k, k, 1, 1))
            inverses.append(unit + powers[-1])
        for level in range(STRETCH.bit_length() - 2):
            powers = [mm(power, power) for power in powers]
            inverses = [
                inverse + mm(inverse, power) for inverse, power in zip(inverses, powers)
            ]
        for (s, n), inverse in zip(streams, inverses):
            rows = block_rows(n)
            beta = aux_ref[s, rows, 0:1]
            gamma = aux_ref[s, rows, 1:2]
            inv_ref[s, n] = inverse
            w_ref[s, rows] = mm(inverse, beta * gamma * k_ref[s, rows])
            u_ref[s, rows] = mm(inverse, beta * v_ref[s, rows])
        return carry

    lax.fori_loop(0, blocks // 4, prepare_block, 0)
    halfway()
    lax.fori_loop(blocks // 4, blocks // 2, prepare_block, 0)

    wide = (dk, dk + dv)
    start = (
        lax.broadcasted_iota(jnp.int32, wide, 0) == lax.broadcasted_iota(jnp.int32, wide, 1)
    ).astype(f32)

    def chain_block(n, states):
        rows = block_rows(n)
        after = []
        for s in range(sequences):
            x = states[s]
            x_ref[s, n] = x
            gone = mm(w_ref[s, rows], x)
            update = jnp.concatenate([-gone[:, :dk], u_ref[s, rows] - gone[:, dk:]], 1)
            rho = aux_ref[s, rows, 2:3]
            last = aux_ref[s, rows, 1:2][STRETCH - 1 :]
            after.append(last * x + mm(k_ref[s, rows], rho * update, 0, 0))
        return tuple(after)

    ends = lax.fori_loop(0, blocks, chain_block, (start,) * sequences)
    for s in range(sequences):
        end_ref[s] = ends[s].astype(end_ref.dtype)


def run_segment(
    entry_ref, x_ref, q_ref, k_ref, aux_ref, between_ref, w_ref, u_ref,
    out_ref, state_ref, update_ref,
):
    sequences, length, dk = k_ref.shape
    blocks = length // STRETCH

    def run_block(n, carry):
        rows = block_rows(n)
        for s in range(sequences):
            q, k = q_ref[s, rows], k_ref[s, rows]
            state = mm(x_ref[s, n, :, :dk], entry_ref[s]) + x_ref[s, n, :, dk:]
            update = u_ref[s, rows] - mm(w_ref[s, rows], state)
            scores = mm(q, k, 1, 1) * between_ref[s, n]
            out = aux_ref[s, rows, 1:2] * mm(q, state) + mm(scores, update)
            state_ref[s, n] = state
            update_ref[s, rows] = update
            out_ref[s, rows] = out.astype(out_ref.dtype)
        return carry

    lax.fori_loop(0, blocks, run_block, 0)


def segment_local(
    q_ref, k_ref, aux_ref, between_ref, w_ref, grad_ref, through_ref, inflow_ref, local_ref
):
    sequences, length, dk = k_ref.shape
    dv = grad_ref.shape[2]
    blocks = length // STRETCH

    def prepare_block(n, carry):
        rows = block_rows(n)
        for s in range(sequences):
            q, k = q_ref[s, rows], k_ref[s, rows]
            grad = grad_ref[s, rows].astype(f32)
            scores = mm(q, k, 1, 1) * between_ref[s, n]
            through_ref[s, rows] = mm(scores, grad, 0, 0)
            inflow_ref[s, n] = mm(q, aux_ref[s, rows, 1:2] * grad, 0, 0)
        return carry

    lax.fori_loop(0, blocks, prepare_block, 0)

    def chain_block(back, states):
        n = blocks - 1 - back
        rows = block_rows(n)
        after = []
        for s in range(sequences):
            rho = aux_ref[s, rows, 2:3]
            last = aux_ref[s, rows, 1:2][STRETCH - 1 :]
            grad_update = through_ref[s, rows] + rho * mm(k_ref[s, rows], states[s])
            after.append(
                last * states[s] + inflow_ref[s, n] - mm(w_ref[s, rows], grad_update, 0, 0)
            )
        return tuple(after)

    ends = lax.fori_loop(0, blocks, chain_block, (jnp.zeros((dk, dv), f32),) * sequences)
    for s in range(sequences):
        local_ref[s] = ends[s].astype(local_ref.dtype)


def back_blocks(
    first, count, exits,
    q_ref, k_ref, v_ref, aux_ref, between_ref, w_ref, inv_ref,
    state_ref, update_ref, grad_ref, through_ref, inflow_ref,
    grad_q_ref, grad_k_ref, grad_v_ref, grad_aux_ref, grad_row_ref,
):
    sequences, length, dk = k_ref.shape
    blocks = length // STRETCH
    strict, _ = lower_strict()
    at_last = lax.broadcasted_iota(jnp.int32, (STRETCH, 1), 0) == STRETCH - 1
    lane = lax.broadcasted_iota(jnp.int32, (STRETCH, grad_aux_ref.shape[2]), 1)

    def row_sum(a):
        return jnp.sum(a, axis=1, keepdims=True)

    def chain_block(back, states):
        n = blocks - 1 - back
        rows = block_rows(n)
        after = []
        for s in range(sequences):
            grad_next = states[s]
            q, k, v = q_ref[s, rows], k_ref[s, rows], v_ref[s, rows]
            beta, gamma, rho = (aux_ref[s, rows, c : c + 1] for c in range(3))
            last = gamma[STRETCH - 1 :]
            between = between_ref[s, n]
            state, update = state_ref[s, n], update_ref[s, rows]
            grad = grad_ref[s, rows].astype(f32)
            key_next = mm(k, grad_next)
            grad_update = through_ref[s, rows] + rho * key_next
            after.append(last * grad_next + inflow_ref[s, n] - mm(w_ref[s, rows], grad_update, 0, 0))
            grad_target = mm(inv_ref[s, n], grad_update, 0, 0)
            key_state, query_state = mm(k, state), mm(q, state)
            key_key, query_key = mm(k, k, 1, 1), mm(q, k, 1, 1)
            grad_query_key = mm(grad, update, 1, 1) * between
            grad_system = -mm(grad_target, update, 1, 1) * strict * between
            grad_key_key = beta * grad_system
            grad_key_state = -(beta * gamma) * grad_target
            grad_q_ref[s, rows] = gamma * mm(grad, state, 1, 1) + mm(grad_query_key, k)
            grad_k_ref[s, rows] = (
                mm(grad_query_key, q, 0, 0)
                + mm(rho * update, grad_next, 1, 1)
                + mm(grad_key_key, k)
                + mm(grad_key_key, k, 0, 0)
                + mm(grad_key_state, state, 1, 1)
            )
            grad_v_ref[s, rows] = beta * grad_target
            grad_beta = row_sum(grad_system * key_key) + row_sum(
                grad_target * (v - gamma * key_state)
            )
            grad_gamma = row_sum(grad * query_state) - beta * row_sum(grad_target * key_state)
            spread = grad_query_key * query_key + grad_key_key * key_key
            grad_rho = row_sum(key_next * update) * rho
            at_end = jnp.sum(grad_rho) + jnp.sum(row_sum(state * grad_next) * last)
            grad_cumulative = (
                row_sum(spread) + grad_gamma * gamma - grad_rho + jnp.where(at_last, at_end, 0.0)
            )
            grad_row_ref[s, pl.ds(n, 1)] = jnp.sum(spread, axis=0, keepdims=True)
            grad_aux_ref[s, rows] = jnp.where(lane == 0, grad_beta, grad_cumulative)
        return tuple(after)

    return lax.fori_loop(first, first + count, chain_block, exits)


def shaped(shape, kind=f32):
    return jax.ShapeDtypeStruct(shape, kind)


def norm_gain(source, gain_vec):
    return source * lax.rsqrt(jnp.mean(source * source, -1, keepdims=True) + EPSILON) * gain_vec


def unit_rows(source):
    return source * lax.rsqrt(jnp.sum(source * source, -1, keepdims=True) + EPSILON)


def gated_norm(mixed_head, gate_pre, gain_vec):
    scale = lax.rsqrt(jnp.mean(mixed_head * mixed_head, -1, keepdims=True) + EPSILON)
    return mixed_head * scale * gain_vec * jax.nn.silu(gate_pre)


def conv_core(padded, weight, doc_pad):
    tap_count = weight.shape[0]
    length = padded.shape[1] - (tap_count - 1)
    current = doc_pad[:, tap_count - 1 :]
    summed = jnp.zeros((padded.shape[0], length, padded.shape[2]), f32)
    for offset in range(tap_count):
        first_row = tap_count - 1 - offset
        window = padded[:, first_row : first_row + length]
        same_doc = (doc_pad[:, first_row : first_row + length] == current).astype(f32)
        summed = summed + weight[offset] * window * same_doc[:, :, None]
    return jax.nn.silu(summed)


def prepare(packed_ext, decay_head, beta_head, taps, decay_log, decay_bias, doc_ext, dk):
    mixed = conv_core(packed_ext, taps, doc_ext)
    queries = unit_rows(mixed[:, :, :dk]) * dk ** (-0.5)
    key_rows = unit_rows(mixed[:, :, dk : 2 * dk])
    values = mixed[:, :, 2 * dk :]
    beta_rows = jax.nn.sigmoid(beta_head)
    decays = -jnp.exp(decay_log) * jax.nn.softplus(decay_head + decay_bias)
    sequences, length = decays.shape
    cumulative = jnp.cumsum(decays.reshape(sequences, length // STRETCH, STRETCH), -1)
    return queries, key_rows, values, beta_rows, cumulative


def block_gates(cumulative, doc_blocks, doc_starts):
    places = jnp.arange(STRETCH)
    linked = (places[:, None] >= places[None, :]) & (
        doc_blocks[..., :, None] == doc_blocks[..., None, :]
    )
    apart = cumulative[..., :, None] - cumulative[..., None, :]
    between = jnp.where(linked, jnp.exp(jnp.where(linked, apart, 0.0)), 0.0)
    survive = jnp.exp(cumulative) * (doc_blocks == doc_starts[..., None]).astype(f32)
    return survive, between, between[..., -1, :]


def each_peer(axis, action):
    count, me = lax.axis_size(axis), lax.axis_index(axis)

    def step(distance, carry):
        action(distance, lax.rem(me + distance, count), lax.rem(me + count - distance, count))
        return carry

    lax.fori_loop(1, count, step, 0)


def far_devices(axis, action):
    count, me = lax.axis_size(axis) // CORES, lax.axis_index(axis)
    group, place = me // CORES, lax.rem(me, CORES)

    def step(distance, carry):
        ahead, behind = lax.rem(group + distance, count), lax.rem(group + count - distance, count)
        action(distance, ahead * CORES + place, behind * CORES + place)
        return carry

    lax.fori_loop(1, count, step, 0)


def chip_devices(action):
    far_devices("cp", action)


def near(axis):
    me = lax.axis_index(axis)
    return me + 1 - 2 * lax.rem(me, CORES)


def sibling():
    return near("cp")


def owner_target(turn):
    hd = lax.axis_size("hd")
    share = lax.axis_size("cp") // hd
    piece = CORES * turn + lax.rem(lax.axis_index("cp"), CORES)
    return share * lax.axis_index("hd") + piece // hd, lax.rem(piece, hd)


def owner_source(chip):
    share = lax.axis_size("cp") // lax.axis_size("hd")
    core = lax.rem(lax.axis_index("hd"), CORES)
    return CORES * chip + core, lax.axis_index("cp") // share


def column_target(turn):
    return CORES * turn + lax.rem(lax.axis_index("cp"), CORES), lax.axis_index("hd")


def row_target(turn):
    me = lax.axis_index("cp")
    return CORES * lax.axis_index("hd") + lax.rem(me, CORES), me // CORES


def is_me(at):
    return (at[0] == lax.axis_index("cp")) & (at[1] == lax.axis_index("hd"))


def each(count, action):
    def step(turn, carry):
        action(turn)
        return carry

    lax.fori_loop(0, count, step, 0)


def signal(target):
    pl.semaphore_signal(
        pltpu.get_barrier_semaphore(), inc=1, device_id=target,
        device_id_type=pl.DeviceIdType.MESH,
    )


def meet(heads=False, chips=False, owners=False, rows=False):
    cp, hd = lax.axis_size("cp"), lax.axis_size("hd")
    total = jnp.int32(0)
    if heads:
        each_peer("hd", lambda _, to, source: signal({"hd": to}))
        total += hd - 1
    if chips:
        chip_devices(lambda _, to, source: signal({"cp": to}))
        signal({"cp": sibling()})
        total += cp // CORES
    for wanted, count, source_of, target_of in (
        (owners, cp // CORES, owner_source, owner_target),
        (rows, 1, row_target, row_target),
    ):
        if wanted:

            def greet(turn, source_of=source_of):
                at = source_of(turn)

                @pl.when(jnp.logical_not(is_me(at)))
                def _():
                    signal(at)

            each(count, greet)
            total += count
            for turn in range(count):
                total -= is_me(target_of(turn)).astype(jnp.int32)
    pl.semaphore_wait(pltpu.get_barrier_semaphore(), total)


def remote(src, dst, send, recv, target):
    return pltpu.make_async_remote_copy(
        src_ref=src,
        dst_ref=dst,
        send_sem=send,
        recv_sem=recv,
        device_id=target,
        device_id_type=pl.DeviceIdType.MESH,
    )


class Exchange:
    def __init__(self, axis, source, landing, send, recv, local):
        self.axis, self.source, self.landing = axis, source, landing
        self.send, self.recv = send, recv
        me = lax.axis_index(axis)
        self.own = pltpu.make_async_copy(source(me), landing(me), local)

    def copy(self, distance, block, place, to):
        return remote(
            block, place, self.send.at[distance], self.recv.at[distance], {self.axis: to}
        )

    def start(self):
        me = lax.axis_index(self.axis)
        each_peer(
            self.axis,
            lambda distance, to, source: self.copy(
                distance, self.source(to), self.landing(me), to
            ).start(),
        )
        self.own.start()

    def arrive(self):
        each_peer(
            self.axis,
            lambda distance, to, source: self.copy(
                distance, self.source(to), self.landing(source), to
            ).wait_recv(),
        )
        self.own.wait()

    def leave(self):
        each_peer(
            self.axis,
            lambda distance, to, source: self.copy(
                distance, self.source(to), self.landing(source), to
            ).wait_send(),
        )


class PairGather:
    def __init__(self, axis, source, landing, send, recv, local, near_first=False):
        self.axis, self.near_first = axis, near_first
        self.source, self.landing, self.send, self.recv = source, landing, send, recv
        self.me, self.near = lax.axis_index(axis), near(axis)
        self.count = lax.axis_size(axis) // CORES
        self.own = pltpu.make_async_copy(source, landing(self.me), local)

    def copy(self, block, index, slot, to):
        return remote(
            block, self.landing(index), self.send.at[slot], self.recv.at[index], {self.axis: to}
        )

    def far(self, action):
        far_devices(self.axis, action)

    def start(self):
        self.copy(self.source, self.me, 0, self.near).start()
        self.far(lambda d, to, source: self.copy(self.source, self.me, d, to).start())
        self.own.start()

    def hand_on(self):
        if self.near_first:
            self.copy(self.source, self.near, 0, self.near).wait_recv()
            self.far(
                lambda d, to, source: self.copy(
                    self.landing(self.near), self.near, self.count + d, to
                ).start()
            )
        else:

            def pass_far(d, to, source):
                self.copy(self.source, source, d, to).wait_recv()
                self.copy(self.landing(source), source, self.count + d, self.near).start()

            self.far(pass_far)

    def arrive(self):
        shift = self.near - self.me
        if self.near_first:
            self.far(lambda d, to, source: self.copy(self.source, source, d, to).wait_recv())
        else:
            self.copy(self.source, self.near, 0, self.near).wait_recv()
        self.far(
            lambda d, to, source: self.copy(
                self.source, source + shift, d, self.near
            ).wait_recv()
        )
        self.own.wait()

    def leave(self):
        self.copy(self.source, self.me, 0, self.near).wait_send()
        self.far(lambda d, to, source: self.copy(self.source, self.me, d, to).wait_send())
        self.far(
            lambda d, to, source: self.copy(
                self.source, source, self.count + d, self.near
            ).wait_send()
        )


class PairReduce:
    def __init__(self, parts, inbox, sums, landed, swap, send, recv, local, target, source):
        self.parts, self.inbox, self.sums, self.landed = parts, inbox, sums, landed
        self.send, self.recv, self.local = send, recv, local
        self.target, self.source = target, source
        me = lax.axis_index("cp")
        self.chip, self.core = me // CORES, lax.rem(me, CORES)
        self.swap = remote(
            parts.at[:, 1 - self.core], inbox, swap.at[0], swap.at[1], {"cp": sibling()}
        )

    def start(self):
        self.swap.start()

    def move(self, turn, slot, to):
        return remote(
            self.sums.at[turn], self.landed.at[slot], self.send.at[turn], self.recv.at[slot], to
        )

    def add_pairs(self):
        self.swap.wait()

        def go(turn):
            total = self.parts[turn, self.core].astype(f32) + self.inbox[turn].astype(f32)
            self.sums[turn] = total.astype(bf16)
            to = self.target(turn)
            own = is_me(to)

            @pl.when(own)
            def _():
                pltpu.make_async_copy(
                    self.sums.at[turn], self.landed.at[self.chip], self.local
                ).start()

            @pl.when(jnp.logical_not(own))
            def _():
                self.move(turn, self.chip, to).start()

        each(self.sums.shape[0], go)

    def total(self):
        def get(chip):
            at = self.source(chip)
            own = is_me(at)

            @pl.when(own)
            def _():
                pltpu.make_async_copy(
                    self.sums.at[chip], self.landed.at[chip], self.local
                ).wait()

            @pl.when(jnp.logical_not(own))
            def _():
                self.move(chip, chip, at).wait_recv()

        each(self.landed.shape[0], get)
        return added(self.landed).astype(bf16)

    def leave(self):
        def done(turn):
            to = self.target(turn)

            @pl.when(jnp.logical_not(is_me(to)))
            def _():
                self.move(turn, turn, to).wait_send()

        each(self.sums.shape[0], done)


class RowMove:
    def __init__(self, rows, landing, send, recv, local):
        self.rows, self.send, self.recv, self.local = rows, send, recv, local
        self.slot = lax.rem(lax.axis_index("cp"), CORES)
        self.landing = lambda slot: lead_rows(landing, slot, rows.shape[0])
        self.to = row_target(0)
        self.own = is_me(self.to)
        self.move = remote(self.rows, self.landing(self.slot), send.at[0], recv.at[0], self.to)
        self.kept = pltpu.make_async_copy(rows, self.landing(self.slot), local)

    def shared(self, slot):
        return remote(
            self.landing(self.slot), self.landing(slot), self.send.at[1], self.recv.at[1],
            {"cp": sibling()},
        )

    def start(self):
        @pl.when(self.own)
        def _():
            self.kept.start()

        @pl.when(jnp.logical_not(self.own))
        def _():
            self.move.start()

    def hand_on(self):
        @pl.when(self.own)
        def _():
            self.kept.wait()

        @pl.when(jnp.logical_not(self.own))
        def _():
            self.move.wait_recv()

        self.shared(self.slot).start()

    def arrive(self):
        self.shared(1 - self.slot).wait_recv()

    def leave(self):
        self.shared(self.slot).wait_send()

        @pl.when(jnp.logical_not(self.own))
        def _():
            self.move.wait_send()


def sems(*counts):
    found = []
    for count in counts:
        found += [pltpu.SemaphoreType.DMA((count,))] * 2 + [pltpu.SemaphoreType.DMA]
    return found


def reduce_scratch(parts):
    half = (parts.shape[0], *parts.shape[2:])
    return [pltpu.VMEM(half, bf16)] * 3 + [
        pltpu.SemaphoreType.DMA((2,)), *sems(parts.shape[0])
    ]


def token_rows(ref, index, tokens):
    return ref.at[:, pl.ds(pl.multiple_of(index * tokens, tokens), tokens)]


def lead_rows(ref, index, rows):
    return ref.at[pl.ds(pl.multiple_of(index * rows, rows), rows)]


def comm_call(body, out_shape, places, operands, spots, scratch, number):
    kinds = {"any": pl.ANY, "vmem": pltpu.VMEM}
    return pl.pallas_call(
        body,
        out_shape=out_shape,
        in_specs=[pl.BlockSpec(memory_space=kinds[k]) for k in places],
        out_specs=tuple(pl.BlockSpec(memory_space=kinds[k]) for k in spots),
        scratch_shapes=scratch,
        compiler_params=pltpu.CompilerParams(
            collective_id=number, has_side_effects=True, vmem_limit_bytes=VMEM_LIMIT
        ),
    )(*operands)


def open_kernel(hidden_ref, front_ref, hidden_all_ref, front_all_ref, *flags):
    tokens, shard = hidden_ref.shape[1], front_ref.shape[0]
    meet(heads=True, chips=True)
    moves = (
        PairGather(
            "hd", hidden_ref, lambda at: token_rows(hidden_all_ref, at, tokens), *flags[:3],
            near_first=True,
        ),
        PairGather("cp", front_ref, lambda at: lead_rows(front_all_ref, at, shard), *flags[3:6]),
    )
    for move in moves:
        move.start()
    for move in moves:
        move.hand_on()
    for move in moves:
        move.arrive()
        move.leave()


def place_of():
    me = lax.axis_index("cp")
    return me // CORES, lax.rem(me, CORES)


def forward_kernel(
    q_ref, k_ref, v_ref, aux_ref, between_ref, cot_ref, ffn_ref, output_ref, down_ref,
    mixed_ref, state_ref, update_ref, w_ref, inv_ref, maps_ref, both_ref,
    cot_all_ref, ffn_all_ref, output_part_ref, down_part_ref,
    x_ref, u_ref, own_ref, other_ref, entry_ref, give_ref, pair_sems, *flags
):
    sequences, _, dk = k_ref.shape
    dv = v_ref.shape[2]
    tokens, shard = cot_ref.shape[1], ffn_ref.shape[0]
    chip, core = place_of()
    early = core == 0
    meet(heads=True, chips=True, rows=True)
    carried = (
        RowMove(output_ref, output_part_ref, *flags[3:6]),
        RowMove(down_ref, down_part_ref, *flags[6:9]),
        PairGather("cp", ffn_ref, lambda at: lead_rows(ffn_all_ref, at, shard), *flags[:3]),
    )
    cot_move = PairGather(
        "hd", cot_ref, lambda at: token_rows(cot_all_ref, at, tokens), *flags[9:12],
        near_first=True,
    )
    cot_move.start()
    for move in reversed(carried):
        move.start()
    segment_maps(
        k_ref, v_ref, aux_ref, between_ref, x_ref, own_ref, w_ref, u_ref, inv_ref,
        cot_move.hand_on,
    )
    swap = remote(
        own_ref.at[1 - core], other_ref, pair_sems.at[0], pair_sems.at[1], {"cp": sibling()}
    )
    swap.start()
    swap.wait()
    mine, theirs = own_ref[core], other_ref[...]
    both_ref[0] = jnp.where(early, mine, theirs)
    both_ref[1] = jnp.where(early, theirs, mine)
    first, second = both_ref[0].astype(f32), both_ref[1].astype(f32)
    pair = mm(second[:, :dk], first)
    pair = jnp.concatenate([pair[:, :dk], pair[:, dk:] + second[:, dk:]], 1)
    maps_ref[chip] = pair.astype(bf16)
    settle = spread_chips(maps_ref, flags[12], flags[13])
    for move in carried:
        move.hand_on()
    settle()

    def enter(hop, state):
        return mm(maps_ref[hop, :, :dk].astype(f32), state) + maps_ref[hop, :, dk:].astype(f32)

    entered = lax.fori_loop(0, chip, enter, jnp.zeros((dk, dv), f32))
    halfway = mm(first[:, :dk], entered) + first[:, dk:]
    entry_ref[core] = jnp.where(early, entered, halfway)
    give_ref[...] = jnp.where(early, halfway, entered)
    give = remote(
        give_ref, entry_ref.at[core], pair_sems.at[2], pair_sems.at[3], {"cp": sibling()}
    )
    give.start()
    remote(
        give_ref, entry_ref.at[1 - core], pair_sems.at[2], pair_sems.at[3], {"cp": sibling()}
    ).wait()
    run_segment(
        entry_ref, x_ref, q_ref, k_ref, aux_ref, between_ref, w_ref, u_ref,
        mixed_ref, state_ref, update_ref,
    )
    for move in (*carried, cot_move):
        move.arrive()
        move.leave()


def spread_chips(ref, send, recv):
    chip, _ = place_of()

    def copy(distance, index, to):
        return remote(ref.at[index], ref.at[index], send.at[distance], recv.at[distance], {"cp": to})

    chip_devices(lambda d, to, source: copy(d, chip, to).start())

    def settle():
        chip_devices(lambda d, to, source: copy(d, source // CORES, to).wait_recv())
        chip_devices(lambda d, to, source: copy(d, chip, to).wait_send())

    return settle


def backward_kernel(
    q_ref, k_ref, v_ref, aux_ref, between_ref, w_ref, inv_ref, state_ref, update_ref, grad_ref,
    maps_ref, both_ref, ffn_ref, down_ref, output_ref, out_part_ref, middle_ref,
    grad_q_ref, grad_k_ref, grad_v_ref, grad_aux_ref, grad_row_ref, ffn_all_ref, down_all_ref,
    output_all_ref, block_ref,
    through_ref, inflow_ref, own_ref, other_ref, locals_ref, exit_ref, give_ref,
    ffn_own_ref, down_own_ref, output_own_ref, out_landed_ref, pair_sems, chip_send, chip_recv,
    *flags
):
    sequences, length, dk = k_ref.shape
    dv = v_ref.shape[2]
    blocks = length // STRETCH
    chip, core = place_of()
    chips = locals_ref.shape[0]
    late = core == CORES - 1
    meet(heads=True, chips=True, owners=True)
    reduces = (
        PairReduce(ffn_ref, *flags[:7], column_target, column_source),
        PairReduce(down_ref, *flags[7:14], owner_target, owner_source),
        PairReduce(output_ref, *flags[14:21], owner_target, owner_source),
    )
    tokens = middle_ref.shape[1]
    out_move = Exchange(
        "hd",
        lambda to: token_rows(out_part_ref, to, tokens),
        lambda at: out_landed_ref.at[at],
        *flags[30:33],
    )
    for move in (*reduces, out_move):
        move.start()
    segment_local(
        q_ref, k_ref, aux_ref, between_ref, w_ref, grad_ref, through_ref, inflow_ref, own_ref
    )
    swap = remote(
        own_ref.at[1 - core], other_ref, pair_sems.at[0], pair_sems.at[1], {"cp": sibling()}
    )
    swap.start()
    swap.wait()
    mine, theirs = own_ref[core].astype(f32), other_ref[...].astype(f32)
    first, second = jnp.where(late, theirs, mine), jnp.where(late, mine, theirs)
    locals_ref[chip] = (mm(both_ref[0, :, :dk].astype(f32), second, 0, 0) + first).astype(bf16)
    settle = spread_chips(locals_ref, chip_send, chip_recv)
    for move in reduces:
        move.add_pairs()
    settle()

    def leave(hop, state):
        source = chips - 1 - hop
        return mm(maps_ref[source, :, :dk].astype(f32), state, 0, 0) + locals_ref[
            source
        ].astype(f32)

    left = lax.fori_loop(0, chips - 1 - chip, leave, jnp.zeros((dk, dv), f32))
    halfway = mm(both_ref[1, :, :dk].astype(f32), left, 0, 0) + second
    exit_ref[core] = jnp.where(late, left, halfway)
    give_ref[...] = jnp.where(late, halfway, left)
    remote(
        give_ref, exit_ref.at[core], pair_sems.at[2], pair_sems.at[3], {"cp": sibling()}
    ).start()
    remote(
        give_ref, exit_ref.at[1 - core], pair_sems.at[2], pair_sems.at[3], {"cp": sibling()}
    ).wait()
    refs = (
        q_ref, k_ref, v_ref, aux_ref, between_ref, w_ref, inv_ref, state_ref, update_ref,
        grad_ref, through_ref, inflow_ref,
        grad_q_ref, grad_k_ref, grad_v_ref, grad_aux_ref, grad_row_ref,
    )
    exits = tuple(exit_ref[s] for s in range(sequences))
    exits = back_blocks(0, blocks // 2, exits, *refs)
    spreads = []
    for n, (move, own, everywhere) in enumerate(
        zip(
            reduces,
            (ffn_own_ref, down_own_ref, output_own_ref),
            (ffn_all_ref, down_all_ref, output_all_ref),
        )
    ):
        own[...] = move.total()
        spreads.append(spread_piece(own, everywhere, flags[21 + 3 * n : 24 + 3 * n]))
    out_move.arrive()
    block_ref[...] = (middle_ref[...] + added(out_landed_ref)).astype(bf16)
    for spread in spreads:
        spread.hand_on()
    back_blocks(blocks // 2, blocks - blocks // 2, exits, *refs)
    for move in (*reduces, out_move):
        move.leave()
    for spread in spreads:
        spread.arrive()
        spread.leave()


def column_source(chip):
    return column_target(chip)


def spread_piece(own, everywhere, flags):
    spread = PairGather("hd", own, lambda at: everywhere.at[at], *flags, near_first=True)
    spread.start()
    return spread


def added(landed_ref):
    total = landed_ref[0].astype(f32)
    for index in range(1, landed_ref.shape[0]):
        total += landed_ref[index].astype(f32)
    return total


def spread_own(own_ref, all_ref, tokens, flags):
    moves = [
        PairGather(
            "hd",
            own_ref.at[s],
            lambda at, s=s: all_ref.at[s, pl.ds(pl.multiple_of(at * tokens, tokens), tokens)],
            *flags[3 * s : 3 * s + 3],
            near_first=s % 2 == 0,
        )
        for s in range(own_ref.shape[0])
    ]
    for move in moves:
        move.start()
    return moves


def settle_all(moves):
    for move in moves:
        move.hand_on()
    for move in moves:
        move.arrive()
        move.leave()


def middle_kernel(
    partial_ref, hidden_ref, gain_ref, middle_ref, ffn_all_ref, landed_ref, own_ref, *flags
):
    tokens = hidden_ref.shape[1]
    meet(heads=True)
    move = Exchange(
        "hd", lambda to: token_rows(partial_ref, to, tokens), lambda at: landed_ref.at[at], *flags[:3]
    )
    move.start()
    move.arrive()
    middle = hidden_ref[...].astype(f32) + added(landed_ref)
    middle_ref[...] = middle
    own_ref[...] = norm_gain(middle, gain_ref[...]).astype(bf16)
    after = spread_own(own_ref, ffn_all_ref, tokens, flags[3:])
    settle_all(after)
    move.leave()


def norm_back(source, gain_vec, grad):
    scale = lax.rsqrt(jnp.mean(source * source, -1, keepdims=True) + EPSILON)
    lifted = grad * gain_vec
    mixed = jnp.mean(source * lifted, -1, keepdims=True)
    return scale * lifted - source * (scale * scale * scale) * mixed, source * scale * grad


def ffn_back_kernel(
    grad_part_ref, middle_ref, cot_ref, gain_ref,
    grad_middle_ref, grad_gain_ref, grad_all_ref, grad_landed_ref, own_ref, *flags
):
    tokens = middle_ref.shape[1]
    meet(heads=True)
    move = Exchange(
        "hd",
        lambda to: token_rows(grad_part_ref, to, tokens),
        lambda at: grad_landed_ref.at[at],
        *flags[:3],
    )
    move.start()
    move.arrive()
    back, gain_terms = norm_back(middle_ref[...], gain_ref[...], added(grad_landed_ref))
    grad_middle = cot_ref[...].astype(f32) + back
    own_ref[...] = grad_middle.astype(bf16)
    after = spread_own(own_ref, grad_all_ref, tokens, flags[3:])
    grad_middle_ref[...] = grad_middle
    grad_gain_ref[...] = jnp.sum(jnp.sum(gain_terms, axis=0), axis=0, keepdims=True)
    settle_all(after)
    move.leave()


def close_kernel(
    normed_part_ref, front_ref, small_ref, hidden_ref, grad_middle_ref, gain_ref,
    grad_in_ref, front_all_ref, small_sum_ref,
    normed_landed, small_landed, front_own, *flags
):
    tokens = hidden_ref.shape[1]
    meet(heads=True, chips=True)
    reduce = PairReduce(front_ref, *flags[:7], column_target, column_source)
    normed_move = Exchange(
        "hd",
        lambda to: token_rows(normed_part_ref, to, tokens),
        lambda at: normed_landed.at[at],
        *flags[7:10],
    )
    small_move = PairGather("cp", small_ref, lambda at: small_landed.at[at], *flags[10:13])
    reduce.start()
    small_move.start()
    normed_move.start()
    reduce.add_pairs()
    small_move.hand_on()
    front_own[...] = reduce.total()
    spread = spread_piece(front_own, front_all_ref, flags[13:16])
    normed_move.arrive()
    spread.hand_on()
    back, _ = norm_back(hidden_ref[...].astype(f32), gain_ref[...], added(normed_landed))
    grad_in_ref[...] = (grad_middle_ref[...] + back).astype(bf16)
    small_move.arrive()
    small_sum_ref[...] = added(small_landed)
    for move in (normed_move, small_move, reduce):
        move.leave()
    spread.arrive()
    spread.leave()


def passed_along(block, axis, distance):
    devices = range(lax.axis_size(axis))
    route = [(i - distance, i) for i in devices if i - distance in devices]
    return lax.ppermute(block, axis, route)


def on_device(
    hidden_in, doc_ids, w_query, w_key, w_value, w_decay, w_beta, w_gate_out, w_output,
    w_ffn_gate, w_ffn_up, w_ffn_down, conv_query, conv_key, conv_value, decay_log, decay_bias,
    gain_attn, gain_ffn, gain_head, cotangent,
):
    place, head = lax.axis_index("cp"), lax.axis_index("hd")
    cp, hd = lax.axis_size("cp"), lax.axis_size("hd")
    sequences, tokens, width = hidden_in.shape
    shard = w_query.shape[0]
    dk, dv = w_query.shape[1] // hd, w_value.shape[1] // hd
    ff = w_ffn_gate.shape[1] // hd
    ffp = -(-ff // LANES) * LANES
    qkv = 2 * dk + dv
    side, gate_at = qkv, qkv + LANES
    span = tokens * hd
    blocks = span // STRETCH

    def part(weight):
        cols = weight.shape[1] // hd
        return lax.dynamic_slice_in_dim(weight, head * cols, cols, 1)

    def ff_pad(weight):
        return jnp.pad(part(weight), ((0, 0), (0, ffp - ff)))

    head_share = gain_head.shape[0]
    side_cols = jnp.stack(
        [
            part(w_decay)[:, 0],
            part(w_beta)[:, 0],
            gain_attn,
            gain_ffn,
            jnp.pad(gain_head, (0, shard - head_share)),
        ],
        1,
    )
    front = jnp.concatenate(
        [
            part(w_query),
            part(w_key),
            part(w_value),
            jnp.pad(side_cols, ((0, 0), (0, LANES - side_cols.shape[1]))),
            part(w_gate_out),
        ],
        1,
    )
    hidden_all, front_full = comm_call(
        open_kernel,
        (shaped((sequences, span, width), bf16), shaped((width, front.shape[1]), bf16)),
        ("any", "any"),
        (hidden_in, front),
        ("any", "any"),
        sems(hd, cp),
        1,
    )
    ffn_front = jnp.concatenate([ff_pad(w_ffn_gate), ff_pad(w_ffn_up)], 1)

    attn_gain = front_full[:, side + 2].astype(f32)
    ffn_gain = front_full[:, side + 3].astype(f32)
    head_gain = front_full[:, side + 4].reshape(cp, shard)[:, :head_share].reshape(-1).astype(f32)

    def dot(a, b, spec):
        return jnp.einsum(spec, a, b, preferred_element_type=f32)

    inputs_all = hidden_all.astype(f32)
    scale_all = lax.rsqrt(jnp.mean(inputs_all * inputs_all, -1, keepdims=True) + EPSILON)
    normed = (inputs_all * scale_all * attn_gain).astype(bf16)
    projected = dot(normed, front_full, "std,de->ste")
    packed = projected[:, :, :qkv].astype(bf16)
    gate_pre = projected[:, :, gate_at:]
    decay_head = projected[:, :, side].astype(bf16).astype(f32)
    beta_head = projected[:, :, side + 1].astype(bf16).astype(f32)

    margin = conv_query.shape[0] - 1
    rim = passed_along(packed[:, -margin:], "cp", 1)
    doc_pad = jnp.concatenate([jnp.full((sequences, margin), -1, jnp.int32), doc_ids], 1)
    doc_ext = lax.dynamic_slice_in_dim(doc_pad, place * span, span + margin, 1)
    doc_blocks = doc_ext[:, margin:].reshape(sequences, blocks, STRETCH)
    doc_starts = doc_ext[:, margin - 1 : -1].reshape(sequences, blocks, STRETCH)[:, :, 0]
    taps = jnp.concatenate([conv_query, conv_key, conv_value], 1).astype(f32)
    prepared, prepare_pull = jax.vjp(
        lambda *entries: prepare(*entries, doc_ext, dk),
        jnp.concatenate([rim, packed], 1).astype(f32),
        decay_head,
        beta_head,
        taps,
        decay_log.astype(f32),
        decay_bias.astype(f32),
    )
    queries, key_rows, values, beta_rows, cumulative = prepared
    survive, between, rho = block_gates(cumulative, doc_blocks, doc_starts)
    flat = (sequences, span)
    aux = jnp.stack([beta_rows, survive.reshape(flat), rho.reshape(flat)], -1)
    aux = jnp.pad(aux, ((0, 0), (0, 0), (0, 5)))
    chips = cp // CORES
    share = cp // hd
    (
        mixed, states, updates, weighted, inverse, maps, both,
        cot_all, ffn_full, output_part, down_part,
    ) = comm_call(
        forward_kernel,
        (
            shaped((sequences, span, dv), bf16),
            shaped((sequences, blocks, dk, dv)),
            shaped((sequences, span, dv)),
            shaped((sequences, span, dk)),
            shaped((sequences, blocks, STRETCH, STRETCH)),
            shaped((chips, dk, dk + dv), bf16),
            shaped((CORES, dk, dk + dv), bf16),
            shaped((sequences, span, width), bf16),
            shaped((width, 2 * ffp), bf16),
            shaped((share * w_output.shape[0], width), bf16),
            shaped((share * w_ffn_down.shape[0], width), bf16),
        ),
        ("vmem",) * 5 + ("any",) * 4,
        (
            queries, key_rows, values, aux, between, cotangent, ffn_front, w_output, w_ffn_down,
        ),
        ("vmem",) * 7 + ("any",) * 4,
        [
            pltpu.VMEM((sequences, blocks, dk, dk + dv), f32),
            pltpu.VMEM((sequences, span, dv), f32),
            pltpu.VMEM((sequences, dk, dk + dv), bf16),
            pltpu.VMEM((dk, dk + dv), bf16),
            pltpu.VMEM((sequences, dk, dv), f32),
            pltpu.VMEM((dk, dv), f32),
            pltpu.SemaphoreType.DMA((4,)),
            *sems(cp, CORES, CORES, hd),
            pltpu.SemaphoreType.DMA((chips,)),
            pltpu.SemaphoreType.DMA((chips,)),
        ],
        2,
    )
    down_part = jnp.pad(down_part, ((0, ffp - ff), (0, 0)))
    mixed_float = mixed.astype(f32)
    normed_head, gated_pull = jax.vjp(gated_norm, mixed_float, gate_pre, head_gain)
    normed_head = normed_head.astype(bf16)
    landing = pltpu.VMEM((hd, sequences, tokens, width), bf16)
    own_tokens = pltpu.VMEM((sequences, tokens, width), bf16)
    ffn_gain = ffn_gain[None]
    middle, ffn_all = comm_call(
        middle_kernel,
        (shaped(hidden_in.shape), shaped((sequences, span, width), bf16)),
        ("any", "vmem", "vmem"),
        (dot(normed_head, output_part, "ste,ed->std").astype(bf16), hidden_in, ffn_gain),
        ("vmem", "any"),
        [landing, own_tokens, *sems(hd, *(hd,) * sequences)],
        4,
    )
    gate_up = dot(ffn_all, ffn_full, "std,df->stf")
    inner, swiglu_pull = jax.vjp(
        lambda both: jax.nn.silu(both[..., :ffp]) * both[..., ffp:], gate_up
    )
    inner = inner.astype(bf16)
    grad_inner = dot(cot_all, down_part, "std,fd->stf")
    grad_gate_up = swiglu_pull(grad_inner)[0].astype(bf16)
    out_partial = dot(inner, down_part, "stf,fd->std").astype(bf16)
    grad_middle, grad_ffn_gain, grad_attention = comm_call(
        ffn_back_kernel,
        (shaped(hidden_in.shape), shaped((1, width)), shaped((sequences, span, width), bf16)),
        ("any", "vmem", "vmem", "vmem"),
        (
            dot(grad_gate_up, ffn_full, "stf,df->std").astype(bf16),
            middle, cotangent, ffn_gain,
        ),
        ("vmem", "vmem", "any"),
        [landing, own_tokens, *sems(hd, *(hd,) * sequences)],
        5,
    )

    def weight_grad(left_side, right_side):
        return dot(left_side, right_side, "std,ste->de")

    def pieces(grad):
        rows = grad.shape[0] // cp
        split = grad.reshape(chips, CORES, rows, width)
        return jnp.pad(split, ((0, 0), (0, 0), (0, -rows % 16), (0, 0))).astype(bf16)

    def by_owner(grad):
        return grad.reshape(chips, CORES, shard, grad.shape[1]).astype(bf16)

    grad_down = pieces(weight_grad(inner, cot_all)[:ff])

    grad_normed_head = dot(grad_attention, output_part, "std,ed->ste")
    grad_output = pieces(weight_grad(normed_head, grad_attention))
    grad_mixed, grad_gate_pre, grad_head_gain = gated_pull(grad_normed_head)
    grad_mixed = grad_mixed.astype(bf16)
    grad_gate_pre = grad_gate_pre.astype(bf16)
    grad_ffn = by_owner(
        jnp.concatenate(
            [
                weight_grad(ffn_all, grad_gate_up).astype(bf16),
                weight_grad(normed, grad_gate_pre).astype(bf16),
            ],
            1,
        )
    )
    ffn_share, down_share, output_share = (
        entry.shape[2:] for entry in (grad_ffn, grad_down, grad_output)
    )
    (
        grad_q, grad_k, grad_v, grad_aux, grad_row, grad_ffn, grad_down, new_output, block_out,
    ) = comm_call(
        backward_kernel,
        (
            shaped((sequences, span, dk)),
            shaped((sequences, span, dk)),
            shaped((sequences, span, dv)),
            shaped((sequences, span, 8)),
            shaped((sequences, blocks, STRETCH)),
            shaped((hd, *ffn_share), bf16),
            shaped((hd, *down_share), bf16),
            shaped((hd, *output_share), bf16),
            shaped(hidden_in.shape, bf16),
        ),
        ("vmem",) * 15 + ("any", "vmem"),
        (
            queries, key_rows, values, aux, between, weighted, inverse, states, updates,
            grad_mixed, maps, both, grad_ffn, grad_down, grad_output, out_partial, middle,
        ),
        ("vmem",) * 5 + ("any",) * 3 + ("vmem",),
        [
            pltpu.VMEM((sequences, span, dv), f32),
            pltpu.VMEM((sequences, blocks, dk, dv), f32),
            pltpu.VMEM((sequences, dk, dv), bf16),
            pltpu.VMEM((dk, dv), bf16),
            pltpu.VMEM((chips, dk, dv), bf16),
            pltpu.VMEM((sequences, dk, dv), f32),
            pltpu.VMEM((dk, dv), f32),
            pltpu.VMEM(ffn_share, bf16),
            pltpu.VMEM(down_share, bf16),
            pltpu.VMEM(output_share, bf16),
            landing,
            pltpu.SemaphoreType.DMA((4,)),
            pltpu.SemaphoreType.DMA((chips,)),
            pltpu.SemaphoreType.DMA((chips,)),
            *reduce_scratch(grad_ffn),
            *reduce_scratch(grad_down),
            *reduce_scratch(grad_output),
            *sems(hd, hd, hd, hd),
        ],
        3,
    )
    grad_cumulative = grad_aux[:, :, 1].reshape(sequences, blocks, STRETCH) - grad_row
    grad_ext, grad_decay, grad_beta, grad_taps, grad_log, grad_bias = prepare_pull(
        (grad_q, grad_k, grad_v, grad_aux[:, :, 0], grad_cumulative)
    )
    back = passed_along(grad_ext[:, :margin], "cp", -1)
    grad_packed = grad_ext[:, margin:].at[:, -margin:].add(back).astype(bf16)
    grad_projected = jnp.concatenate(
        [
            grad_packed,
            jnp.pad(
                jnp.stack([grad_decay, grad_beta], -1).astype(bf16),
                ((0, 0), (0, 0), (0, LANES - 2)),
            ),
            grad_gate_pre,
        ],
        -1,
    )
    partial_normed = dot(grad_projected, front_full, "ste,de->std")
    grad_attn_gain = jnp.sum(inputs_all * scale_all * partial_normed, (0, 1))
    grad_front = weight_grad(normed, grad_projected[:, :, :gate_at])
    spread_gain = jnp.pad(
        grad_head_gain.reshape(cp, head_share), ((0, 0), (0, shard - head_share))
    ).reshape(-1)
    gains = jnp.stack([grad_attn_gain, grad_ffn_gain[0], spread_gain], 1)
    grad_front += jnp.pad(gains, ((0, 0), (side + 2, LANES - 2 - gains.shape[1])))

    small = jnp.concatenate(
        [
            grad_taps,
            jnp.pad(jnp.stack([grad_log, grad_bias], 1), ((0, 0), (0, qkv - 2))),
        ],
        0,
    )
    small = jnp.pad(small, ((0, -small.shape[0] % 8), (0, 0)))
    grad_front = by_owner(grad_front)
    front_share = grad_front.shape[2:]
    grad_in, grad_front, small = comm_call(
        close_kernel,
        (shaped(hidden_in.shape, bf16), shaped((hd, *front_share), bf16), shaped(small.shape)),
        ("any", "vmem", "any") + ("vmem",) * 3,
        (
            partial_normed.astype(bf16), grad_front, small, hidden_in, grad_middle,
            attn_gain[None],
        ),
        ("vmem", "any", "vmem"),
        [
            landing,
            pltpu.VMEM((cp, *small.shape), f32),
            pltpu.VMEM(front_share, bf16),
            *reduce_scratch(grad_front),
            *sems(hd, cp, hd),
        ],
        6,
    )

    def owned(grad, rows):
        return grad[:, : rows // hd].reshape(rows, width).astype(f32)

    taps_rows = margin + 1

    def columns(grad):
        return jnp.swapaxes(grad, 0, 1).reshape(grad.shape[1], -1).astype(f32)

    gain_sums = jnp.sum(grad_front[:, :, side + 2 : side + 5].astype(f32), 0)
    return (
        block_out,
        grad_in,
        columns(grad_front[:, :, :dk]),
        columns(grad_front[:, :, dk : 2 * dk]),
        columns(grad_front[:, :, 2 * dk : qkv]),
        columns(grad_front[:, :, side : side + 1]),
        columns(grad_front[:, :, side + 1 : side + 2]),
        columns(grad_ffn[:, :, 2 * ffp :]),
        owned(new_output, w_output.shape[0]),
        columns(grad_ffn[:, :, :ff]),
        columns(grad_ffn[:, :, ffp : ffp + ff]),
        owned(grad_down, w_ffn_down.shape[0]),
        small[:taps_rows, :dk],
        small[:taps_rows, dk : 2 * dk],
        small[:taps_rows, 2 * dk :],
        small[taps_rows, :1],
        small[taps_rows, 1:2],
        gain_sums[:, 0],
        gain_sums[:, 1],
        gain_sums[:head_share, 2],
    )


def solution(mesh):
    tokens, rows, cols = P(None, ("cp", "hd"), None), P("cp", None), P(None, "hd")
    weights = (rows,) * 10
    return jax.shard_map(
        on_device,
        mesh=mesh,
        in_specs=(tokens, P(), *weights, cols, cols, cols, P("hd"), P("hd"))
        + (P("cp"),) * 3
        + (tokens,),
        out_specs=(tokens, tokens, *weights, cols, cols, cols, P("hd"), P("hd"))
        + (P("cp"),) * 3,
        check_vma=False,
    )
```

```python
import jax
import jax.numpy as jnp
from jax import lax
from jax.experimental import pallas as pl
from jax.experimental.pallas import tpu as pltpu
from jax.sharding import PartitionSpec as P

STRETCH = 64
LANES = 128
CORES = 2
HIGHEST = lax.Precision.HIGHEST
EPSILON = 1e-06
bf16, f32 = jnp.bfloat16, jnp.float32
VMEM_LIMIT = 48 * 1024 * 1024


def mm(a, b, ca=1, cb=0):
    return lax.dot_general(
        a, b, (((ca,), (cb,)), ((), ())), precision=HIGHEST, preferred_element_type=f32
    )


def lower_strict():
    rows = lax.broadcasted_iota(jnp.int32, (STRETCH, STRETCH), 0)
    cols = lax.broadcasted_iota(jnp.int32, (STRETCH, STRETCH), 1)
    return (rows > cols).astype(f32), (rows == cols).astype(f32)


def block_rows(n):
    return pl.ds(pl.multiple_of(n * STRETCH, STRETCH), STRETCH)


def segment_maps(
    k_ref, v_ref, aux_ref, between_ref, x_ref, end_ref, w_ref, u_ref, inv_ref, halfway
):
    sequences, length, dk = k_ref.shape
    dv = v_ref.shape[2]
    blocks = length // STRETCH
    strict, unit = lower_strict()

    def prepare_block(pair, carry):
        streams = [(s, 2 * pair + half) for s in range(sequences) for half in range(2)]
        powers, inverses = [], []
        for s, n in streams:
            k = k_ref[s, block_rows(n)]
            beta = aux_ref[s, block_rows(n), 0:1]
            powers.append(-beta * (between_ref[s, n] * strict) * mm(k, k, 1, 1))
            inverses.append(unit + powers[-1])
        for level in range(STRETCH.bit_length() - 2):
            powers = [mm(power, power) for power in powers]
            inverses = [
                inverse + mm(inverse, power) for inverse, power in zip(inverses, powers)
            ]
        for (s, n), inverse in zip(streams, inverses):
            rows = block_rows(n)
            beta = aux_ref[s, rows, 0:1]
            gamma = aux_ref[s, rows, 1:2]
            inv_ref[s, n] = inverse
            w_ref[s, rows] = mm(inverse, beta * gamma * k_ref[s, rows])
            u_ref[s, rows] = mm(inverse, beta * v_ref[s, rows])
        return carry

    lax.fori_loop(0, blocks // 4, prepare_block, 0)
    halfway()
    lax.fori_loop(blocks // 4, blocks // 2, prepare_block, 0)

    wide = (dk, dk + dv)
    start = (
        lax.broadcasted_iota(jnp.int32, wide, 0) == lax.broadcasted_iota(jnp.int32, wide, 1)
    ).astype(f32)

    def chain_block(n, states):
        rows = block_rows(n)
        after = []
        for s in range(sequences):
            x = states[s]
            x_ref[s, n] = x
            gone = mm(w_ref[s, rows], x)
            update = jnp.concatenate([-gone[:, :dk], u_ref[s, rows] - gone[:, dk:]], 1)
            rho = aux_ref[s, rows, 2:3]
            last = aux_ref[s, rows, 1:2][STRETCH - 1 :]
            after.append(last * x + mm(k_ref[s, rows], rho * update, 0, 0))
        return tuple(after)

    ends = lax.fori_loop(0, blocks, chain_block, (start,) * sequences)
    for s in range(sequences):
        end_ref[s] = ends[s].astype(end_ref.dtype)


def run_segment(
    entry_ref, x_ref, q_ref, k_ref, aux_ref, between_ref, w_ref, u_ref,
    out_ref, state_ref, update_ref,
):
    sequences, length, dk = k_ref.shape
    blocks = length // STRETCH

    def run_block(n, carry):
        rows = block_rows(n)
        for s in range(sequences):
            q, k = q_ref[s, rows], k_ref[s, rows]
            state = mm(x_ref[s, n, :, :dk], entry_ref[s]) + x_ref[s, n, :, dk:]
            update = u_ref[s, rows] - mm(w_ref[s, rows], state)
            scores = mm(q, k, 1, 1) * between_ref[s, n]
            out = aux_ref[s, rows, 1:2] * mm(q, state) + mm(scores, update)
            state_ref[s, n] = state
            update_ref[s, rows] = update
            out_ref[s, rows] = out.astype(out_ref.dtype)
        return carry

    lax.fori_loop(0, blocks, run_block, 0)


def segment_local(
    q_ref, k_ref, aux_ref, between_ref, w_ref, grad_ref, through_ref, inflow_ref, local_ref
):
    sequences, length, dk = k_ref.shape
    dv = grad_ref.shape[2]
    blocks = length // STRETCH

    def prepare_block(n, carry):
        rows = block_rows(n)
        for s in range(sequences):
            q, k = q_ref[s, rows], k_ref[s, rows]
            grad = grad_ref[s, rows].astype(f32)
            scores = mm(q, k, 1, 1) * between_ref[s, n]
            through_ref[s, rows] = mm(scores, grad, 0, 0)
            inflow_ref[s, n] = mm(q, aux_ref[s, rows, 1:2] * grad, 0, 0)
        return carry

    lax.fori_loop(0, blocks, prepare_block, 0)

    def chain_block(back, states):
        n = blocks - 1 - back
        rows = block_rows(n)
        after = []
        for s in range(sequences):
            rho = aux_ref[s, rows, 2:3]
            last = aux_ref[s, rows, 1:2][STRETCH - 1 :]
            grad_update = through_ref[s, rows] + rho * mm(k_ref[s, rows], states[s])
            after.append(
                last * states[s] + inflow_ref[s, n] - mm(w_ref[s, rows], grad_update, 0, 0)
            )
        return tuple(after)

    ends = lax.fori_loop(0, blocks, chain_block, (jnp.zeros((dk, dv), f32),) * sequences)
    for s in range(sequences):
        local_ref[s] = ends[s].astype(local_ref.dtype)


def back_blocks(
    first, count, exits,
    q_ref, k_ref, v_ref, aux_ref, between_ref, w_ref, inv_ref,
    state_ref, update_ref, grad_ref, through_ref, inflow_ref,
    grad_q_ref, grad_k_ref, grad_v_ref, grad_aux_ref, grad_row_ref,
):
    sequences, length, dk = k_ref.shape
    blocks = length // STRETCH
    strict, _ = lower_strict()
    at_last = lax.broadcasted_iota(jnp.int32, (STRETCH, 1), 0) == STRETCH - 1
    lane = lax.broadcasted_iota(jnp.int32, (STRETCH, grad_aux_ref.shape[2]), 1)

    def row_sum(a):
        return jnp.sum(a, axis=1, keepdims=True)

    def chain_block(back, states):
        n = blocks - 1 - back
        rows = block_rows(n)
        after = []
        for s in range(sequences):
            grad_next = states[s]
            q, k, v = q_ref[s, rows], k_ref[s, rows], v_ref[s, rows]
            beta, gamma, rho = (aux_ref[s, rows, c : c + 1] for c in range(3))
            last = gamma[STRETCH - 1 :]
            between = between_ref[s, n]
            state, update = state_ref[s, n], update_ref[s, rows]
            grad = grad_ref[s, rows].astype(f32)
            key_next = mm(k, grad_next)
            grad_update = through_ref[s, rows] + rho * key_next
            after.append(last * grad_next + inflow_ref[s, n] - mm(w_ref[s, rows], grad_update, 0, 0))
            grad_target = mm(inv_ref[s, n], grad_update, 0, 0)
            key_state, query_state = mm(k, state), mm(q, state)
            key_key, query_key = mm(k, k, 1, 1), mm(q, k, 1, 1)
            grad_query_key = mm(grad, update, 1, 1) * between
            grad_system = -mm(grad_target, update, 1, 1) * strict * between
            grad_key_key = beta * grad_system
            grad_key_state = -(beta * gamma) * grad_target
            grad_q_ref[s, rows] = gamma * mm(grad, state, 1, 1) + mm(grad_query_key, k)
            grad_k_ref[s, rows] = (
                mm(grad_query_key, q, 0, 0)
                + mm(rho * update, grad_next, 1, 1)
                + mm(grad_key_key, k)
                + mm(grad_key_key, k, 0, 0)
                + mm(grad_key_state, state, 1, 1)
            )
            grad_v_ref[s, rows] = beta * grad_target
            grad_beta = row_sum(grad_system * key_key) + row_sum(
                grad_target * (v - gamma * key_state)
            )
            grad_gamma = row_sum(grad * query_state) - beta * row_sum(grad_target * key_state)
            spread = grad_query_key * query_key + grad_key_key * key_key
            grad_rho = row_sum(key_next * update) * rho
            at_end = jnp.sum(grad_rho) + jnp.sum(row_sum(state * grad_next) * last)
            grad_cumulative = (
                row_sum(spread) + grad_gamma * gamma - grad_rho + jnp.where(at_last, at_end, 0.0)
            )
            grad_row_ref[s, pl.ds(n, 1)] = jnp.sum(spread, axis=0, keepdims=True)
            grad_aux_ref[s, rows] = jnp.where(lane == 0, grad_beta, grad_cumulative)
        return tuple(after)

    return lax.fori_loop(first, first + count, chain_block, exits)


def shaped(shape, kind=f32):
    return jax.ShapeDtypeStruct(shape, kind)


def norm_gain(source, gain_vec):
    return source * lax.rsqrt(jnp.mean(source * source, -1, keepdims=True) + EPSILON) * gain_vec


def unit_rows(source):
    return source * lax.rsqrt(jnp.sum(source * source, -1, keepdims=True) + EPSILON)


def gated_norm(mixed_head, gate_pre, gain_vec):
    scale = lax.rsqrt(jnp.mean(mixed_head * mixed_head, -1, keepdims=True) + EPSILON)
    return mixed_head * scale * gain_vec * jax.nn.silu(gate_pre)


def conv_core(padded, weight, doc_pad):
    tap_count = weight.shape[0]
    length = padded.shape[1] - (tap_count - 1)
    current = doc_pad[:, tap_count - 1 :]
    summed = jnp.zeros((padded.shape[0], length, padded.shape[2]), f32)
    for offset in range(tap_count):
        first_row = tap_count - 1 - offset
        window = padded[:, first_row : first_row + length]
        same_doc = (doc_pad[:, first_row : first_row + length] == current).astype(f32)
        summed = summed + weight[offset] * window * same_doc[:, :, None]
    return jax.nn.silu(summed)


def prepare(packed_ext, decay_head, beta_head, taps, decay_log, decay_bias, doc_ext, dk):
    mixed = conv_core(packed_ext, taps, doc_ext)
    queries = unit_rows(mixed[:, :, :dk]) * dk ** (-0.5)
    key_rows = unit_rows(mixed[:, :, dk : 2 * dk])
    values = mixed[:, :, 2 * dk :]
    beta_rows = jax.nn.sigmoid(beta_head)
    decays = -jnp.exp(decay_log) * jax.nn.softplus(decay_head + decay_bias)
    sequences, length = decays.shape
    cumulative = jnp.cumsum(decays.reshape(sequences, length // STRETCH, STRETCH), -1)
    return queries, key_rows, values, beta_rows, cumulative


def block_gates(cumulative, doc_blocks, doc_starts):
    places = jnp.arange(STRETCH)
    linked = (places[:, None] >= places[None, :]) & (
        doc_blocks[..., :, None] == doc_blocks[..., None, :]
    )
    apart = cumulative[..., :, None] - cumulative[..., None, :]
    between = jnp.where(linked, jnp.exp(jnp.where(linked, apart, 0.0)), 0.0)
    survive = jnp.exp(cumulative) * (doc_blocks == doc_starts[..., None]).astype(f32)
    return survive, between, between[..., -1, :]


def each_peer(axis, action):
    count, me = lax.axis_size(axis), lax.axis_index(axis)

    def step(distance, carry):
        action(distance, lax.rem(me + distance, count), lax.rem(me + count - distance, count))
        return carry

    lax.fori_loop(1, count, step, 0)


def far_devices(axis, action):
    count, me = lax.axis_size(axis) // CORES, lax.axis_index(axis)
    group, place = me // CORES, lax.rem(me, CORES)

    def step(distance, carry):
        ahead, behind = lax.rem(group + distance, count), lax.rem(group + count - distance, count)
        action(distance, ahead * CORES + place, behind * CORES + place)
        return carry

    lax.fori_loop(1, count, step, 0)


def chip_devices(action):
    far_devices("cp", action)


def near(axis):
    me = lax.axis_index(axis)
    return me + 1 - 2 * lax.rem(me, CORES)


def sibling():
    return near("cp")


def owner_target(turn):
    hd = lax.axis_size("hd")
    share = lax.axis_size("cp") // hd
    piece = CORES * turn + lax.rem(lax.axis_index("cp"), CORES)
    return share * lax.axis_index("hd") + piece // hd, lax.rem(piece, hd)


def owner_source(chip):
    share = lax.axis_size("cp") // lax.axis_size("hd")
    core = lax.rem(lax.axis_index("hd"), CORES)
    return CORES * chip + core, lax.axis_index("cp") // share


def column_target(turn):
    return CORES * turn + lax.rem(lax.axis_index("cp"), CORES), lax.axis_index("hd")


def row_target(turn):
    me = lax.axis_index("cp")
    return CORES * lax.axis_index("hd") + lax.rem(me, CORES), me // CORES


def is_me(at):
    return (at[0] == lax.axis_index("cp")) & (at[1] == lax.axis_index("hd"))


def each(count, action):
    def step(turn, carry):
        action(turn)
        return carry

    lax.fori_loop(0, count, step, 0)


def signal(target):
    pl.semaphore_signal(
        pltpu.get_barrier_semaphore(), inc=1, device_id=target,
        device_id_type=pl.DeviceIdType.MESH,
    )


def meet(heads=False, chips=False, owners=False, rows=False):
    cp, hd = lax.axis_size("cp"), lax.axis_size("hd")
    total = jnp.int32(0)
    if heads:
        each_peer("hd", lambda _, to, source: signal({"hd": to}))
        total += hd - 1
    if chips:
        chip_devices(lambda _, to, source: signal({"cp": to}))
        signal({"cp": sibling()})
        total += cp // CORES
    for wanted, count, source_of, target_of in (
        (owners, cp // CORES, owner_source, owner_target),
        (rows, 1, row_target, row_target),
    ):
        if wanted:

            def greet(turn, source_of=source_of):
                at = source_of(turn)

                @pl.when(jnp.logical_not(is_me(at)))
                def _():
                    signal(at)

            each(count, greet)
            total += count
            for turn in range(count):
                total -= is_me(target_of(turn)).astype(jnp.int32)
    pl.semaphore_wait(pltpu.get_barrier_semaphore(), total)


def remote(src, dst, send, recv, target):
    return pltpu.make_async_remote_copy(
        src_ref=src,
        dst_ref=dst,
        send_sem=send,
        recv_sem=recv,
        device_id=target,
        device_id_type=pl.DeviceIdType.MESH,
    )


class Exchange:
    def __init__(self, axis, source, landing, send, recv, local):
        self.axis, self.source, self.landing = axis, source, landing
        self.send, self.recv = send, recv
        me = lax.axis_index(axis)
        self.own = pltpu.make_async_copy(source(me), landing(me), local)

    def copy(self, distance, block, place, to):
        return remote(
            block, place, self.send.at[distance], self.recv.at[distance], {self.axis: to}
        )

    def start(self):
        me = lax.axis_index(self.axis)
        each_peer(
            self.axis,
            lambda distance, to, source: self.copy(
                distance, self.source(to), self.landing(me), to
            ).start(),
        )
        self.own.start()

    def arrive(self):
        each_peer(
            self.axis,
            lambda distance, to, source: self.copy(
                distance, self.source(to), self.landing(source), to
            ).wait_recv(),
        )
        self.own.wait()

    def leave(self):
        each_peer(
            self.axis,
            lambda distance, to, source: self.copy(
                distance, self.source(to), self.landing(source), to
            ).wait_send(),
        )


class PairGather:
    def __init__(self, axis, source, landing, send, recv, local, near_first=False):
        self.axis, self.near_first = axis, near_first
        self.source, self.landing, self.send, self.recv = source, landing, send, recv
        self.me, self.near = lax.axis_index(axis), near(axis)
        self.count = lax.axis_size(axis) // CORES
        self.own = pltpu.make_async_copy(source, landing(self.me), local)

    def copy(self, block, index, slot, to):
        return remote(
            block, self.landing(index), self.send.at[slot], self.recv.at[index], {self.axis: to}
        )

    def far(self, action):
        far_devices(self.axis, action)

    def start(self):
        self.copy(self.source, self.me, 0, self.near).start()
        self.far(lambda d, to, source: self.copy(self.source, self.me, d, to).start())
        self.own.start()

    def hand_on(self):
        if self.near_first:
            self.copy(self.source, self.near, 0, self.near).wait_recv()
            self.far(
                lambda d, to, source: self.copy(
                    self.landing(self.near), self.near, self.count + d, to
                ).start()
            )
        else:

            def pass_far(d, to, source):
                self.copy(self.source, source, d, to).wait_recv()
                self.copy(self.landing(source), source, self.count + d, self.near).start()

            self.far(pass_far)

    def arrive(self):
        shift = self.near - self.me
        if self.near_first:
            self.far(lambda d, to, source: self.copy(self.source, source, d, to).wait_recv())
        else:
            self.copy(self.source, self.near, 0, self.near).wait_recv()
        self.far(
            lambda d, to, source: self.copy(
                self.source, source + shift, d, self.near
            ).wait_recv()
        )
        self.own.wait()

    def leave(self):
        self.copy(self.source, self.me, 0, self.near).wait_send()
        self.far(lambda d, to, source: self.copy(self.source, self.me, d, to).wait_send())
        self.far(
            lambda d, to, source: self.copy(
                self.source, source, self.count + d, self.near
            ).wait_send()
        )


class PairReduce:
    def __init__(self, parts, inbox, sums, landed, swap, send, recv, local, target, source):
        self.parts, self.inbox, self.sums, self.landed = parts, inbox, sums, landed
        self.send, self.recv, self.local = send, recv, local
        self.target, self.source = target, source
        me = lax.axis_index("cp")
        self.chip, self.core = me // CORES, lax.rem(me, CORES)
        self.swap = remote(
            parts.at[:, 1 - self.core], inbox, swap.at[0], swap.at[1], {"cp": sibling()}
        )

    def start(self):
        self.swap.start()

    def move(self, turn, slot, to):
        return remote(
            self.sums.at[turn], self.landed.at[slot], self.send.at[turn], self.recv.at[slot], to
        )

    def add_pairs(self):
        self.swap.wait()

        def go(turn):
            total = self.parts[turn, self.core].astype(f32) + self.inbox[turn].astype(f32)
            self.sums[turn] = total.astype(bf16)
            to = self.target(turn)
            own = is_me(to)

            @pl.when(own)
            def _():
                pltpu.make_async_copy(
                    self.sums.at[turn], self.landed.at[self.chip], self.local
                ).start()

            @pl.when(jnp.logical_not(own))
            def _():
                self.move(turn, self.chip, to).start()

        each(self.sums.shape[0], go)

    def total(self):
        def get(chip):
            at = self.source(chip)
            own = is_me(at)

            @pl.when(own)
            def _():
                pltpu.make_async_copy(
                    self.sums.at[chip], self.landed.at[chip], self.local
                ).wait()

            @pl.when(jnp.logical_not(own))
            def _():
                self.move(chip, chip, at).wait_recv()

        each(self.landed.shape[0], get)
        return added(self.landed).astype(bf16)

    def leave(self):
        def done(turn):
            to = self.target(turn)

            @pl.when(jnp.logical_not(is_me(to)))
            def _():
                self.move(turn, turn, to).wait_send()

        each(self.sums.shape[0], done)


class RowMove:
    def __init__(self, rows, landing, send, recv, local):
        self.rows, self.send, self.recv, self.local = rows, send, recv, local
        self.slot = lax.rem(lax.axis_index("cp"), CORES)
        self.landing = lambda slot: lead_rows(landing, slot, rows.shape[0])
        self.to = row_target(0)
        self.own = is_me(self.to)
        self.move = remote(self.rows, self.landing(self.slot), send.at[0], recv.at[0], self.to)
        self.kept = pltpu.make_async_copy(rows, self.landing(self.slot), local)

    def shared(self, slot):
        return remote(
            self.landing(self.slot), self.landing(slot), self.send.at[1], self.recv.at[1],
            {"cp": sibling()},
        )

    def start(self):
        @pl.when(self.own)
        def _():
            self.kept.start()

        @pl.when(jnp.logical_not(self.own))
        def _():
            self.move.start()

    def hand_on(self):
        @pl.when(self.own)
        def _():
            self.kept.wait()

        @pl.when(jnp.logical_not(self.own))
        def _():
            self.move.wait_recv()

        self.shared(self.slot).start()

    def arrive(self):
        self.shared(1 - self.slot).wait_recv()

    def leave(self):
        self.shared(self.slot).wait_send()

        @pl.when(jnp.logical_not(self.own))
        def _():
            self.move.wait_send()


def sems(*counts):
    found = []
    for count in counts:
        found += [pltpu.SemaphoreType.DMA((count,))] * 2 + [pltpu.SemaphoreType.DMA]
    return found


def reduce_scratch(parts):
    half = (parts.shape[0], *parts.shape[2:])
    return [pltpu.VMEM(half, bf16)] * 3 + [
        pltpu.SemaphoreType.DMA((2,)), *sems(parts.shape[0])
    ]


def token_rows(ref, index, tokens):
    return ref.at[:, pl.ds(pl.multiple_of(index * tokens, tokens), tokens)]


def lead_rows(ref, index, rows):
    return ref.at[pl.ds(pl.multiple_of(index * rows, rows), rows)]


def comm_call(body, out_shape, places, operands, spots, scratch, number):
    kinds = {"any": pl.ANY, "vmem": pltpu.VMEM}
    return pl.pallas_call(
        body,
        out_shape=out_shape,
        in_specs=[pl.BlockSpec(memory_space=kinds[k]) for k in places],
        out_specs=tuple(pl.BlockSpec(memory_space=kinds[k]) for k in spots),
        scratch_shapes=scratch,
        compiler_params=pltpu.CompilerParams(
            collective_id=number, has_side_effects=True, vmem_limit_bytes=VMEM_LIMIT
        ),
    )(*operands)


def open_kernel(hidden_ref, front_ref, hidden_all_ref, front_all_ref, *flags):
    tokens, shard = hidden_ref.shape[1], front_ref.shape[0]
    meet(heads=True, chips=True)
    moves = (
        PairGather(
            "hd", hidden_ref, lambda at: token_rows(hidden_all_ref, at, tokens), *flags[:3],
            near_first=True,
        ),
        PairGather("cp", front_ref, lambda at: lead_rows(front_all_ref, at, shard), *flags[3:6]),
    )
    for move in moves:
        move.start()
    for move in moves:
        move.hand_on()
    for move in moves:
        move.arrive()
        move.leave()


def place_of():
    me = lax.axis_index("cp")
    return me // CORES, lax.rem(me, CORES)


def forward_kernel(
    q_ref, k_ref, v_ref, aux_ref, between_ref, cot_ref, ffn_ref, output_ref, down_ref,
    mixed_ref, state_ref, update_ref, w_ref, inv_ref, maps_ref, both_ref,
    cot_all_ref, ffn_all_ref, output_part_ref, down_part_ref,
    x_ref, u_ref, own_ref, other_ref, entry_ref, give_ref, pair_sems, *flags
):
    sequences, _, dk = k_ref.shape
    dv = v_ref.shape[2]
    tokens, shard = cot_ref.shape[1], ffn_ref.shape[0]
    chip, core = place_of()
    early = core == 0
    meet(heads=True, chips=True, rows=True)
    carried = (
        RowMove(output_ref, output_part_ref, *flags[3:6]),
        RowMove(down_ref, down_part_ref, *flags[6:9]),
        PairGather("cp", ffn_ref, lambda at: lead_rows(ffn_all_ref, at, shard), *flags[:3]),
    )
    cot_move = PairGather(
        "hd", cot_ref, lambda at: token_rows(cot_all_ref, at, tokens), *flags[9:12],
        near_first=True,
    )
    cot_move.start()
    for move in reversed(carried):
        move.start()
    segment_maps(
        k_ref, v_ref, aux_ref, between_ref, x_ref, own_ref, w_ref, u_ref, inv_ref,
        cot_move.hand_on,
    )
    swap = remote(
        own_ref.at[1 - core], other_ref, pair_sems.at[0], pair_sems.at[1], {"cp": sibling()}
    )
    swap.start()
    swap.wait()
    mine, theirs = own_ref[core], other_ref[...]
    both_ref[0] = jnp.where(early, mine, theirs)
    both_ref[1] = jnp.where(early, theirs, mine)
    first, second = both_ref[0].astype(f32), both_ref[1].astype(f32)
    pair = mm(second[:, :dk], first)
    pair = jnp.concatenate([pair[:, :dk], pair[:, dk:] + second[:, dk:]], 1)
    maps_ref[chip] = pair.astype(bf16)
    settle = spread_chips(maps_ref, flags[12], flags[13])
    for move in carried:
        move.hand_on()
    settle()

    def enter(hop, state):
        return mm(maps_ref[hop, :, :dk].astype(f32), state) + maps_ref[hop, :, dk:].astype(f32)

    entered = lax.fori_loop(0, chip, enter, jnp.zeros((dk, dv), f32))
    halfway = mm(first[:, :dk], entered) + first[:, dk:]
    entry_ref[core] = jnp.where(early, entered, halfway)
    give_ref[...] = jnp.where(early, halfway, entered)
    give = remote(
        give_ref, entry_ref.at[core], pair_sems.at[2], pair_sems.at[3], {"cp": sibling()}
    )
    give.start()
    remote(
        give_ref, entry_ref.at[1 - core], pair_sems.at[2], pair_sems.at[3], {"cp": sibling()}
    ).wait()
    run_segment(
        entry_ref, x_ref, q_ref, k_ref, aux_ref, between_ref, w_ref, u_ref,
        mixed_ref, state_ref, update_ref,
    )
    for move in (*carried, cot_move):
        move.arrive()
        move.leave()


def spread_chips(ref, send, recv):
    chip, _ = place_of()

    def copy(distance, index, to):
        return remote(ref.at[index], ref.at[index], send.at[distance], recv.at[distance], {"cp": to})

    chip_devices(lambda d, to, source: copy(d, chip, to).start())

    def settle():
        chip_devices(lambda d, to, source: copy(d, source // CORES, to).wait_recv())
        chip_devices(lambda d, to, source: copy(d, chip, to).wait_send())

    return settle


def backward_kernel(
    q_ref, k_ref, v_ref, aux_ref, between_ref, w_ref, inv_ref, state_ref, update_ref, grad_ref,
    maps_ref, both_ref, ffn_ref, down_ref, output_ref, out_part_ref, middle_ref,
    grad_q_ref, grad_k_ref, grad_v_ref, grad_aux_ref, grad_row_ref, ffn_all_ref, down_all_ref,
    output_all_ref, block_ref,
    through_ref, inflow_ref, own_ref, other_ref, locals_ref, exit_ref, give_ref,
    ffn_own_ref, down_own_ref, output_own_ref, out_landed_ref, pair_sems, chip_send, chip_recv,
    *flags
):
    sequences, length, dk = k_ref.shape
    dv = v_ref.shape[2]
    blocks = length // STRETCH
    chip, core = place_of()
    chips = locals_ref.shape[0]
    late = core == CORES - 1
    meet(heads=True, chips=True, owners=True)
    reduces = (
        PairReduce(ffn_ref, *flags[:7], column_target, column_source),
        PairReduce(down_ref, *flags[7:14], owner_target, owner_source),
        PairReduce(output_ref, *flags[14:21], owner_target, owner_source),
    )
    tokens = middle_ref.shape[1]
    out_move = Exchange(
        "hd",
        lambda to: token_rows(out_part_ref, to, tokens),
        lambda at: out_landed_ref.at[at],
        *flags[30:33],
    )
    for move in reduces:
        move.start()
    segment_local(
        q_ref, k_ref, aux_ref, between_ref, w_ref, grad_ref, through_ref, inflow_ref, own_ref
    )
    swap = remote(
        own_ref.at[1 - core], other_ref, pair_sems.at[0], pair_sems.at[1], {"cp": sibling()}
    )
    swap.start()
    swap.wait()
    mine, theirs = own_ref[core].astype(f32), other_ref[...].astype(f32)
    first, second = jnp.where(late, theirs, mine), jnp.where(late, mine, theirs)
    locals_ref[chip] = (mm(both_ref[0, :, :dk].astype(f32), second, 0, 0) + first).astype(bf16)
    settle = spread_chips(locals_ref, chip_send, chip_recv)
    for move in reduces:
        move.add_pairs()
    settle()
    out_move.start()

    def leave(hop, state):
        source = chips - 1 - hop
        return mm(maps_ref[source, :, :dk].astype(f32), state, 0, 0) + locals_ref[
            source
        ].astype(f32)

    left = lax.fori_loop(0, chips - 1 - chip, leave, jnp.zeros((dk, dv), f32))
    halfway = mm(both_ref[1, :, :dk].astype(f32), left, 0, 0) + second
    exit_ref[core] = jnp.where(late, left, halfway)
    give_ref[...] = jnp.where(late, halfway, left)
    remote(
        give_ref, exit_ref.at[core], pair_sems.at[2], pair_sems.at[3], {"cp": sibling()}
    ).start()
    remote(
        give_ref, exit_ref.at[1 - core], pair_sems.at[2], pair_sems.at[3], {"cp": sibling()}
    ).wait()
    refs = (
        q_ref, k_ref, v_ref, aux_ref, between_ref, w_ref, inv_ref, state_ref, update_ref,
        grad_ref, through_ref, inflow_ref,
        grad_q_ref, grad_k_ref, grad_v_ref, grad_aux_ref, grad_row_ref,
    )
    exits = tuple(exit_ref[s] for s in range(sequences))
    exits = back_blocks(0, blocks // 2, exits, *refs)
    spreads = []
    for n, (move, own, everywhere) in enumerate(
        zip(
            reduces,
            (ffn_own_ref, down_own_ref, output_own_ref),
            (ffn_all_ref, down_all_ref, output_all_ref),
        )
    ):
        own[...] = move.total()
        spreads.append(spread_piece(own, everywhere, flags[21 + 3 * n : 24 + 3 * n]))
    quarter = (blocks - blocks // 2) // 2
    exits = back_blocks(blocks // 2, quarter, exits, *refs)
    for spread in spreads:
        spread.hand_on()
    back_blocks(blocks // 2 + quarter, blocks - blocks // 2 - quarter, exits, *refs)
    out_move.arrive()
    block_ref[...] = (middle_ref[...] + added(out_landed_ref)).astype(bf16)
    for move in (*reduces, out_move):
        move.leave()
    for spread in spreads:
        spread.arrive()
        spread.leave()


def column_source(chip):
    return column_target(chip)


def spread_piece(own, everywhere, flags):
    spread = PairGather("hd", own, lambda at: everywhere.at[at], *flags, near_first=True)
    spread.start()
    return spread


def added(landed_ref):
    total = landed_ref[0].astype(f32)
    for index in range(1, landed_ref.shape[0]):
        total += landed_ref[index].astype(f32)
    return total


def spread_own(own_ref, all_ref, tokens, flags):
    moves = [
        PairGather(
            "hd",
            own_ref.at[s],
            lambda at, s=s: all_ref.at[s, pl.ds(pl.multiple_of(at * tokens, tokens), tokens)],
            *flags[3 * s : 3 * s + 3],
            near_first=s % 2 == 0,
        )
        for s in range(own_ref.shape[0])
    ]
    for move in moves:
        move.start()
    return moves


def settle_all(moves):
    for move in moves:
        move.hand_on()
    for move in moves:
        move.arrive()
        move.leave()


def middle_kernel(
    partial_ref, hidden_ref, gain_ref, middle_ref, ffn_all_ref, landed_ref, own_ref, *flags
):
    tokens = hidden_ref.shape[1]
    meet(heads=True)
    move = Exchange(
        "hd", lambda to: token_rows(partial_ref, to, tokens), lambda at: landed_ref.at[at], *flags[:3]
    )
    move.start()
    move.arrive()
    middle = hidden_ref[...].astype(f32) + added(landed_ref)
    middle_ref[...] = middle
    own_ref[...] = norm_gain(middle, gain_ref[...]).astype(bf16)
    after = spread_own(own_ref, ffn_all_ref, tokens, flags[3:])
    settle_all(after)
    move.leave()


def norm_back(source, gain_vec, grad):
    scale = lax.rsqrt(jnp.mean(source * source, -1, keepdims=True) + EPSILON)
    lifted = grad * gain_vec
    mixed = jnp.mean(source * lifted, -1, keepdims=True)
    return scale * lifted - source * (scale * scale * scale) * mixed, source * scale * grad


def ffn_back_kernel(
    grad_part_ref, middle_ref, cot_ref, gain_ref,
    grad_middle_ref, grad_gain_ref, grad_all_ref, grad_landed_ref, own_ref, *flags
):
    tokens = middle_ref.shape[1]
    meet(heads=True)
    move = Exchange(
        "hd",
        lambda to: token_rows(grad_part_ref, to, tokens),
        lambda at: grad_landed_ref.at[at],
        *flags[:3],
    )
    move.start()
    move.arrive()
    back, gain_terms = norm_back(middle_ref[...], gain_ref[...], added(grad_landed_ref))
    grad_middle = cot_ref[...].astype(f32) + back
    own_ref[...] = grad_middle.astype(bf16)
    after = spread_own(own_ref, grad_all_ref, tokens, flags[3:])
    grad_middle_ref[...] = grad_middle
    grad_gain_ref[...] = jnp.sum(jnp.sum(gain_terms, axis=0), axis=0, keepdims=True)
    settle_all(after)
    move.leave()


def close_kernel(
    normed_part_ref, front_ref, small_ref, hidden_ref, grad_middle_ref, gain_ref,
    grad_in_ref, front_all_ref, small_sum_ref,
    normed_landed, small_landed, front_own, *flags
):
    tokens = hidden_ref.shape[1]
    meet(heads=True, chips=True)
    reduce = PairReduce(front_ref, *flags[:7], column_target, column_source)
    normed_move = Exchange(
        "hd",
        lambda to: token_rows(normed_part_ref, to, tokens),
        lambda at: normed_landed.at[at],
        *flags[7:10],
    )
    small_move = PairGather("cp", small_ref, lambda at: small_landed.at[at], *flags[10:13])
    reduce.start()
    small_move.start()
    normed_move.start()
    reduce.add_pairs()
    small_move.hand_on()
    front_own[...] = reduce.total()
    spread = spread_piece(front_own, front_all_ref, flags[13:16])
    normed_move.arrive()
    spread.hand_on()
    back, _ = norm_back(hidden_ref[...].astype(f32), gain_ref[...], added(normed_landed))
    grad_in_ref[...] = (grad_middle_ref[...] + back).astype(bf16)
    small_move.arrive()
    small_sum_ref[...] = added(small_landed)
    for move in (normed_move, small_move, reduce):
        move.leave()
    spread.arrive()
    spread.leave()


def passed_along(block, axis, distance):
    devices = range(lax.axis_size(axis))
    route = [(i - distance, i) for i in devices if i - distance in devices]
    return lax.ppermute(block, axis, route)


def on_device(
    hidden_in, doc_ids, w_query, w_key, w_value, w_decay, w_beta, w_gate_out, w_output,
    w_ffn_gate, w_ffn_up, w_ffn_down, conv_query, conv_key, conv_value, decay_log, decay_bias,
    gain_attn, gain_ffn, gain_head, cotangent,
):
    place, head = lax.axis_index("cp"), lax.axis_index("hd")
    cp, hd = lax.axis_size("cp"), lax.axis_size("hd")
    sequences, tokens, width = hidden_in.shape
    shard = w_query.shape[0]
    dk, dv = w_query.shape[1] // hd, w_value.shape[1] // hd
    ff = w_ffn_gate.shape[1] // hd
    ffp = -(-ff // LANES) * LANES
    qkv = 2 * dk + dv
    side, gate_at = qkv, qkv + LANES
    span = tokens * hd
    blocks = span // STRETCH

    def part(weight):
        cols = weight.shape[1] // hd
        return lax.dynamic_slice_in_dim(weight, head * cols, cols, 1)

    def ff_pad(weight):
        return jnp.pad(part(weight), ((0, 0), (0, ffp - ff)))

    head_share = gain_head.shape[0]
    side_cols = jnp.stack(
        [
            part(w_decay)[:, 0],
            part(w_beta)[:, 0],
            gain_attn,
            gain_ffn,
            jnp.pad(gain_head, (0, shard - head_share)),
        ],
        1,
    )
    front = jnp.concatenate(
        [
            part(w_query),
            part(w_key),
            part(w_value),
            jnp.pad(side_cols, ((0, 0), (0, LANES - side_cols.shape[1]))),
            part(w_gate_out),
        ],
        1,
    )
    hidden_all, front_full = comm_call(
        open_kernel,
        (shaped((sequences, span, width), bf16), shaped((width, front.shape[1]), bf16)),
        ("any", "any"),
        (hidden_in, front),
        ("any", "any"),
        sems(hd, cp),
        1,
    )
    ffn_front = jnp.concatenate([ff_pad(w_ffn_gate), ff_pad(w_ffn_up)], 1)

    attn_gain = front_full[:, side + 2].astype(f32)
    ffn_gain = front_full[:, side + 3].astype(f32)
    head_gain = front_full[:, side + 4].reshape(cp, shard)[:, :head_share].reshape(-1).astype(f32)

    def dot(a, b, spec):
        return jnp.einsum(spec, a, b, preferred_element_type=f32)

    inputs_all = hidden_all.astype(f32)
    scale_all = lax.rsqrt(jnp.mean(inputs_all * inputs_all, -1, keepdims=True) + EPSILON)
    normed = (inputs_all * scale_all * attn_gain).astype(bf16)
    projected = dot(normed, front_full, "std,de->ste")
    packed = projected[:, :, :qkv].astype(bf16)
    gate_pre = projected[:, :, gate_at:]
    decay_head = projected[:, :, side].astype(bf16).astype(f32)
    beta_head = projected[:, :, side + 1].astype(bf16).astype(f32)

    margin = conv_query.shape[0] - 1
    rim = passed_along(packed[:, -margin:], "cp", 1)
    doc_pad = jnp.concatenate([jnp.full((sequences, margin), -1, jnp.int32), doc_ids], 1)
    doc_ext = lax.dynamic_slice_in_dim(doc_pad, place * span, span + margin, 1)
    doc_blocks = doc_ext[:, margin:].reshape(sequences, blocks, STRETCH)
    doc_starts = doc_ext[:, margin - 1 : -1].reshape(sequences, blocks, STRETCH)[:, :, 0]
    taps = jnp.concatenate([conv_query, conv_key, conv_value], 1).astype(f32)
    prepared, prepare_pull = jax.vjp(
        lambda *entries: prepare(*entries, doc_ext, dk),
        jnp.concatenate([rim, packed], 1).astype(f32),
        decay_head,
        beta_head,
        taps,
        decay_log.astype(f32),
        decay_bias.astype(f32),
    )
    queries, key_rows, values, beta_rows, cumulative = prepared
    survive, between, rho = block_gates(cumulative, doc_blocks, doc_starts)
    flat = (sequences, span)
    aux = jnp.stack([beta_rows, survive.reshape(flat), rho.reshape(flat)], -1)
    aux = jnp.pad(aux, ((0, 0), (0, 0), (0, 5)))
    chips = cp // CORES
    share = cp // hd
    (
        mixed, states, updates, weighted, inverse, maps, both,
        cot_all, ffn_full, output_part, down_part,
    ) = comm_call(
        forward_kernel,
        (
            shaped((sequences, span, dv), bf16),
            shaped((sequences, blocks, dk, dv)),
            shaped((sequences, span, dv)),
            shaped((sequences, span, dk)),
            shaped((sequences, blocks, STRETCH, STRETCH)),
            shaped((chips, dk, dk + dv), bf16),
            shaped((CORES, dk, dk + dv), bf16),
            shaped((sequences, span, width), bf16),
            shaped((width, 2 * ffp), bf16),
            shaped((share * w_output.shape[0], width), bf16),
            shaped((share * w_ffn_down.shape[0], width), bf16),
        ),
        ("vmem",) * 5 + ("any",) * 4,
        (
            queries, key_rows, values, aux, between, cotangent, ffn_front, w_output, w_ffn_down,
        ),
        ("vmem",) * 7 + ("any",) * 4,
        [
            pltpu.VMEM((sequences, blocks, dk, dk + dv), f32),
            pltpu.VMEM((sequences, span, dv), f32),
            pltpu.VMEM((sequences, dk, dk + dv), bf16),
            pltpu.VMEM((dk, dk + dv), bf16),
            pltpu.VMEM((sequences, dk, dv), f32),
            pltpu.VMEM((dk, dv), f32),
            pltpu.SemaphoreType.DMA((4,)),
            *sems(cp, CORES, CORES, hd),
            pltpu.SemaphoreType.DMA((chips,)),
            pltpu.SemaphoreType.DMA((chips,)),
        ],
        2,
    )
    down_part = jnp.pad(down_part, ((0, ffp - ff), (0, 0)))
    mixed_float = mixed.astype(f32)
    normed_head, gated_pull = jax.vjp(gated_norm, mixed_float, gate_pre, head_gain)
    normed_head = normed_head.astype(bf16)
    landing = pltpu.VMEM((hd, sequences, tokens, width), bf16)
    own_tokens = pltpu.VMEM((sequences, tokens, width), bf16)
    ffn_gain = ffn_gain[None]
    middle, ffn_all = comm_call(
        middle_kernel,
        (shaped(hidden_in.shape), shaped((sequences, span, width), bf16)),
        ("any", "vmem", "vmem"),
        (dot(normed_head, output_part, "ste,ed->std").astype(bf16), hidden_in, ffn_gain),
        ("vmem", "any"),
        [landing, own_tokens, *sems(hd, *(hd,) * sequences)],
        4,
    )
    gate_up = dot(ffn_all, ffn_full, "std,df->stf")
    inner, swiglu_pull = jax.vjp(
        lambda both: jax.nn.silu(both[..., :ffp]) * both[..., ffp:], gate_up
    )
    inner = inner.astype(bf16)
    grad_inner = dot(cot_all, down_part, "std,fd->stf")
    grad_gate_up = swiglu_pull(grad_inner)[0].astype(bf16)
    out_partial = dot(inner, down_part, "stf,fd->std").astype(bf16)
    grad_middle, grad_ffn_gain, grad_attention = comm_call(
        ffn_back_kernel,
        (shaped(hidden_in.shape), shaped((1, width)), shaped((sequences, span, width), bf16)),
        ("any", "vmem", "vmem", "vmem"),
        (
            dot(grad_gate_up, ffn_full, "stf,df->std").astype(bf16),
            middle, cotangent, ffn_gain,
        ),
        ("vmem", "vmem", "any"),
        [landing, own_tokens, *sems(hd, *(hd,) * sequences)],
        5,
    )

    def weight_grad(left_side, right_side):
        return dot(left_side, right_side, "std,ste->de")

    def pieces(grad):
        rows = grad.shape[0] // cp
        split = grad.reshape(chips, CORES, rows, width)
        return jnp.pad(split, ((0, 0), (0, 0), (0, -rows % 16), (0, 0))).astype(bf16)

    def by_owner(grad):
        return grad.reshape(chips, CORES, shard, grad.shape[1]).astype(bf16)

    grad_down = pieces(weight_grad(inner, cot_all)[:ff])

    grad_normed_head = dot(grad_attention, output_part, "std,ed->ste")
    grad_output = pieces(weight_grad(normed_head, grad_attention))
    grad_mixed, grad_gate_pre, grad_head_gain = gated_pull(grad_normed_head)
    grad_mixed = grad_mixed.astype(bf16)
    grad_gate_pre = grad_gate_pre.astype(bf16)
    grad_ffn = by_owner(
        jnp.concatenate(
            [
                weight_grad(ffn_all, grad_gate_up).astype(bf16),
                weight_grad(normed, grad_gate_pre).astype(bf16),
            ],
            1,
        )
    )
    ffn_share, down_share, output_share = (
        entry.shape[2:] for entry in (grad_ffn, grad_down, grad_output)
    )
    (
        grad_q, grad_k, grad_v, grad_aux, grad_row, grad_ffn, grad_down, new_output, block_out,
    ) = comm_call(
        backward_kernel,
        (
            shaped((sequences, span, dk)),
            shaped((sequences, span, dk)),
            shaped((sequences, span, dv)),
            shaped((sequences, span, 8)),
            shaped((sequences, blocks, STRETCH)),
            shaped((hd, *ffn_share), bf16),
            shaped((hd, *down_share), bf16),
            shaped((hd, *output_share), bf16),
            shaped(hidden_in.shape, bf16),
        ),
        ("vmem",) * 15 + ("any", "vmem"),
        (
            queries, key_rows, values, aux, between, weighted, inverse, states, updates,
            grad_mixed, maps, both, grad_ffn, grad_down, grad_output, out_partial, middle,
        ),
        ("vmem",) * 5 + ("any",) * 3 + ("vmem",),
        [
            pltpu.VMEM((sequences, span, dv), f32),
            pltpu.VMEM((sequences, blocks, dk, dv), f32),
            pltpu.VMEM((sequences, dk, dv), bf16),
            pltpu.VMEM((dk, dv), bf16),
            pltpu.VMEM((chips, dk, dv), bf16),
            pltpu.VMEM((sequences, dk, dv), f32),
            pltpu.VMEM((dk, dv), f32),
            pltpu.VMEM(ffn_share, bf16),
            pltpu.VMEM(down_share, bf16),
            pltpu.VMEM(output_share, bf16),
            landing,
            pltpu.SemaphoreType.DMA((4,)),
            pltpu.SemaphoreType.DMA((chips,)),
            pltpu.SemaphoreType.DMA((chips,)),
            *reduce_scratch(grad_ffn),
            *reduce_scratch(grad_down),
            *reduce_scratch(grad_output),
            *sems(hd, hd, hd, hd),
        ],
        3,
    )
    grad_cumulative = grad_aux[:, :, 1].reshape(sequences, blocks, STRETCH) - grad_row
    grad_ext, grad_decay, grad_beta, grad_taps, grad_log, grad_bias = prepare_pull(
        (grad_q, grad_k, grad_v, grad_aux[:, :, 0], grad_cumulative)
    )
    back = passed_along(grad_ext[:, :margin], "cp", -1)
    grad_packed = grad_ext[:, margin:].at[:, -margin:].add(back).astype(bf16)
    grad_projected = jnp.concatenate(
        [
            grad_packed,
            jnp.pad(
                jnp.stack([grad_decay, grad_beta], -1).astype(bf16),
                ((0, 0), (0, 0), (0, LANES - 2)),
            ),
            grad_gate_pre,
        ],
        -1,
    )
    partial_normed = dot(grad_projected, front_full, "ste,de->std")
    grad_attn_gain = jnp.sum(inputs_all * scale_all * partial_normed, (0, 1))
    grad_front = weight_grad(normed, grad_projected[:, :, :gate_at])
    spread_gain = jnp.pad(
        grad_head_gain.reshape(cp, head_share), ((0, 0), (0, shard - head_share))
    ).reshape(-1)
    gains = jnp.stack([grad_attn_gain, grad_ffn_gain[0], spread_gain], 1)
    grad_front += jnp.pad(gains, ((0, 0), (side + 2, LANES - 2 - gains.shape[1])))

    small = jnp.concatenate(
        [
            grad_taps,
            jnp.pad(jnp.stack([grad_log, grad_bias], 1), ((0, 0), (0, qkv - 2))),
        ],
        0,
    )
    small = jnp.pad(small, ((0, -small.shape[0] % 8), (0, 0)))
    grad_front = by_owner(grad_front)
    front_share = grad_front.shape[2:]
    grad_in, grad_front, small = comm_call(
        close_kernel,
        (shaped(hidden_in.shape, bf16), shaped((hd, *front_share), bf16), shaped(small.shape)),
        ("any", "vmem", "any") + ("vmem",) * 3,
        (
            partial_normed.astype(bf16), grad_front, small, hidden_in, grad_middle,
            attn_gain[None],
        ),
        ("vmem", "any", "vmem"),
        [
            landing,
            pltpu.VMEM((cp, *small.shape), f32),
            pltpu.VMEM(front_share, bf16),
            *reduce_scratch(grad_front),
            *sems(hd, cp, hd),
        ],
        6,
    )

    def owned(grad, rows):
        return grad[:, : rows // hd].reshape(rows, width).astype(f32)

    taps_rows = margin + 1

    def columns(grad):
        return jnp.swapaxes(grad, 0, 1).reshape(grad.shape[1], -1).astype(f32)

    gain_sums = jnp.sum(grad_front[:, :, side + 2 : side + 5].astype(f32), 0)
    return (
        block_out,
        grad_in,
        columns(grad_front[:, :, :dk]),
        columns(grad_front[:, :, dk : 2 * dk]),
        columns(grad_front[:, :, 2 * dk : qkv]),
        columns(grad_front[:, :, side : side + 1]),
        columns(grad_front[:, :, side + 1 : side + 2]),
        columns(grad_ffn[:, :, 2 * ffp :]),
        owned(new_output, w_output.shape[0]),
        columns(grad_ffn[:, :, :ff]),
        columns(grad_ffn[:, :, ffp : ffp + ff]),
        owned(grad_down, w_ffn_down.shape[0]),
        small[:taps_rows, :dk],
        small[:taps_rows, dk : 2 * dk],
        small[:taps_rows, 2 * dk :],
        small[taps_rows, :1],
        small[taps_rows, 1:2],
        gain_sums[:, 0],
        gain_sums[:, 1],
        gain_sums[:head_share, 2],
    )


def solution(mesh):
    tokens, rows, cols = P(None, ("cp", "hd"), None), P("cp", None), P(None, "hd")
    weights = (rows,) * 10
    return jax.shard_map(
        on_device,
        mesh=mesh,
        in_specs=(tokens, P(), *weights, cols, cols, cols, P("hd"), P("hd"))
        + (P("cp"),) * 3
        + (tokens,),
        out_specs=(tokens, tokens, *weights, cols, cols, cols, P("hd"), P("hd"))
        + (P("cp"),) * 3,
        check_vma=False,
    )
```
